32 devices in a mesh: section: 2 (over x), dp: 16 (over z, y, core).
Axes of the slice: x: 2, y: 2, z: 4, core: 2. Of those that a mesh axis runs over, the one named last changes fastest.
Arguments:
- embeddings: bfloat16 [2, 48, 512, 512], P('section', 'dp'), may hold values from -6 to 6
- segments: int32 [2, 48, 512], P(None, 'dp'), may hold values from 0 to 23, as said below
- cotangent: bfloat16 [48, 512, 512], P('dp'), may hold values from -6 to 6
- attn_qkv: bfloat16 [2, 512, 1536], P('section'), may hold values from -0.25 to 0.25
- attn_out: bfloat16 [2, 512, 512], P('section'), may hold values from -1 to 1
- cross_proj: bfloat16 [2, 512, 1024], P('section'), may hold values from -0.375 to 0.375
- ffn_up: bfloat16 [2, 512, 2048], P('section'), may hold values from -0.25 to 0.25
- ffn_down: bfloat16 [2, 2048, 512], P('section'), may hold values from -0.125 to 0.125
- norm_gain: bfloat16 [2, 3, 512], P('section'), may hold values from 0.25 to 1.75
- norm_bias: bfloat16 [2, 3, 512], P('section'), may hold values from -1 to 1
Outputs:
- layer_out: bfloat16 [2, 48, 512, 512], P('section', 'dp')
- input_grad: float32 [2, 48, 512, 512], P('section', 'dp')
- grad_qkv: float32 [2, 512, 1536], P('section')
- grad_attn_out: float32 [2, 512, 512], P('section')
- grad_cross: float32 [2, 512, 1024], P('section')
- grad_up: float32 [2, 512, 2048], P('section')
- grad_down: float32 [2, 2048, 512], P('section')
- grad_gain: float32 [2, 3, 512], P('section')
- grad_bias: float32 [2, 3, 512], P('section')
The draws below stay inside these ranges and needn't reach their ends.
Inputs may be any that keep to these rules, and one draw needn't show every extreme that they name: Segment numbers start at 0 in each row and rise by one at each boundary; a source row and the target row of the same index hold the same number of segments, between 8 and 24, and target segment k pairs with source segment k; some row holds 24 segments.
All inputs are finite; a program needn't handle non-finite values.
Results may differ from the reference program's by a relative error of at most 0.025.
Values may be sent and summed in bfloat16 or wider, within the bound.
A program may use at most 192 MiB of HBM per device.

```python
import jax
import jax.numpy as jnp
from jax import lax

D = 512
HEADS = 8
FF = 2048
SEQ = 512
SEGS = 24
ROWS = 48


def draw_segments(key, part):
    key = jax.random.fold_in(key, 11)
    count_key, pick_key, order_key = jax.random.split(key, 3)
    fewest = max(SEGS // 3, 1)
    counts = jax.random.randint(count_key, (ROWS,), fewest, SEGS + 1)
    chosen = jax.random.randint(pick_key, (), 0, ROWS)
    counts = jnp.where(jnp.arange(ROWS) == chosen, SEGS, counts)
    row_keys = jax.random.split(order_key, 2 * ROWS)
    orders = jax.vmap(lambda row_key: jax.random.permutation(row_key, SEQ - 1))(row_keys).reshape(2, ROWS, SEQ - 1)
    starts = (orders < (counts - 1)[None, :, None]).astype(jnp.int32)
    numbers = jnp.cumsum(starts, axis=-1)
    return jnp.concatenate([jnp.zeros((2, ROWS, 1), jnp.int32), numbers], axis=-1).astype(jnp.int32)


def block_levels(rng, shape, shards, smallest, top_value):
    gain, own = 1.0, jax.random.fold_in(rng, 6)
    for axis_at, parts in shards:
        steps = jnp.exp(jax.random.uniform(jax.random.fold_in(own, axis_at), (parts,), jnp.float32, smallest / len(shards), top_value / len(shards)))
        gain = gain * jnp.repeat(steps, shape[axis_at] // parts).reshape([-1 if axis == axis_at else 1 for axis in range(len(shape))])
    return gain


def scatter_about(own_key, shape, scale, most, shards=(), held_as=jnp.bfloat16):
    drawn = scale * jax.random.normal(own_key, shape, jnp.float32)
    if shards:
        drawn = drawn * block_levels(own_key, shape, shards, -0.22, 0.18)
    return jnp.clip(drawn, -most, most).astype(held_as)


def setup_inputs(seed: int = 0) -> dict:
    seeds = jax.random.split(jax.random.key(seed), 11)
    embeddings = scatter_about(seeds[0], (2, ROWS, SEQ, D), 1.0, 6.0, ((0, 2), (1, 16)))
    segments = draw_segments(jax.random.fold_in(seeds[10], 71), 0)
    cotangent = scatter_about(seeds[2], (ROWS, SEQ, D), 1.0, 6.0, ((0, 16),))
    attn_qkv = scatter_about(seeds[3], (2, D, 3 * D), D ** -0.5, 0.25, ((0, 2),))
    attn_out = scatter_about(seeds[4], (2, D, D), (D // 16) ** -0.5, 1.0, ((0, 2),))
    cross_proj = scatter_about(seeds[5], (2, D, 2 * D), (D // 2) ** -0.5, 0.375, ((0, 2),))
    ffn_up = scatter_about(seeds[6], (2, D, FF), D ** -0.5, 0.25, ((0, 2),))
    ffn_down = scatter_about(seeds[7], (2, FF, D), FF ** -0.5, 0.125, ((0, 2),))
    norm_gain = jnp.clip(1.0 + 0.15 * jax.random.normal(seeds[8], (2, 3, D), jnp.float32), 0.25, 1.75).astype(jnp.bfloat16)
    norm_bias = scatter_about(seeds[9], (2, 3, D), 0.2, 1.0, ((0, 2),))
    return {"embeddings": embeddings, "segments": segments, "cotangent": cotangent, "attn_qkv": attn_qkv, "attn_out": attn_out, "cross_proj": cross_proj, "ffn_up": ffn_up, "ffn_down": ffn_down, "norm_gain": norm_gain, "norm_bias": norm_bias}


@jax.custom_vjp
def low(v):
    return lax.optimization_barrier(v.astype(jnp.bfloat16)).astype(jnp.float32)

@jax.custom_vjp
def low_back(v):
    return v

def low_keep(v):
    return (low(v), None)

def low_pass(kept, grad):
    return (grad,)

def back_keep(v):
    return (v, None)

def back_low(kept, grad):
    return (low(grad),)
low.defvjp(low_keep, low_pass)
low_back.defvjp(back_keep, back_low)
highest = lax.Precision.HIGHEST
epsilon = 1e-05
masked_score = -1e+30

def round_both(values):
    return low(low_back(values))

def matmul(left_side, right_side):
    return jnp.dot(left_side, right_side, precision=highest)

def layer_norm(values, gain_vec, bias_vec):
    center = values - lax.optimization_barrier(jnp.mean(values, axis=-1, keepdims=True))
    spread = lax.optimization_barrier(jnp.mean(center * center, axis=-1, keepdims=True))
    return center * lax.rsqrt(spread + epsilon) * gain_vec + bias_vec

def split_heads(values):
    return values.reshape(values.shape[0], HEADS, values.shape[1] // HEADS)

def attend(queries, key_rows, value_rows, allowed):
    score_scale = (queries.shape[1] // HEADS) ** (-0.5)
    scores = low_back(jnp.einsum('qhd,khd->hqk', split_heads(queries), split_heads(key_rows), precision=highest) * score_scale)
    scores = jnp.where(allowed[None], scores, masked_score)
    row_top = lax.optimization_barrier(jnp.max(scores, axis=-1, keepdims=True))
    exponent = jnp.exp(scores - row_top)
    attention = low(exponent / lax.optimization_barrier(jnp.sum(exponent, axis=-1, keepdims=True)))
    mixed_heads = jnp.einsum('hqk,khd->qhd', attention, split_heads(value_rows), precision=highest)
    return round_both(mixed_heads.reshape(queries.shape))

def feed_forward(hidden, up_weight, down_weight):
    up_values = low_back(matmul(low(hidden), up_weight))
    activated = low(up_values * jax.nn.sigmoid(up_values))
    return low_back(matmul(activated, down_weight))

def encoder_row(source, source_ids, qkv_weight, out_weight, kv_weight, up_weight, down_weight, gains, biases):
    features = source.shape[1]
    first_norm = layer_norm(source, gains[0], biases[0])
    packed = round_both(matmul(low(first_norm), qkv_weight))
    allowed = source_ids[:, None] == source_ids[None, :]
    mixed_heads = attend(packed[:, :features], packed[:, features:2 * features], packed[:, 2 * features:], allowed)
    hidden = layer_norm(first_norm + low_back(matmul(mixed_heads, out_weight)), gains[1], biases[1])
    hidden = layer_norm(hidden + feed_forward(hidden, up_weight, down_weight), gains[2], biases[2])
    return (hidden, round_both(matmul(low(hidden), kv_weight)))

def decoder_row(target, target_ids, source_ids, memory_kv, qkv_weight, out_weight, query_weight, output_weight, up_weight, down_weight, gains, biases):
    features = target.shape[1]
    packed = round_both(matmul(low(target), qkv_weight))
    places = jnp.arange(target.shape[0])
    allowed = (target_ids[:, None] == target_ids[None, :]) & (places[None, :] <= places[:, None])
    mixed_heads = attend(packed[:, :features], packed[:, features:2 * features], packed[:, 2 * features:], allowed)
    hidden_one = layer_norm(target + low_back(matmul(mixed_heads, out_weight)), gains[0], biases[0])
    queries = round_both(matmul(low(hidden_one), query_weight))
    cross_allowed = target_ids[:, None] == source_ids[None, :]
    cross_mixed = attend(queries, memory_kv[:, :features], memory_kv[:, features:], cross_allowed)
    hidden_two = layer_norm(hidden_one + low_back(matmul(cross_mixed, output_weight)), gains[1], biases[1])
    return layer_norm(hidden_two + feed_forward(hidden_two, up_weight, down_weight), gains[2], biases[2])

def forward(embeds, qkv_all, out_all, cross_all, up_all, down_all, gain_all, bias_all, segments):
    features = embeds.shape[-1]

    def row_step(carry, operands):
        source, target, source_ids, target_ids = operands
        memory, memory_kv = encoder_row(source, source_ids, qkv_all[0], out_all[0], cross_all[0], up_all[0], down_all[0], gain_all[0], bias_all[0])
        result = decoder_row(target, target_ids, source_ids, memory_kv, qkv_all[1], out_all[1], cross_all[1][:, :features], cross_all[1][:, features:], up_all[1], down_all[1], gain_all[1], bias_all[1])
        return (carry, (memory, result))
    ignored, outputs = lax.scan(jax.checkpoint(row_step), jnp.zeros((), jnp.float32), (embeds[0], embeds[1], segments[0], segments[1]))
    return outputs

def reference(embeddings, segments, cotangent, attn_qkv, attn_out, cross_proj, ffn_up, ffn_down, norm_gain, norm_bias):
    primals = tuple((member.astype(jnp.float32) for member in (embeddings, attn_qkv, attn_out, cross_proj, ffn_up, ffn_down, norm_gain, norm_bias)))

    def whole(embeds, qkv_all, out_all, cross_all, up_all, down_all, gain_all, bias_all):
        return forward(embeds, qkv_all, out_all, cross_all, up_all, down_all, gain_all, bias_all, segments)
    (memory, result), pullback = jax.vjp(whole, *primals)
    grads = pullback((jnp.zeros_like(memory), cotangent.astype(jnp.float32)))
    layer_out = jnp.stack([memory, result]).astype(jnp.bfloat16)
    return (layer_out, grads[0], grads[1], grads[2], grads[3], grads[4], grads[5], grads[6], grads[7])
```

```python
import jax
import jax.numpy as jnp
from jax import lax
from jax.sharding import PartitionSpec as P
import functools
from jax.experimental import pallas as pl
from jax.experimental.pallas import tpu as pltpu

bf16, f32 = jnp.bfloat16, jnp.float32
PARTS = 3

def ring_place(index, chips):
    chip = lax.div(index, 2)
    level, side = lax.div(chip, 2), lax.rem(chip, 2)
    return jnp.where(side == 0, level, chips - 1 - level)

def ring_device(place, chips, core):
    half = chips // 2
    chip = jnp.where(place < half, 2 * place, 2 * (chips - 1 - place) + 1)
    return 2 * chip + core

def sum_kernel(chips, local, total, paired, landed, pair_sems, ring_sems, gather_sems, share_sems):
    width = local.shape[1]
    part = width // PARTS
    me = lax.axis_index("dp")
    core = lax.rem(me, 2)
    place = ring_place(me, chips)
    sibling = me + 1 - 2 * core
    ahead = ring_device(lax.rem(place + 1, chips), chips, core)
    behind = ring_device(lax.rem(place + chips - 1, chips), chips, core)
    targets = (ahead, behind)

    barrier = pltpu.get_barrier_semaphore()
    for other in (sibling, ahead, behind):
        pl.semaphore_signal(barrier, inc=1, device_id={"dp": other}, device_id_type=pl.DeviceIdType.MESH)
    pl.semaphore_wait(barrier, 3)

    def slot(way, step):
        return lax.rem(place + (chips - step if way == 0 else step), chips)

    def rows(way, step, owner):
        return pl.ds(pl.multiple_of(64 * slot(way, step) + 32 * owner + 16 * way, 16), 16)

    def pair_copy(way, step):
        return pltpu.make_async_remote_copy(
            src_ref=local.at[rows(way, step, 1 - core)],
            dst_ref=paired.at[way, step],
            send_sem=pair_sems.at[0, way, step],
            recv_sem=pair_sems.at[1, way, step],
            device_id={"dp": sibling}, device_id_type=pl.DeviceIdType.MESH)

    def columns(p):
        return pl.ds(p * part, part)

    def ring_copy(way, step, p):
        return pltpu.make_async_remote_copy(
            src_ref=paired.at[way, step, :, columns(p)],
            dst_ref=landed.at[way, step, :, columns(p)],
            send_sem=ring_sems.at[0, way, step, p],
            recv_sem=ring_sems.at[1, way, step, p],
            device_id={"dp": targets[way]}, device_id_type=pl.DeviceIdType.MESH)

    def gather_copy(way, step, p):
        span = rows_gather(way, step)
        return pltpu.make_async_remote_copy(
            src_ref=total.at[span, columns(p)],
            dst_ref=total.at[span, columns(p)],
            send_sem=gather_sems.at[0, way, step, p],
            recv_sem=gather_sems.at[1, way, step, p],
            device_id={"dp": targets[way]}, device_id_type=pl.DeviceIdType.MESH)

    def rows_gather(way, step):
        shift = lax.rem(chips - 1 + step, chips)
        place_of = lax.rem(place + (chips - shift if way == 0 else shift), chips)
        return pl.ds(pl.multiple_of(64 * place_of + 32 * core + 16 * way, 16), 16)

    def share_copy(way, step):
        span = rows_gather(way, step)
        return pltpu.make_async_remote_copy(
            src_ref=total.at[span],
            dst_ref=total.at[span],
            send_sem=share_sems.at[0, way, step],
            recv_sem=share_sems.at[1, way, step],
            device_id={"dp": sibling}, device_id_type=pl.DeviceIdType.MESH)

    def pair_start(step, carry):
        for way in range(2):
            pair_copy(way, step).start()
        return carry
    lax.fori_loop(0, chips, pair_start, 0)

    for way in range(2):
        pair_copy(way, 0).wait_recv()
        for p in range(PARTS):
            mine = local[rows(way, 0, core), p * part:(p + 1) * part].astype(f32)
            paired[way, 0, :, p * part:(p + 1) * part] = (mine + paired[way, 0, :, p * part:(p + 1) * part].astype(f32)).astype(bf16)
            ring_copy(way, 0, p).start()

    def reduce_step(step, carry):
        for way in range(2):
            pair_copy(way, step).wait_recv()
        for p in range(PARTS):
            for way in range(2):
                ring_copy(way, step - 1, p).wait_recv()
                cols = slice(p * part, (p + 1) * part)
                mine = local[rows(way, step, core), cols].astype(f32)
                paired[way, step, :, cols] = (
                    mine + paired[way, step, :, cols].astype(f32) + landed[way, step - 1, :, cols].astype(f32)
                ).astype(bf16)
                ring_copy(way, step, p).start()
        return carry
    lax.fori_loop(1, chips - 1, reduce_step, 0)

    last = chips - 1
    for way in range(2):
        pair_copy(way, last).wait_recv()
    for p in range(PARTS):
        for way in range(2):
            ring_copy(way, last - 1, p).wait_recv()
            cols = slice(p * part, (p + 1) * part)
            mine = local[rows(way, last, core), cols].astype(f32)
            total[rows(way, last, core), cols] = (
                mine + paired[way, last, :, cols].astype(f32) + landed[way, last - 1, :, cols].astype(f32)
            ).astype(bf16)
            gather_copy(way, 0, p).start()
    for way in range(2):
        share_copy(way, 0).start()

    def gather_step(step, carry):
        for p in range(PARTS):
            for way in range(2):
                gather_copy(way, step - 1, p).wait_recv()
                gather_copy(way, step, p).start()
        for way in range(2):
            share_copy(way, step).start()
        return carry
    lax.fori_loop(1, chips - 1, gather_step, 0)
    for p in range(PARTS):
        for way in range(2):
            gather_copy(way, last - 1, p).wait_recv()
    for way in range(2):
        share_copy(way, last).start()

    def finish(step, carry):
        for way in range(2):
            pair_copy(way, step).wait_send()
            share_copy(way, step).wait()
        return carry
    lax.fori_loop(0, chips, finish, 0)

    def finish_ring(step, carry):
        for way in range(2):
            for p in range(PARTS):
                ring_copy(way, step, p).wait_send()
                gather_copy(way, step, p).wait_send()
        return carry
    lax.fori_loop(0, chips - 1, finish_ring, 0)


def sum_over(local, devices):
    chips = devices // 2
    width = local.shape[1]
    return pl.pallas_call(
        functools.partial(sum_kernel, chips),
        out_shape=jax.ShapeDtypeStruct(local.shape, bf16),
        in_specs=[pl.BlockSpec(memory_space=pltpu.VMEM)],
        out_specs=pl.BlockSpec(memory_space=pltpu.VMEM),
        scratch_shapes=[
            pltpu.VMEM((2, chips, 16, width), bf16),
            pltpu.VMEM((2, chips - 1, 16, width), bf16),
            pltpu.SemaphoreType.DMA((2, 2, chips)),
            pltpu.SemaphoreType.DMA((2, 2, chips - 1, PARTS)),
            pltpu.SemaphoreType.DMA((2, 2, chips - 1, PARTS)),
            pltpu.SemaphoreType.DMA((2, 2, chips)),
        ],
        compiler_params=pltpu.CompilerParams(collective_id=0, has_side_effects=True, vmem_limit_bytes=60 << 20),
    )(local)

HEADS = 8


epsilon = 1e-05
masked_score = -1e30


def shifted(shard, axis, by):
    size = lax.axis_size(axis)
    pairs = [(i, i + by) for i in range(size) if 0 <= i + by < size]
    return lax.ppermute(shard, axis, pairs)


def matmul(left_side, right_side):
    return jnp.dot(left_side, right_side, preferred_element_type=jnp.float32)


def left_product(left_side, right_side):
    return lax.dot_general(
        left_side, right_side, (((0,), (0,)), ((), ())), preferred_element_type=jnp.float32
    )


def right_product(left_side, right_side):
    return lax.dot_general(
        left_side, right_side, (((1,), (1,)), ((), ())), preferred_element_type=jnp.float32
    )


def normalize(values, gain_vec, bias_vec):
    center = values - jnp.mean(values, axis=-1, keepdims=True)
    spread = jnp.mean(center * center, axis=-1, keepdims=True)
    return center * lax.rsqrt(spread + epsilon) * gain_vec + bias_vec


def split_heads(values):
    return values.reshape(values.shape[0], HEADS, values.shape[1] // HEADS)


def scores_of(query_row, key_row, allowed_row):
    score_scale = (query_row.shape[1] // HEADS) ** (-0.5)
    scores = (
        jnp.einsum(
            "qhd,khd->hqk",
            split_heads(query_row),
            split_heads(key_row),
            preferred_element_type=jnp.float32,
        )
        * score_scale
    )
    return jnp.where(allowed_row[None], scores, masked_score)


def attend_rows(queries, key_rows, value_rows, allowed):

    def one_row(operands):
        query_row, key_row, value_row, allowed_row = operands
        scores = scores_of(query_row, key_row, allowed_row)
        row_top = jnp.max(scores, axis=-1, keepdims=True)
        exponent = jnp.exp(scores - row_top)
        total_mass = jnp.sum(exponent, axis=-1, keepdims=True)
        attention = (exponent / total_mass).astype(jnp.bfloat16)
        mixed_heads = jnp.einsum(
            "hqk,khd->qhd", attention, split_heads(value_row), preferred_element_type=jnp.float32
        )
        return (
            mixed_heads.reshape(query_row.shape).astype(jnp.bfloat16),
            row_top + jnp.log(total_mass),
        )

    return lax.map(one_row, (queries, key_rows, value_rows, allowed))


def attend_back(queries, key_rows, value_rows, allowed, log_mass, grad_mixed):

    def one_row(operands):
        query_row, key_row, value_row, allowed_row, mass_row, grad_row = operands
        score_scale = (query_row.shape[1] // HEADS) ** (-0.5)
        attention = jnp.exp(scores_of(query_row, key_row, allowed_row) - mass_row)
        heads_grad = split_heads(grad_row)
        grad_attention = jnp.einsum(
            "qhd,khd->hqk", heads_grad, split_heads(value_row), preferred_element_type=jnp.float32
        )
        correction = jnp.sum(grad_attention * attention, axis=-1, keepdims=True)
        grad_scores = (attention * (grad_attention - correction)).astype(jnp.bfloat16)
        grads_q = (
            jnp.einsum(
                "hqk,khd->qhd",
                grad_scores,
                split_heads(key_row),
                preferred_element_type=jnp.float32,
            )
            * score_scale
        )
        grads_k = (
            jnp.einsum(
                "hqk,qhd->khd",
                grad_scores,
                split_heads(query_row),
                preferred_element_type=jnp.float32,
            )
            * score_scale
        )
        grads_v = jnp.einsum(
            "hqk,qhd->khd",
            attention.astype(jnp.bfloat16),
            heads_grad,
            preferred_element_type=jnp.float32,
        )
        return (
            grads_q.reshape(query_row.shape),
            grads_k.reshape(key_row.shape),
            grads_v.reshape(key_row.shape),
        )

    return lax.map(one_row, (queries, key_rows, value_rows, allowed, log_mass, grad_mixed))


def self_mask(segment_ids, causal):
    allowed = segment_ids[:, :, None] == segment_ids[:, None, :]
    if causal:
        places = jnp.arange(segment_ids.shape[-1])
        allowed = allowed & (places[None, :, None] >= places[None, None, :])
    return allowed


def self_forward(low_tokens, qkv_weight, allowed, row_count):
    features = low_tokens.shape[1]
    packed = (
        matmul(low_tokens, qkv_weight).astype(jnp.bfloat16).reshape(row_count, -1, 3 * features)
    )
    mixed_heads, log_mass = attend_rows(
        packed[..., :features],
        packed[..., features : 2 * features],
        packed[..., 2 * features :],
        allowed,
    )
    return (packed, mixed_heads.reshape(-1, features), log_mass)


def self_backward(packed, allowed, log_mass, grad_mixed):
    features = packed.shape[-1] // 3
    grads_q, grads_k, grads_v = attend_back(
        packed[..., :features],
        packed[..., features : 2 * features],
        packed[..., 2 * features :],
        allowed,
        log_mass,
        grad_mixed.reshape(packed.shape[0], packed.shape[1], features),
    )
    return (
        jnp.concatenate([grads_q, grads_k, grads_v], axis=-1)
        .reshape(-1, 3 * features)
        .astype(jnp.bfloat16)
    )


def feed_forward(low_hidden, up_weight, down_weight):
    up_values = matmul(low_hidden, up_weight)
    activated = (up_values * jax.nn.sigmoid(up_values)).astype(jnp.bfloat16)
    return (matmul(activated, down_weight), up_values, activated)


def feed_backward(low_hidden, up_weight, down_weight, up_values, activated, grad_output):
    sigmoid_up = jax.nn.sigmoid(up_values)
    grad_down = left_product(activated, grad_output)
    grad_active = right_product(grad_output, down_weight)
    grad_up_values = (grad_active * (sigmoid_up * (1.0 + up_values * (1.0 - sigmoid_up)))).astype(
        jnp.bfloat16
    )
    return (
        right_product(grad_up_values, up_weight),
        left_product(low_hidden, grad_up_values),
        grad_down,
    )


def encoder_forward(weights, embed, source_ids):
    qkv_weight, out_weight, kv_weight, up_weight, down_weight, gains, biases = weights
    row_count, positions, features = embed.shape
    tokens = embed.reshape(-1, features).astype(jnp.float32)
    first_norm = normalize(tokens, gains[0], biases[0])
    packed, mixed_heads, log_mass = self_forward(
        first_norm.astype(jnp.bfloat16), qkv_weight, self_mask(source_ids, False), row_count
    )
    hidden = normalize(first_norm + matmul(mixed_heads, out_weight), gains[1], biases[1])
    branch, up_values, activated = feed_forward(hidden.astype(jnp.bfloat16), up_weight, down_weight)
    hidden = normalize(hidden + branch, gains[2], biases[2])
    low_hidden = hidden.astype(jnp.bfloat16)
    return (low_hidden, matmul(low_hidden, kv_weight).astype(jnp.bfloat16))


def encoder_backward(weights, embed, source_ids, grad_memory):
    qkv_weight, out_weight, kv_weight, up_weight, down_weight, gains, biases = weights
    row_count, positions, features = embed.shape
    tokens = embed.reshape(-1, features).astype(jnp.float32)
    first_norm, pull_first = jax.vjp(normalize, tokens, gains[0], biases[0])
    low_first = first_norm.astype(jnp.bfloat16)
    allowed = self_mask(source_ids, False)
    packed, mixed_heads, log_mass = self_forward(low_first, qkv_weight, allowed, row_count)
    hidden_one, pull_one = jax.vjp(
        normalize, first_norm + matmul(mixed_heads, out_weight), gains[1], biases[1]
    )
    low_one = hidden_one.astype(jnp.bfloat16)
    branch, up_values, activated = feed_forward(low_one, up_weight, down_weight)
    hidden_two, pull_two = jax.vjp(normalize, hidden_one + branch, gains[2], biases[2])
    low_two = hidden_two.astype(jnp.bfloat16)
    grad_kv_weight = left_product(low_two, grad_memory)
    grad_two, gain_two, bias_two = pull_two(right_product(grad_memory, kv_weight))
    grad_hidden, grad_up, grad_down = feed_backward(
        low_one, up_weight, down_weight, up_values, activated, grad_two.astype(jnp.bfloat16)
    )
    grad_one, gain_one, bias_one = pull_one(grad_two + grad_hidden)
    grad_branch = grad_one.astype(jnp.bfloat16)
    grad_out_weight = left_product(mixed_heads, grad_branch)
    grad_packed = self_backward(
        packed, allowed, log_mass, right_product(grad_branch, out_weight).astype(jnp.bfloat16)
    )
    grad_qkv_weight = left_product(low_first, grad_packed)
    grad_tokens, gain_first, bias_first = pull_first(
        grad_one + right_product(grad_packed, qkv_weight)
    )
    grads = (
        grad_qkv_weight,
        grad_out_weight,
        grad_kv_weight,
        grad_up,
        grad_down,
        jnp.stack([gain_first, gain_one, gain_two]),
        jnp.stack([bias_first, bias_one, bias_two]),
    )
    return (grad_tokens, grads)


def decoder_backward(weights, embed, target_ids, source_ids, memory_kv, cotangent):
    qkv_weight, out_weight, cross_weight, up_weight, down_weight, gains, biases = weights
    row_count, positions, features = embed.shape
    query_weight = cross_weight[:, :features]
    output_weight = cross_weight[:, features:]
    tokens = embed.reshape(-1, features).astype(jnp.float32)
    lowered = embed.reshape(-1, features)
    own_mask = self_mask(target_ids, True)
    packed, mixed_heads, log_mass = self_forward(lowered, qkv_weight, own_mask, row_count)
    hidden_one, pull_one = jax.vjp(
        normalize, tokens + matmul(mixed_heads, out_weight), gains[0], biases[0]
    )
    low_one = hidden_one.astype(jnp.bfloat16)
    queries = (
        matmul(low_one, query_weight).astype(jnp.bfloat16).reshape(row_count, positions, features)
    )
    memory_rows = memory_kv.reshape(row_count, positions, 2 * features)
    cross_mask = target_ids[:, :, None] == source_ids[:, None, :]
    cross_mixed, cross_mass = attend_rows(
        queries, memory_rows[..., :features], memory_rows[..., features:], cross_mask
    )
    cross_mixed = cross_mixed.reshape(-1, features)
    hidden_two, pull_two = jax.vjp(
        normalize, hidden_one + matmul(cross_mixed, output_weight), gains[1], biases[1]
    )
    low_two = hidden_two.astype(jnp.bfloat16)
    branch, up_values, activated = feed_forward(low_two, up_weight, down_weight)
    result, pull_three = jax.vjp(normalize, hidden_two + branch, gains[2], biases[2])
    grad_three, gain_three, bias_three = pull_three(
        cotangent.reshape(-1, features).astype(jnp.float32)
    )
    grad_hidden, grad_up, grad_down = feed_backward(
        low_two, up_weight, down_weight, up_values, activated, grad_three.astype(jnp.bfloat16)
    )
    grad_two, gain_two, bias_two = pull_two(grad_three + grad_hidden)
    grad_cross_branch = grad_two.astype(jnp.bfloat16)
    grad_output_weight = left_product(cross_mixed, grad_cross_branch)
    grad_cross_mixed = (
        right_product(grad_cross_branch, output_weight)
        .astype(jnp.bfloat16)
        .reshape(row_count, positions, features)
    )
    grads_q, grads_k, grads_v = attend_back(
        queries,
        memory_rows[..., :features],
        memory_rows[..., features:],
        cross_mask,
        cross_mass,
        grad_cross_mixed,
    )
    grad_queries = grads_q.reshape(-1, features).astype(jnp.bfloat16)
    grad_memory = (
        jnp.concatenate([grads_k, grads_v], axis=-1).reshape(-1, 2 * features).astype(jnp.bfloat16)
    )
    grad_query_weight = left_product(low_one, grad_queries)
    grad_one, gain_one, bias_one = pull_one(grad_two + right_product(grad_queries, query_weight))
    grad_branch = grad_one.astype(jnp.bfloat16)
    grad_out_weight = left_product(mixed_heads, grad_branch)
    grad_packed = self_backward(
        packed, own_mask, log_mass, right_product(grad_branch, out_weight).astype(jnp.bfloat16)
    )
    grad_qkv_weight = left_product(lowered, grad_packed)
    grad_tokens = grad_one + right_product(grad_packed, qkv_weight)
    grads = (
        grad_qkv_weight,
        grad_out_weight,
        jnp.concatenate([grad_query_weight, grad_output_weight], axis=1),
        grad_up,
        grad_down,
        jnp.stack([gain_one, gain_two, gain_three]),
        jnp.stack([bias_one, bias_two, bias_three]),
    )
    return (result.astype(jnp.bfloat16), grad_tokens, grad_memory, grads)


def per_device(
    embeddings,
    segments,
    cotangent,
    attn_qkv,
    attn_out,
    cross_proj,
    ffn_up,
    ffn_down,
    norm_gain,
    norm_bias,
):
    is_encoder = lax.axis_index("section") == 0
    weights = (
        attn_qkv[0],
        attn_out[0],
        cross_proj[0],
        ffn_up[0],
        ffn_down[0],
        norm_gain[0].astype(jnp.float32),
        norm_bias[0].astype(jnp.float32),
    )
    embed = embeddings[0]
    row_total, positions, features = embed.shape
    zero_grads = tuple((jnp.zeros(member.shape, jnp.float32) for member in weights))
    pieces = 1
    per_piece = row_total // pieces
    token_count = per_piece * positions
    piece_index = 0
    first_row = piece_index * per_piece

    def active():
        return encoder_forward(weights, embed, segments[0, first_row : first_row + per_piece])

    def resting():
        return (
            jnp.zeros((token_count, features), jnp.bfloat16),
            jnp.zeros((token_count, 2 * features), jnp.bfloat16),
        )

    memory, memory_kv = lax.cond(is_encoder, active, resting)
    memories = [memory]
    received_list = [shifted(memory_kv, "section", 1)]
    grand_total = zero_grads
    piece_index = 0
    decode_first_row = piece_index * per_piece
    received = received_list[piece_index]

    def active():
        return decoder_backward(
            weights,
            embed,
            segments[1, decode_first_row : decode_first_row + per_piece],
            segments[0, decode_first_row : decode_first_row + per_piece],
            received,
            cotangent,
        )

    def resting():
        return (
            jnp.zeros((token_count, features), jnp.bfloat16),
            jnp.zeros((token_count, features), jnp.float32),
            jnp.zeros((token_count, 2 * features), jnp.bfloat16),
            zero_grads,
        )

    result, decoder_tokens, grad_memory, decoder_grads = lax.cond(is_encoder, resting, active)
    returned = shifted(grad_memory, "section", -1)
    encode_first_row = piece_index * per_piece

    def active():
        return encoder_backward(
            weights, embed, segments[0, encode_first_row : encode_first_row + per_piece], returned
        )

    def resting():
        return (jnp.zeros((token_count, features), jnp.float32), zero_grads)

    encoder_tokens, encoder_grads = lax.cond(is_encoder, active, resting)
    block_sum = tuple(
        (
            jnp.add(first_term, second_term)
            for first_term, second_term in zip(decoder_grads, encoder_grads)
        )
    )
    grand_total = tuple(
        (
            jnp.add(first_term, second_term)
            for first_term, second_term in zip(grand_total, block_sum)
        )
    )
    results = jnp.where(is_encoder, memories[piece_index], result)
    token_grads = decoder_tokens + encoder_tokens
    grand_total = sum_gradients(grand_total)
    layer_out = results.reshape(1, row_total, positions, features)
    input_grad = token_grads.reshape(1, row_total, positions, features)
    return (
        layer_out,
        input_grad,
        grand_total[0][None],
        grand_total[1][None],
        grand_total[2][None],
        grand_total[3][None],
        grand_total[4][None],
        grand_total[5][None],
        grand_total[6][None],
    )


def sum_gradients(grads):
    qkv, out, cross, up, down, gain, bias = grads
    features, hidden = up.shape
    devices = lax.axis_size("dp")
    blocks = hidden // features
    norms = jnp.concatenate([gain, bias]).T
    norms = jnp.pad(norms, ((0, 0), (0, 128 - norms.shape[1])))
    packed = jnp.concatenate(
        [qkv, out, cross, up]
        + [down[i * features : (i + 1) * features] for i in range(blocks)]
        + [norms],
        axis=1,
    ).astype(bf16)
    if features == 32 * devices:
        packed = sum_over(packed, devices)
    else:
        packed = lax.psum(packed, "dp")
    packed = packed.astype(f32)
    pieces, start = [], 0
    for member in (qkv, out, cross, up):
        pieces.append(packed[:, start : start + member.shape[1]])
        start += member.shape[1]
    down = jnp.concatenate(
        [packed[:, start + i * features : start + (i + 1) * features] for i in range(blocks)]
    )
    norms = packed[:, start + blocks * features :]
    return (*pieces, down, norms[:, :3].T, norms[:, 3:6].T)


def solution(mesh):
    in_specs = (
        P("section", "dp", None, None),
        P(None, "dp", None),
        P("dp", None, None),
        P("section", None, None),
        P("section", None, None),
        P("section", None, None),
        P("section", None, None),
        P("section", None, None),
        P("section", None, None),
        P("section", None, None),
    )
    out_specs = (
        P("section", "dp", None, None),
        P("section", "dp", None, None),
        P("section", None, None),
        P("section", None, None),
        P("section", None, None),
        P("section", None, None),
        P("section", None, None),
        P("section", None, None),
        P("section", None, None),
    )
    return jax.shard_map(
        per_device, mesh=mesh, in_specs=in_specs, out_specs=out_specs, check_vma=False
    )
```

```python
import functools

import jax
import jax.numpy as jnp
from jax import lax
from jax.experimental import pallas as pl
from jax.experimental.pallas import tpu as pltpu
from jax.sharding import PartitionSpec as P

HEADS = 8
PAIRS = HEADS // 2
EPSILON = 1e-05
MASKED = -1e30
BLOCK = 256
VMEM_LIMIT = 60 << 20
bf16, f32 = jnp.bfloat16, jnp.float32


def nn(left, right):
    return lax.dot_general(left, right, (((1,), (0,)), ((), ())), preferred_element_type=f32)


def nt(left, right):
    return lax.dot_general(left, right, (((1,), (1,)), ((), ())), preferred_element_type=f32)


def tn(left, right):
    return lax.dot_general(left, right, (((0,), (0,)), ((), ())), preferred_element_type=f32)


def blocks(total):
    return [slice(i, i + BLOCK) for i in range(0, total, BLOCK)]


def standardize(values):
    center = values - jnp.mean(values, axis=-1, keepdims=True)
    scale = lax.rsqrt(jnp.mean(center * center, axis=-1, keepdims=True) + EPSILON)
    return center * scale, scale


def norm_back(grad, unit, scale, gain):
    scaled = grad * gain
    first = jnp.mean(scaled, axis=-1, keepdims=True)
    second = jnp.mean(scaled * unit, axis=-1, keepdims=True)
    return (scaled - first - unit * second) * scale


def fold(values):
    return jnp.sum(values.reshape(-1, 8, values.shape[-1]), axis=0)


def half_masks(value):
    lanes = lax.broadcasted_iota(jnp.int32, (1, 128), 1)
    return [jnp.where((lanes < 64) == (a == 0), value, 0.0).astype(bf16) for a in range(2)]


def pair_lanes(pair, start=0):
    return pl.ds(pl.multiple_of(start + pair * 128, 128), 128)


class Mover:
    def __init__(self, sems):
        self.sems, self.used, self.open = sems, 0, []

    def make(self, source, target):
        copy = pltpu.make_async_copy(source, target, self.sems.at[self.used])
        self.used += 1
        return copy

    def load(self, source, target):
        copy = self.make(source, target)
        copy.start()
        return copy

    def store(self, source, target):
        copy = self.make(source, target)
        copy.start()
        self.open.append(copy)

    def finish(self):
        for copy in self.open:
            copy.wait()
        self.open = []


def attend(q_ref, q_start, k_ref, k_start, v_ref, v_start, bias_ref, out_ref, mass_ref):
    scale = 64 ** -0.5
    masks = half_masks(scale)

    def one_pair(pair, carry):
        keys = k_ref[:, pair_lanes(pair, k_start)]
        values = v_ref[:, pair_lanes(pair, v_start)]
        lanes = lax.broadcasted_iota(jnp.int32, (BLOCK, 128), 1)
        for rows in blocks(q_ref.shape[0]):
            query = q_ref[rows, pair_lanes(pair, q_start)]
            mixed = []
            mass = mass_ref[rows, :]
            for a in range(2):
                scores = nt(query * masks[a], keys) + bias_ref[rows, :]
                top = jnp.max(scores, axis=-1, keepdims=True)
                weight = jnp.exp(scores - top)
                total = jnp.sum(weight, axis=-1, keepdims=True)
                mixed.append(nn(weight.astype(bf16), values) * (1.0 / total))
                mass = jnp.where(lanes == 2 * pair + a, top + jnp.log(total), mass)
            mass_ref[rows, :] = mass
            out_ref[rows, pair_lanes(pair)] = jnp.where(lanes < 64, mixed[0], mixed[1]).astype(bf16)
        return carry

    lax.fori_loop(0, PAIRS, one_pair, 0)


def head_sums(left_ref, right_ref, out_ref):
    features = left_ref.shape[1]
    depth = features // HEADS
    heads = lax.broadcasted_iota(jnp.int32, (HEADS, features), 0)
    members = lax.broadcasted_iota(jnp.int32, (HEADS, features), 1) // depth
    pick = jnp.where(heads == members, 1.0, 0.0).astype(bf16)
    for rows in blocks(left_ref.shape[0]):
        product = left_ref[rows, :].astype(f32) * right_ref[rows, :].astype(f32)
        high = product.astype(bf16)
        low = (product - high.astype(f32)).astype(bf16)
        out_ref[:, rows] = nt(pick, high) + nt(pick, low)


def attend_back(q_ref, q_start, k_ref, k_start, v_ref, v_start, grad_ref, bias_ref, mass_ref,
                delta_ref, dq_ref, dq_start, dk_ref, dk_start, dv_ref, dv_start, turned_ref):
    scale = 64 ** -0.5
    scaled, plain = half_masks(scale), half_masks(1.0)

    def one_pair(pair, carry):
        query = q_ref[:, pair_lanes(pair, q_start)]
        grad = grad_ref[:, pair_lanes(pair)]
        queries = [query * m for m in scaled]
        grads = [grad * m for m in plain]
        for index, rows in enumerate(blocks(k_ref.shape[0])):
            keys = k_ref[rows, pair_lanes(pair, k_start)]
            values = v_ref[rows, pair_lanes(pair, v_start)]
            dk, dv, turned = 0.0, 0.0, 0.0
            for a in range(2):
                head = pl.ds(2 * pair + a, 1)
                scores = nt(keys, queries[a]) + bias_ref[rows, :]
                weight = jnp.exp(scores - mass_ref[head, :])
                dv = dv + nn(weight.astype(bf16), grads[a])
                inner = nt(values, grads[a]) - delta_ref[head, :]
                slope = (weight * inner).astype(bf16)
                dk = dk + nn(slope, queries[a])
                turned = turned + nn((keys * scaled[a]).T, slope)
            dk_ref[rows, pair_lanes(pair, dk_start)] = dk.astype(bf16)
            dv_ref[rows, pair_lanes(pair, dv_start)] = dv.astype(bf16)
            if index == 0:
                turned_ref[...] = turned
            else:
                turned_ref[...] += turned
        dq_ref[:, pair_lanes(pair, dq_start)] = turned_ref[...].T.astype(bf16)
        return carry

    lax.fori_loop(0, PAIRS, one_pair, 0)


def as_column(row):
    return jnp.broadcast_to(row, (128, row.shape[1])).T[:, :1]


def self_bias(ids_row, is_encoder, turned):
    size = ids_row.shape[1]
    column = as_column(ids_row.astype(f32))
    place_row = lax.broadcasted_iota(jnp.int32, (size, size), 1)
    place_column = lax.broadcasted_iota(jnp.int32, (size, size), 0)
    order = place_column - place_row if turned else place_row - place_column
    allowed = (column == ids_row.astype(f32)) & ((order <= 0) | is_encoder)
    return jnp.where(allowed, 0.0, MASKED)


def cross_bias(column_ids, row_ids):
    column = as_column(column_ids.astype(f32))
    return jnp.where(column == row_ids.astype(f32), 0.0, MASKED)


def role():
    return lax.axis_index("section") == 0


def front_kernel(row, x_hbm, ids_ref, qkv_hbm, out_hbm, cross_hbm, up_hbm, down_hbm, gain_ref, shift_ref,
                 lowin_o, packed_o, mixed_o, mass_o, unit_o, scale_o, low_o, hidden_o, z_o, slope_o,
                 unit2_o, scale2_o, tail_o,
                 x_v, wqkv, wout, wq, wup, wdown, base_v, bias_v, lowin_v, packed_v, mixed_v, mass_v,
                 massrow_v, unit_v, scale_v, low_v, z_v, slope_v, unit2_v, scale2_v, tail_v, sems):
    is_encoder = role()
    features = x_v.shape[1]
    move = Mover(sems)
    load_x = move.load(x_hbm.at[0, row], x_v)
    load_qkv = move.load(qkv_hbm.at[0], wqkv)
    load_out = move.load(out_hbm.at[0], wout)
    load_up = move.make(up_hbm.at[0], wup)
    load_down = move.make(down_hbm.at[0], wdown)
    load_q = move.make(cross_hbm.at[0, :, pl.ds(0, features)], wq)

    @pl.when(is_encoder)
    def _():
        load_up.start()
        load_down.start()

    @pl.when(jnp.logical_not(is_encoder))
    def _():
        load_q.start()

    ids_row = jnp.where(is_encoder, ids_ref[pl.ds(0, 1), row, :], ids_ref[pl.ds(1, 1), row, :])
    bias_v[...] = self_bias(ids_row, is_encoder, False)
    mass_v[...] = jnp.zeros_like(mass_v)
    load_x.wait()

    @pl.when(is_encoder)
    def _():
        for rows in blocks(x_v.shape[0]):
            unit, _ = standardize(x_v[rows, :].astype(f32))
            value = unit * gain_ref[0:1, :] + shift_ref[0:1, :]
            base_v[rows, :] = value
            lowin_v[rows, :] = value.astype(bf16)

    @pl.when(jnp.logical_not(is_encoder))
    def _():
        base_v[...] = x_v[...].astype(f32)
        lowin_v[...] = x_v[...]

    move.store(lowin_v, lowin_o)
    load_qkv.wait()
    for rows in blocks(x_v.shape[0]):
        packed_v[rows, :] = nn(lowin_v[rows, :], wqkv[...]).astype(bf16)
    move.store(packed_v, packed_o)
    attend(packed_v, 0, packed_v, features, packed_v, 2 * features, bias_v, mixed_v, mass_v)
    massrow_v[...] = mass_v[...].T[:HEADS, :]
    move.store(massrow_v, mass_o)
    move.store(mixed_v, mixed_o)
    load_out.wait()
    which = jnp.where(is_encoder, 1, 0)
    gain, shift = gain_ref[pl.ds(which, 1), :], shift_ref[pl.ds(which, 1), :]
    for rows in blocks(x_v.shape[0]):
        unit, scale = standardize(base_v[rows, :] + nn(mixed_v[rows, :], wout[...]))
        unit_v[rows, :] = unit.astype(bf16)
        scale_v[rows, :] = jnp.broadcast_to(scale, (BLOCK, 128))
        hidden = unit * gain + shift
        base_v[rows, :] = hidden
        low_v[rows, :] = hidden.astype(bf16)
    move.store(unit_v, unit_o)
    move.store(scale_v, scale_o)
    move.store(low_v, low_o)

    store_hidden = move.make(base_v, hidden_o)
    stores = [move.make(a, b) for a, b in ((z_v, z_o), (slope_v, slope_o), (unit2_v, unit2_o), (scale2_v, scale2_o))]

    @pl.when(jnp.logical_not(is_encoder))
    def _():
        store_hidden.start()
        load_q.wait()
        for rows in blocks(x_v.shape[0]):
            tail_v[rows, :] = nn(low_v[rows, :], wq[...]).astype(bf16)
        store_hidden.wait()

    @pl.when(is_encoder)
    def _():
        load_up.wait()
        load_down.wait()
        for rows in blocks(x_v.shape[0]):
            feed_forward(low_v, rows, wup, z_v, slope_v)
            unit, scale = standardize(base_v[rows, :] + nn(z_v[rows, :], wdown[...]))
            unit2_v[rows, :] = unit.astype(bf16)
            scale2_v[rows, :] = jnp.broadcast_to(scale, (BLOCK, 128))
            tail_v[rows, :] = (unit * gain_ref[2:3, :] + shift_ref[2:3, :]).astype(bf16)
        for copy in stores:
            copy.start()
        for copy in stores:
            copy.wait()

    move.store(tail_v, tail_o)
    move.finish()


def feed_forward(low_ref, rows, wup, z_ref, slope_ref):
    for start in range(0, wup.shape[1], 512):
        columns = slice(start, start + 512)
        up = nn(low_ref[rows, :], wup[:, columns])
        gate = 1.0 / (1.0 + jnp.exp(-up))
        z = up * gate
        z_ref[rows, columns] = z.astype(bf16)
        slope_ref[rows, columns] = (gate + z * (1.0 - gate)).astype(bf16)


def feed_back(grad_ref, rows, wup, wdown, slope_ref, du_ref):
    for start in range(0, wup.shape[1], 512):
        columns = slice(start, start + 512)
        dz = nt(grad_ref[rows, :], wdown[columns, :])
        du_ref[rows, columns] = (dz * slope_ref[rows, columns].astype(f32)).astype(bf16)
    return nt(du_ref[rows, :], wup[...])


def cross_kernel(row, memory_hbm, query_hbm, hidden_hbm, cot_hbm, ids_ref, kv_hbm, cross_hbm, up_hbm, down_hbm,
                 gain_ref, shift_ref,
                 out_o, low_o, z_o, du_o, df_o, mixed_o, dbranch_o, dr_o, dq_o, dkv_o, dmem_o, sums_o,
                 memory_v, query_v, hidden_v, cot_v, wkv, wout, wup, wdown, kv_v, bias_v, mixed_v, mass_v, massrow_v,
                 delta_v, low_v, z_v, slope_v, unit_v, scale_v, du_v, df_v, dbranch_v, dmixed_v, dq_v, dkv_v, dmem_v,
                 out_v, turned_v, sums_v, sems):
    is_encoder = role()
    features = memory_v.shape[1]
    size = memory_v.shape[0]

    @pl.when(jnp.logical_not(is_encoder))
    def _():
        move = Mover(sems)
        load_kv = move.load(kv_hbm, wkv)
        load_memory = move.load(memory_hbm, memory_v)
        load_query = move.load(query_hbm, query_v)
        load_hidden = move.load(hidden_hbm, hidden_v)
        load_out = move.load(cross_hbm.at[0, :, pl.ds(features, features)], wout)
        load_up = move.load(up_hbm.at[0], wup)
        load_down = move.load(down_hbm.at[0], wdown)
        load_cot = move.load(cot_hbm.at[row], cot_v)
        source, target = ids_ref[0, row:row + 1, :], ids_ref[1, row:row + 1, :]
        bias_v[...] = cross_bias(target, source)
        mass_v[...] = jnp.zeros_like(mass_v)
        sums_v[...] = jnp.zeros_like(sums_v)
        load_kv.wait()
        load_memory.wait()
        for rows in blocks(size):
            kv_v[rows, :] = nn(memory_v[rows, :], wkv[...]).astype(bf16)
        load_query.wait()
        attend(query_v, 0, kv_v, 0, kv_v, features, bias_v, mixed_v, mass_v)
        massrow_v[...] = mass_v[...].T[:HEADS, :]
        move.store(mixed_v, mixed_o)
        load_hidden.wait()
        load_out.wait()
        for rows in blocks(size):
            unit, scale = standardize(hidden_v[rows, :] + nn(mixed_v[rows, :], wout[...]))
            unit_v[rows, :] = unit.astype(bf16)
            scale_v[rows, :] = jnp.broadcast_to(scale, (BLOCK, 128))
            hidden = unit * gain_ref[1:2, :] + shift_ref[1:2, :]
            hidden_v[rows, :] = hidden
            low_v[rows, :] = hidden.astype(bf16)
        move.store(low_v, low_o)
        load_up.wait()
        load_down.wait()
        load_cot.wait()
        for rows in blocks(size):
            feed_forward(low_v, rows, wup, z_v, slope_v)
            unit, scale = standardize(hidden_v[rows, :] + nn(z_v[rows, :], wdown[...]))
            out_v[rows, :] = (unit * gain_ref[2:3, :] + shift_ref[2:3, :]).astype(bf16)
            grad = cot_v[rows, :].astype(f32)
            sums_v[2] += fold(grad * unit)
            sums_v[5] += fold(grad)
            dr = norm_back(grad, unit, scale, gain_ref[2:3, :])
            hidden_v[rows, :] = dr
            df_v[rows, :] = dr.astype(bf16)
        move.store(z_v, z_o)
        move.store(df_v, df_o)
        move.store(out_v, out_o)
        for rows in blocks(size):
            grad = hidden_v[rows, :] + feed_back(df_v, rows, wup, wdown, slope_v, du_v)
            unit = unit_v[rows, :].astype(f32)
            sums_v[1] += fold(grad * unit)
            sums_v[4] += fold(grad)
            dr = norm_back(grad, unit, scale_v[rows, :1], gain_ref[1:2, :])
            hidden_v[rows, :] = dr
            dbranch_v[rows, :] = dr.astype(bf16)
            dmixed_v[rows, :] = nt(dbranch_v[rows, :], wout[...]).astype(bf16)
        move.store(du_v, du_o)
        move.store(dbranch_v, dbranch_o)
        move.store(hidden_v, dr_o)
        move.store(sums_v, sums_o)
        bias_v[...] = cross_bias(source, target)
        head_sums(dmixed_v, mixed_v, delta_v)
        attend_back(query_v, 0, kv_v, 0, kv_v, features, dmixed_v, bias_v, massrow_v, delta_v,
                    dq_v, 0, dkv_v, 0, dkv_v, features, turned_v)
        move.store(dq_v, dq_o)
        move.store(dkv_v, dkv_o)
        for rows in blocks(size):
            dmem_v[rows, :] = nt(dkv_v[rows, :], wkv[...]).astype(bf16)
        move.store(dmem_v, dmem_o)
        move.finish()


def back_kernel(enc_row, dec_row, dmem_hbm, unit2_hbm, scale2_hbm, slope_hbm, dr_hbm, dq_hbm,
                eunit_hbm, escale_hbm, epacked_hbm, emixed_hbm, emass_hbm,
                dunit_hbm, dscale_hbm, dpacked_hbm, dmixed_hbm, dmass_hbm,
                x_hbm, ids_ref, qkv_hbm, out_hbm, cross_hbm, up_hbm, down_hbm, gain_ref,
                du_o, df_o, dbranch_o, dpacked_o, dx_o, sums_o,
                dmem_v, unit2_v, scale2_v, slope_v, dr_v, dq_v, unit_v, scale_v, packed_v, mixed_v, mass_v, x_v,
                wqkv, wout, wq, wup, wdown, bias_v, delta_v, du_v, df_v, dbranch_v, dout_v, dpacked_v, turned_v,
                sums_v, sems):
    is_encoder = role()
    features = mixed_v.shape[1]
    size = mixed_v.shape[0]

    def run():
        move = Mover(sems)
        is_decoder = jnp.logical_not(is_encoder)
        load_dmem = move.make(dmem_hbm, dmem_v)
        load_unit2 = move.make(unit2_hbm, unit2_v)
        load_scale2 = move.make(scale2_hbm, scale2_v)
        load_slope = move.make(slope_hbm, slope_v)
        load_down = move.make(down_hbm.at[0], wdown)
        load_up = move.make(up_hbm.at[0], wup)
        load_dr = move.make(dr_hbm, dr_v)
        load_dq = move.make(dq_hbm, dq_v)
        load_q = move.make(cross_hbm.at[0, :, pl.ds(0, features)], wq)
        firsts = [load_dmem, load_unit2, load_scale2, load_down, load_slope, load_up]

        sums_v[...] = jnp.zeros_like(sums_v)
        enc_selfs = [(eunit_hbm, unit_v), (escale_hbm, scale_v), (emixed_hbm, mixed_v), (epacked_hbm, packed_v), (emass_hbm, mass_v)]
        dec_selfs = [(dunit_hbm, unit_v), (dscale_hbm, scale_v), (dmixed_hbm, mixed_v), (dpacked_hbm, packed_v), (dmass_hbm, mass_v)]
        enc_pairs, dec_pairs = [], []
        for (es, ev), (ds, dv) in zip(enc_selfs, dec_selfs):
            enc_pairs.append(move.make(es, ev))
            dec_pairs.append(pltpu.make_async_copy(ds, dv, sems.at[move.used - 1]))
        load_x = move.make(x_hbm.at[0, enc_row or 0], x_v)
        load_out = move.make(out_hbm.at[0], wout)
        load_qkv = move.make(qkv_hbm.at[0], wqkv)

        @pl.when(is_encoder)
        def _():
            for copy in firsts:
                copy.start()
            for copy in enc_pairs:
                copy.start()
            load_x.start()

        @pl.when(is_decoder)
        def _():
            load_dq.start()
            load_q.start()
            load_dr.start()
            for copy in dec_pairs:
                copy.start()

        load_out.start()
        load_qkv.start()
        enc_ids, dec_ids = ids_ref[0:1, enc_row or 0, :], ids_ref[1:2, dec_row or 0, :]
        ids_row = jnp.where(is_encoder, enc_ids, dec_ids)
        bias_v[...] = self_bias(ids_row, is_encoder, True)

        stores = [move.make(du_v, du_o), move.make(df_v, df_o)]

        @pl.when(is_encoder)
        def _():
            for copy in firsts[:3]:
                copy.wait()
            for rows in blocks(size):
                grad = dmem_v[rows, :].astype(f32)
                unit = unit2_v[rows, :].astype(f32)
                sums_v[2] += fold(grad * unit)
                sums_v[5] += fold(grad)
                dr = norm_back(grad, unit, scale2_v[rows, :1], gain_ref[2:3, :])
                dr_v[rows, :] = dr
                df_v[rows, :] = dr.astype(bf16)
            stores[1].start()
            for copy in firsts[3:]:
                copy.wait()
            for rows in blocks(size):
                dr_v[rows, :] += feed_back(df_v, rows, wup, wdown, slope_v, du_v)
            stores[0].start()

        @pl.when(is_decoder)
        def _():
            load_dq.wait()
            load_q.wait()
            load_dr.wait()
            for rows in blocks(size):
                dr_v[rows, :] += nt(dq_v[rows, :], wq[...])

        for copy in enc_pairs:
            copy.wait()
        load_out.wait()
        which = jnp.where(is_encoder, 1, 0)
        gain = gain_ref[pl.ds(which, 1), :]
        for rows in blocks(size):
            grad = dr_v[rows, :]
            unit = unit_v[rows, :].astype(f32)
            sums_v[pl.ds(which, 1)] += fold(grad * unit)[None]
            sums_v[pl.ds(which + 3, 1)] += fold(grad)[None]
            dr = norm_back(grad, unit, scale_v[rows, :1], gain)
            dr_v[rows, :] = dr
            dbranch_v[rows, :] = dr.astype(bf16)
            dout_v[rows, :] = nt(dbranch_v[rows, :], wout[...]).astype(bf16)
        move.store(dbranch_v, dbranch_o)
        head_sums(dout_v, mixed_v, delta_v)
        attend_back(packed_v, 0, packed_v, features, packed_v, 2 * features, dout_v, bias_v, mass_v, delta_v,
                    dpacked_v, 0, dpacked_v, features, dpacked_v, 2 * features, turned_v)
        move.store(dpacked_v, dpacked_o)
        load_qkv.wait()
        for rows in blocks(size):
            dr_v[rows, :] += nt(dpacked_v[rows, :], wqkv[...])

        @pl.when(is_encoder)
        def _():
            load_x.wait()
            for rows in blocks(size):
                unit, scale = standardize(x_v[rows, :].astype(f32))
                grad = dr_v[rows, :]
                sums_v[0] += fold(grad * unit)
                sums_v[3] += fold(grad)
                dr_v[rows, :] = norm_back(grad, unit, scale, gain_ref[0:1, :])
            for copy in stores:
                copy.wait()

        move.store(dr_v, dx_o)
        move.store(sums_v, sums_o)
        move.finish()

    if enc_row is not None and dec_row is not None:
        run()
    elif enc_row is not None:
        pl.when(is_encoder)(run)
    else:
        pl.when(jnp.logical_not(is_encoder))(run)


def memory_weight_kernel(*refs):
    memories, grads, out_o = refs[0:3], refs[3:6], refs[6]
    left_v, right_v, out_v, sems = refs[7:]
    size = left_v.shape[0] // 3

    @pl.when(jnp.logical_not(role()))
    def _():
        move = Mover(sems)
        loads = []
        for i in range(3):
            loads.append(move.load(memories[i], left_v.at[pl.ds(i * size, size)]))
            loads.append(move.load(grads[i], right_v.at[pl.ds(i * size, size)]))
        for copy in loads:
            copy.wait()
        for start in range(0, right_v.shape[1], 512):
            out_v[:, start:start + 512] = tn(left_v[...], right_v[:, start:start + 512]).astype(bf16)
        move.store(out_v, out_o)
        move.finish()


def weight_kernel(count, *refs):
    names = ("lowin", "dpacked_e", "dpacked_d", "mixed", "dbranch_e", "dbranch_d", "low", "dq", "cmixed", "cdbranch",
             "du_e", "du_d", "clow", "z_e", "z_d", "df_e", "df_d")
    hbm = {name: refs[i * count:(i + 1) * count] for i, name in enumerate(names)}
    at = len(names) * count
    cross_hbm, esums, csums, bsums, = refs[at], refs[at + 1:at + 1 + count], refs[at + 1 + count:at + 1 + 2 * count], refs[at + 1 + 2 * count:at + 1 + 3 * count]
    out_o = refs[at + 1 + 3 * count]
    in_v, dpacked_v, mixed_v, dbranch_v, low_v, dq_v, cmixed_v, cdbranch_v, du_v, flow_v, z_v, df_v, cross_v, norm_v, out_v, sems = refs[at + 2 + 3 * count:]
    is_encoder = role()
    is_decoder = jnp.logical_not(is_encoder)
    size = in_v.shape[0] // count
    features = in_v.shape[1]
    move = Mover(sems)

    def gather(target, enc=None, dec=None):
        pieces = []
        for i in range(count):
            spot = target.at[pl.ds(i * size, size)]
            at = move.used
            move.used += 1
            pieces.append((enc and pltpu.make_async_copy(hbm[enc][i], spot, sems.at[at]),
                           dec and pltpu.make_async_copy(hbm[dec][i], spot, sems.at[at])))

        def start(side):
            for piece in pieces:
                piece[side].start()

        if enc:
            pl.when(is_encoder)(lambda: start(0))
        if dec:
            pl.when(is_decoder)(lambda: start(1))

        def wait():
            for piece in pieces:
                (piece[0] or piece[1]).wait()
        return wait

    wait_z = gather(z_v, "z_e", "z_d")
    wait_df = gather(df_v, "df_e", "df_d")
    wait_flow = gather(flow_v, "low", "clow")
    wait_du = gather(du_v, "du_e", "du_d")
    wait_in = gather(in_v, "lowin", "lowin")
    wait_dpacked = gather(dpacked_v, "dpacked_e", "dpacked_d")
    wait_mixed = gather(mixed_v, "mixed", "mixed")
    wait_dbranch = gather(dbranch_v, "dbranch_e", "dbranch_d")
    wait_low = gather(low_v, None, "low")
    wait_dq = gather(dq_v, None, "dq")
    wait_cmixed = gather(cmixed_v, None, "cmixed")
    wait_cdbranch = gather(cdbranch_v, None, "cdbranch")
    load_cross = move.make(cross_hbm, cross_v)
    pl.when(is_encoder)(load_cross.start)

    base = 6 * features
    qkv_width = dpacked_v.shape[1]

    def place(start, value):
        out_v[:, start:start + value.shape[1]] = value.astype(bf16)
    wait_z()
    wait_df()
    for j in range(0, z_v.shape[1], features):
        place(base + du_v.shape[1] + j, tn(z_v[:, j:j + features], df_v[...]))
    wait_flow()
    wait_du()
    for j in range(0, du_v.shape[1], features):
        place(base + j, tn(flow_v[...], du_v[:, j:j + features]))
    wait_in()
    wait_dpacked()
    for j in range(0, qkv_width, features):
        place(j, tn(in_v[...], dpacked_v[:, j:j + features]))
    wait_mixed()
    wait_dbranch()
    place(qkv_width, tn(mixed_v[...], dbranch_v[...]))

    @pl.when(is_encoder)
    def _():
        load_cross.wait()
        out_v[:, 4 * features:6 * features] = cross_v[...]
        total = sum(esum[...] for esum in esums)
        norm_v[0:6, :] = jnp.sum(total, axis=1)

    @pl.when(is_decoder)
    def _():
        wait_low()
        wait_dq()
        place(4 * features, tn(low_v[...], dq_v[...]))
        wait_cmixed()
        wait_cdbranch()
        place(5 * features, tn(cmixed_v[...], cdbranch_v[...]))
        total = sum(csum[...] + bsum[...] for csum, bsum in zip(csums, bsums))
        norm_v[0:6, :] = jnp.sum(total, axis=1)

    norm_v[6:, :] = jnp.zeros((norm_v.shape[0] - 6, features), f32)
    out_v[:, base + 2 * du_v.shape[1]:] = norm_v[...].T.astype(bf16)
    move.store(out_v, out_o)
    move.finish()


ANY = pl.BlockSpec(memory_space=pl.ANY)
IN_VMEM = pl.BlockSpec(memory_space=pltpu.VMEM)


def shape(*dims, dtype=bf16):
    return jax.ShapeDtypeStruct(dims, dtype)


def call(body, in_specs, outs, scratch, sems, args, flops=0):
    return pl.pallas_call(
        body,
        out_shape=outs,
        in_specs=in_specs,
        out_specs=[ANY] * len(outs),
        scratch_shapes=[pltpu.VMEM(s.shape, s.dtype) for s in scratch] + [pltpu.SemaphoreType.DMA((sems,))],
        compiler_params=pltpu.CompilerParams(vmem_limit_bytes=VMEM_LIMIT, has_side_effects=True),
        cost_estimate=pl.CostEstimate(flops=flops, bytes_accessed=10 << 20, transcendentals=0),
    )(*args)


def front(row, embed, ids, weights):
    qkv, out, cross, up, down, gain, shift = weights
    size, d = embed.shape[2:]
    hidden = up.shape[2]
    outs = [shape(size, d), shape(size, 3 * d), shape(size, d), shape(HEADS, size, dtype=f32), shape(size, d),
            shape(size, 128, dtype=f32), shape(size, d), shape(size, d, dtype=f32), shape(size, hidden),
            shape(size, hidden), shape(size, d), shape(size, 128, dtype=f32), shape(size, d)]
    scratch = [shape(size, d), shape(d, 3 * d), shape(d, d), shape(d, d), shape(d, hidden), shape(hidden, d),
               shape(size, d, dtype=f32), shape(size, size, dtype=f32), shape(size, d), shape(size, 3 * d),
               shape(size, d), shape(size, 128, dtype=f32), shape(HEADS, size, dtype=f32), shape(size, d),
               shape(size, 128, dtype=f32), shape(size, d), shape(size, hidden), shape(size, hidden),
               shape(size, d), shape(size, 128, dtype=f32), shape(size, d)]
    return call(functools.partial(front_kernel, row), [ANY, IN_VMEM] + [ANY] * 5 + [IN_VMEM] * 2, outs, scratch, 24,
                (embed, ids, qkv, out, cross, up, down, gain, shift), flops=8 * 10**9)


def cross(row, memory, query, hidden_f, cot, ids, kv_weight, weights):
    qkv, out, cross_w, up, down, gain, shift = weights
    size, d = memory.shape
    hidden = up.shape[2]
    outs = [shape(size, d), shape(size, d), shape(size, hidden), shape(size, hidden), shape(size, d), shape(size, d),
            shape(size, d), shape(size, d, dtype=f32), shape(size, d), shape(size, 2 * d), shape(size, d),
            shape(6, 8, d, dtype=f32)]
    scratch = [shape(size, d), shape(size, d), shape(size, d, dtype=f32), shape(size, d), shape(d, 2 * d),
               shape(d, d), shape(d, hidden), shape(hidden, d), shape(size, 2 * d), shape(size, size, dtype=f32),
               shape(size, d), shape(size, 128, dtype=f32), shape(HEADS, size, dtype=f32), shape(HEADS, size, dtype=f32),
               shape(size, d), shape(size, hidden), shape(size, hidden), shape(size, d), shape(size, 128, dtype=f32),
               shape(size, hidden), shape(size, d), shape(size, d), shape(size, d), shape(size, d), shape(size, 2 * d),
               shape(size, d), shape(size, d), shape(128, size, dtype=f32), shape(6, 8, d, dtype=f32)]
    return call(functools.partial(cross_kernel, row), [ANY] * 4 + [IN_VMEM] + [ANY] * 4 + [IN_VMEM] * 2, outs, scratch,
                24, (memory, query, hidden_f, cot, ids, kv_weight, cross_w, up, down, gain, shift), flops=20 * 10**9)


def back(enc_row, dec_row, dmem, e_front, d_front, d_cross, embed, ids, weights):
    qkv, out, cross_w, up, down, gain, shift = weights
    size, d = embed.shape[2:]
    hidden = up.shape[2]
    outs = [shape(size, hidden), shape(size, d), shape(size, d), shape(size, 3 * d), shape(size, d, dtype=f32),
            shape(6, 8, d, dtype=f32)]
    scratch = [shape(size, d), shape(size, d), shape(size, 128, dtype=f32), shape(size, hidden),
               shape(size, d, dtype=f32), shape(size, d), shape(size, d), shape(size, 128, dtype=f32),
               shape(size, 3 * d), shape(size, d), shape(HEADS, size, dtype=f32), shape(size, d),
               shape(d, 3 * d), shape(d, d), shape(d, d), shape(d, hidden), shape(hidden, d),
               shape(size, size, dtype=f32), shape(HEADS, size, dtype=f32), shape(size, hidden), shape(size, d),
               shape(size, d), shape(size, d), shape(size, 3 * d), shape(128, size, dtype=f32),
               shape(6, 8, d, dtype=f32)]
    args = (dmem, e_front["unit2"], e_front["scale2"], e_front["slope"], d_cross["dr"], d_cross["dq"],
            e_front["unit"], e_front["scale"], e_front["packed"], e_front["mixed"], e_front["mass"],
            d_front["unit"], d_front["scale"], d_front["packed"], d_front["mixed"], d_front["mass"],
            embed, ids, qkv, out, cross_w, up, down, gain)
    names = ("du", "df", "dbranch", "dpacked", "dx", "sums")
    results = call(functools.partial(back_kernel, enc_row, dec_row), [ANY] * 17 + [IN_VMEM] + [ANY] * 5 + [IN_VMEM],
                   outs, scratch, 28, args, flops=12 * 10**9)
    return dict(zip(names, results))


def per_device(embeddings, segments, cotangent, attn_qkv, attn_out, cross_proj, ffn_up, ffn_down, norm_gain, norm_bias):
    is_encoder = lax.axis_index("section") == 0
    weights = (attn_qkv, attn_out, cross_proj, ffn_up, ffn_down, norm_gain[0].astype(f32), norm_bias[0].astype(f32))
    row_total, size, d = embeddings.shape[1:]
    hidden = ffn_up.shape[2]
    devices = lax.axis_size("dp")
    kv_weight = lax.ppermute(cross_proj[0], "section", [(0, 1)])

    front_names = ("lowin", "packed", "mixed", "mass", "unit", "scale", "low", "hidden", "z", "slope", "unit2", "scale2", "tail")
    cross_names = ("out", "low", "z", "du", "df", "mixed", "dbranch", "dr", "dq", "dkv", "dmem", "sums")
    rows = range(row_total)
    fronts, memories = [], []
    for row in rows:
        fronts.append(dict(zip(front_names, front(row, embeddings, segments, weights))))
        memories.append(lax.ppermute(fronts[row]["tail"], "section", [(0, 1)]))
    crosses, grads = [], []
    for row in rows:
        crosses.append(dict(zip(cross_names, cross(
            row, memories[row], fronts[row]["tail"], fronts[row]["hidden"], cotangent, segments, kv_weight, weights))))
        grads.append(lax.ppermute(crosses[row]["dmem"], "section", [(1, 0)]))
    memory_weight = pl.pallas_call(
        memory_weight_kernel,
        out_shape=shape(d, 2 * d),
        in_specs=[ANY] * 6,
        out_specs=ANY,
        scratch_shapes=[pltpu.VMEM((row_total * size, d), bf16), pltpu.VMEM((row_total * size, 2 * d), bf16),
                        pltpu.VMEM((d, 2 * d), bf16), pltpu.SemaphoreType.DMA((8,))],
        compiler_params=pltpu.CompilerParams(vmem_limit_bytes=VMEM_LIMIT, has_side_effects=True),
        cost_estimate=pl.CostEstimate(flops=4 * 10**9, bytes_accessed=4 << 20, transcendentals=0),
    )(*memories, *[c["dkv"] for c in crosses])
    memory_weight = lax.ppermute(memory_weight, "section", [(1, 0)])

    backs_e, backs_d = [None] * row_total, [None] * row_total
    for step in range(row_total + 1):
        enc_row = step if step < row_total else None
        dec_row = step - 1 if step > 0 else None
        e, s = enc_row or 0, dec_row or 0
        if enc_row is None:
            e = row_total - 1
        result = back(enc_row, dec_row, grads[e], fronts[e], fronts[s], crosses[s], embeddings, segments, weights)
        if enc_row is not None:
            backs_e[enc_row] = result
        if dec_row is not None:
            backs_d[dec_row] = result

    lists = [
        [f["lowin"] for f in fronts], [b["dpacked"] for b in backs_e], [b["dpacked"] for b in backs_d],
        [f["mixed"] for f in fronts], [b["dbranch"] for b in backs_e], [b["dbranch"] for b in backs_d],
        [f["low"] for f in fronts], [c["dq"] for c in crosses], [c["mixed"] for c in crosses],
        [c["dbranch"] for c in crosses], [b["du"] for b in backs_e], [c["du"] for c in crosses],
        [c["low"] for c in crosses], [f["z"] for f in fronts], [c["z"] for c in crosses],
        [b["df"] for b in backs_e], [c["df"] for c in crosses],
    ]
    flat = [member for group in lists for member in group]
    sums = [b["sums"] for b in backs_e] + [c["sums"] for c in crosses] + [b["sums"] for b in backs_d]
    tokens = row_total * size
    width = 6 * d + 2 * hidden + 128
    scratch = [(tokens, d), (tokens, 3 * d), (tokens, d), (tokens, d), (tokens, d), (tokens, d), (tokens, d), (tokens, d),
               (tokens, hidden), (tokens, d), (tokens, hidden), (tokens, d), (d, 2 * d)]
    packed = pl.pallas_call(
        functools.partial(weight_kernel, row_total),
        out_shape=shape(d, width),
        in_specs=[ANY] * (len(flat) + 1) + [IN_VMEM] * len(sums),
        out_specs=ANY,
        scratch_shapes=[pltpu.VMEM(s, bf16) for s in scratch]
        + [pltpu.VMEM((128, d), f32), pltpu.VMEM((d, width), bf16), pltpu.SemaphoreType.DMA((12 * row_total + 2,))],
        compiler_params=pltpu.CompilerParams(vmem_limit_bytes=VMEM_LIMIT, has_side_effects=True),
        cost_estimate=pl.CostEstimate(flops=23 * 10**9, bytes_accessed=30 << 20, transcendentals=0),
    )(*flat, memory_weight, *sums)

    if d == 32 * devices:
        packed = sum_over(packed, devices)
    else:
        packed = lax.psum(packed, "dp")
    total = packed.astype(f32)
    pieces, start = [], 0
    for width in (3 * d, d, 2 * d, hidden):
        pieces.append(total[None, :, start:start + width])
        start += width
    down = jnp.concatenate([total[:, start + i:start + i + d] for i in range(0, hidden, d)])
    norms = total[:, start + hidden:].T
    layer_out = jnp.stack([jnp.where(is_encoder, f["tail"], c["out"]) for f, c in zip(fronts, crosses)])
    input_grad = jnp.stack([jnp.where(is_encoder, e["dx"], s["dx"]) for e, s in zip(backs_e, backs_d)])
    return (layer_out[None], input_grad[None], *pieces, down[None], norms[None, :3], norms[None, 3:6])


PARTS = 3

def ring_place(index, chips):
    chip = lax.div(index, 2)
    level, side = lax.div(chip, 2), lax.rem(chip, 2)
    return jnp.where(side == 0, level, chips - 1 - level)

def ring_device(place, chips, core):
    half = chips // 2
    chip = jnp.where(place < half, 2 * place, 2 * (chips - 1 - place) + 1)
    return 2 * chip + core

def sum_kernel(chips, local, total, paired, landed, pair_sems, ring_sems, gather_sems, share_sems):
    width = local.shape[1]
    part = width // PARTS
    me = lax.axis_index("dp")
    core = lax.rem(me, 2)
    place = ring_place(me, chips)
    sibling = me + 1 - 2 * core
    ahead = ring_device(lax.rem(place + 1, chips), chips, core)
    behind = ring_device(lax.rem(place + chips - 1, chips), chips, core)
    targets = (ahead, behind)

    barrier = pltpu.get_barrier_semaphore()
    for other in (sibling, ahead, behind):
        pl.semaphore_signal(barrier, inc=1, device_id={"dp": other}, device_id_type=pl.DeviceIdType.MESH)
    pl.semaphore_wait(barrier, 3)

    def slot(way, step):
        return lax.rem(place + (chips - step if way == 0 else step), chips)

    def rows(way, step, owner):
        return pl.ds(pl.multiple_of(64 * slot(way, step) + 32 * owner + 16 * way, 16), 16)

    def pair_copy(way, step):
        return pltpu.make_async_remote_copy(
            src_ref=local.at[rows(way, step, 1 - core)],
            dst_ref=paired.at[way, step],
            send_sem=pair_sems.at[0, way, step],
            recv_sem=pair_sems.at[1, way, step],
            device_id={"dp": sibling}, device_id_type=pl.DeviceIdType.MESH)

    def columns(p):
        return pl.ds(p * part, part)

    def ring_copy(way, step, p):
        return pltpu.make_async_remote_copy(
            src_ref=paired.at[way, step, :, columns(p)],
            dst_ref=landed.at[way, step, :, columns(p)],
            send_sem=ring_sems.at[0, way, step, p],
            recv_sem=ring_sems.at[1, way, step, p],
            device_id={"dp": targets[way]}, device_id_type=pl.DeviceIdType.MESH)

    def gather_copy(way, step, p):
        span = rows_gather(way, step)
        return pltpu.make_async_remote_copy(
            src_ref=total.at[span, columns(p)],
            dst_ref=total.at[span, columns(p)],
            send_sem=gather_sems.at[0, way, step, p],
            recv_sem=gather_sems.at[1, way, step, p],
            device_id={"dp": targets[way]}, device_id_type=pl.DeviceIdType.MESH)

    def rows_gather(way, step):
        shift = lax.rem(chips - 1 + step, chips)
        place_of = lax.rem(place + (chips - shift if way == 0 else shift), chips)
        return pl.ds(pl.multiple_of(64 * place_of + 32 * core + 16 * way, 16), 16)

    def share_copy(way, step):
        span = rows_gather(way, step)
        return pltpu.make_async_remote_copy(
            src_ref=total.at[span],
            dst_ref=total.at[span],
            send_sem=share_sems.at[0, way, step],
            recv_sem=share_sems.at[1, way, step],
            device_id={"dp": sibling}, device_id_type=pl.DeviceIdType.MESH)

    def pair_start(step, carry):
        for way in range(2):
            pair_copy(way, step).start()
        return carry
    lax.fori_loop(0, chips, pair_start, 0)

    for way in range(2):
        pair_copy(way, 0).wait_recv()
        for p in range(PARTS):
            mine = local[rows(way, 0, core), p * part:(p + 1) * part].astype(f32)
            paired[way, 0, :, p * part:(p + 1) * part] = (mine + paired[way, 0, :, p * part:(p + 1) * part].astype(f32)).astype(bf16)
            ring_copy(way, 0, p).start()

    def reduce_step(step, carry):
        for way in range(2):
            pair_copy(way, step).wait_recv()
        for p in range(PARTS):
            for way in range(2):
                ring_copy(way, step - 1, p).wait_recv()
                cols = slice(p * part, (p + 1) * part)
                mine = local[rows(way, step, core), cols].astype(f32)
                paired[way, step, :, cols] = (
                    mine + paired[way, step, :, cols].astype(f32) + landed[way, step - 1, :, cols].astype(f32)
                ).astype(bf16)
                ring_copy(way, step, p).start()
        return carry
    lax.fori_loop(1, chips - 1, reduce_step, 0)

    last = chips - 1
    for way in range(2):
        pair_copy(way, last).wait_recv()
    for p in range(PARTS):
        for way in range(2):
            ring_copy(way, last - 1, p).wait_recv()
            cols = slice(p * part, (p + 1) * part)
            mine = local[rows(way, last, core), cols].astype(f32)
            total[rows(way, last, core), cols] = (
                mine + paired[way, last, :, cols].astype(f32) + landed[way, last - 1, :, cols].astype(f32)
            ).astype(bf16)
            gather_copy(way, 0, p).start()
    for way in range(2):
        share_copy(way, 0).start()

    def gather_step(step, carry):
        for p in range(PARTS):
            for way in range(2):
                gather_copy(way, step - 1, p).wait_recv()
                gather_copy(way, step, p).start()
        for way in range(2):
            share_copy(way, step).start()
        return carry
    lax.fori_loop(1, chips - 1, gather_step, 0)
    for p in range(PARTS):
        for way in range(2):
            gather_copy(way, last - 1, p).wait_recv()
    for way in range(2):
        share_copy(way, last).start()

    def finish(step, carry):
        for way in range(2):
            pair_copy(way, step).wait_send()
            share_copy(way, step).wait()
        return carry
    lax.fori_loop(0, chips, finish, 0)

    def finish_ring(step, carry):
        for way in range(2):
            for p in range(PARTS):
                ring_copy(way, step, p).wait_send()
                gather_copy(way, step, p).wait_send()
        return carry
    lax.fori_loop(0, chips - 1, finish_ring, 0)


def sum_over(local, devices):
    chips = devices // 2
    width = local.shape[1]
    return pl.pallas_call(
        functools.partial(sum_kernel, chips),
        out_shape=jax.ShapeDtypeStruct(local.shape, bf16),
        in_specs=[pl.BlockSpec(memory_space=pltpu.VMEM)],
        out_specs=pl.BlockSpec(memory_space=pltpu.VMEM),
        scratch_shapes=[
            pltpu.VMEM((2, chips, 16, width), bf16),
            pltpu.VMEM((2, chips - 1, 16, width), bf16),
            pltpu.SemaphoreType.DMA((2, 2, chips)),
            pltpu.SemaphoreType.DMA((2, 2, chips - 1, PARTS)),
            pltpu.SemaphoreType.DMA((2, 2, chips - 1, PARTS)),
            pltpu.SemaphoreType.DMA((2, 2, chips)),
        ],
        compiler_params=pltpu.CompilerParams(collective_id=0, has_side_effects=True, vmem_limit_bytes=60 << 20),
    )(local)


def solution(mesh):
    in_specs = (
        P("section", "dp", None, None),
        P(None, "dp", None),
        P("dp", None, None),
        P("section", None, None),
        P("section", None, None),
        P("section", None, None),
        P("section", None, None),
        P("section", None, None),
        P("section", None, None),
        P("section", None, None),
    )
    out_specs = (
        P("section", "dp", None, None),
        P("section", "dp", None, None),
        P("section", None, None),
        P("section", None, None),
        P("section", None, None),
        P("section", None, None),
        P("section", None, None),
        P("section", None, None),
        P("section", None, None),
    )
    return jax.shard_map(
        per_device, mesh=mesh, in_specs=in_specs, out_specs=out_specs, check_vma=False
    )
```

```python
import functools

import jax
import jax.numpy as jnp
from jax import lax
from jax.experimental import pallas as pl
from jax.experimental.pallas import tpu as pltpu
from jax.sharding import PartitionSpec as P

HEADS = 8
PAIRS = HEADS // 2
EPSILON = 1e-05
MASKED = -1e30
BLOCK = 256
STRIP = 128
WIDTHS = (256,)
VMEM_LIMIT = 60 << 20
bf16, f32 = jnp.bfloat16, jnp.float32


def nn(left, right):
    return lax.dot_general(left, right, (((1,), (0,)), ((), ())), preferred_element_type=f32)


def nt(left, right):
    return lax.dot_general(left, right, (((1,), (1,)), ((), ())), preferred_element_type=f32)


def tn(left, right):
    return lax.dot_general(left, right, (((0,), (0,)), ((), ())), preferred_element_type=f32)


def blocks(total):
    return [slice(i, i + BLOCK) for i in range(0, total, BLOCK)]


def standardize(values):
    center = values - jnp.mean(values, axis=-1, keepdims=True)
    scale = lax.rsqrt(jnp.mean(center * center, axis=-1, keepdims=True) + EPSILON)
    return center * scale, scale


def norm_back(grad, unit, scale, gain):
    scaled = grad * gain
    first = jnp.mean(scaled, axis=-1, keepdims=True)
    second = jnp.mean(scaled * unit, axis=-1, keepdims=True)
    return (scaled - first - unit * second) * scale


def fold(values):
    return jnp.sum(values.reshape(-1, 8, values.shape[-1]), axis=0)


def half_masks(value):
    lanes = lax.broadcasted_iota(jnp.int32, (1, 128), 1)
    return [jnp.where((lanes < 64) == (a == 0), value, 0.0).astype(bf16) for a in range(2)]


def pair_lanes(pair, start=0):
    return pl.ds(pl.multiple_of(start + pair * 128, 128), 128)


class Mover:
    def __init__(self, sems):
        self.sems, self.used, self.open = sems, 0, []

    def make(self, source, target):
        copy = pltpu.make_async_copy(source, target, self.sems.at[self.used])
        self.used += 1
        return copy

    def load(self, source, target):
        copy = self.make(source, target)
        copy.start()
        return copy

    def store(self, source, target):
        copy = self.make(source, target)
        copy.start()
        self.open.append(copy)

    def finish(self):
        for copy in self.open:
            copy.wait()
        self.open = []


def window_of(lowest, highest, width, size):
    start = jnp.minimum(lax.div(lowest, 16) * 16, size - width)
    return start, highest - start <= width


def count(flags):
    return jnp.sum(jnp.where(flags, 1.0, 0.0)).astype(jnp.int32)


def turn(rows, start, width):
    size = rows.shape[1]
    if width == size:
        return rows
    return pltpu.roll(rows, size - start, 1)[:, :width]


def spans(own_id, other_row, causal, turned, span_ref):
    for block in range(other_row.shape[1] // STRIP):
        base = block * STRIP
        lowest = count(other_row < own_id(base).astype(f32))
        highest = count(other_row <= own_id(base + STRIP - 1).astype(f32))
        if causal is not None and turned:
            lowest = jnp.where(causal, jnp.maximum(lowest, base), lowest)
        elif causal is not None:
            highest = jnp.where(causal, jnp.minimum(highest, base + STRIP), highest)
        span_ref[0, block] = lowest
        span_ref[1, block] = highest


def attend(q_ref, q_start, k_ref, k_start, v_ref, v_start, span_ref, key_row, column_ref, causal, out_ref, mass_ref):
    size = q_ref.shape[0]
    masks = half_masks(64 ** -0.5)
    key_ids = jnp.broadcast_to(key_row, (8, size))

    def one_block(block, carry):
        base = pl.multiple_of(block * STRIP, STRIP)
        rows = pl.ds(base, STRIP)
        lowest, highest = span_ref[0, block], span_ref[1, block]

        def run(width, start):
            ids = turn(key_ids, start, width)[:1, :]
            allowed = column_ref[rows, :1] == ids
            if causal is not None:
                ahead = (lax.broadcasted_iota(jnp.int32, (STRIP, width), 1) + start
                         - lax.broadcasted_iota(jnp.int32, (STRIP, width), 0) - base)
                allowed = allowed & ((ahead <= 0) | jnp.logical_not(causal))
            bias = jnp.where(allowed, 0.0, MASKED)
            bias = jnp.concatenate([bias, bias], axis=0)
            keys_at = pl.ds(pl.multiple_of(start, 16), width) if width < size else slice(None)
            lanes = lax.broadcasted_iota(jnp.int32, (STRIP, 128), 1)
            mass = jnp.zeros((STRIP, 128), f32)
            for pair in range(PAIRS):
                query = q_ref[rows, q_start + pair * 128:q_start + pair * 128 + 128]
                keys = k_ref[keys_at, k_start + pair * 128:k_start + pair * 128 + 128]
                values = v_ref[keys_at, v_start + pair * 128:v_start + pair * 128 + 128]
                both = jnp.concatenate([query * masks[0], query * masks[1]], axis=0)
                scores = nt(both, keys) + bias
                top = jnp.max(scores, axis=-1, keepdims=True)
                weight = jnp.exp(scores - top)
                mixed = nn(weight.astype(bf16), jnp.concatenate([values, jnp.ones_like(values)], axis=1))
                total = mixed[:, 128:]
                mixed = mixed[:, :128] * (1.0 / total)
                level = top + jnp.log(total)
                mass = jnp.where(lanes == 2 * pair, level[:STRIP], jnp.where(lanes == 2 * pair + 1, level[STRIP:], mass))
                out_ref[rows, pair * 128:pair * 128 + 128] = jnp.where(
                    lanes < 64, mixed[:STRIP], mixed[STRIP:]).astype(bf16)
            mass_ref[rows, :] = mass

        by_width(lowest, highest, size, run)
        return carry

    lax.fori_loop(0, size // STRIP, one_block, 0)


def by_width(lowest, highest, size, run):
    open_ = None
    for width in WIDTHS:
        start, fits = window_of(lowest, highest, width, size)
        chosen = fits if open_ is None else fits & open_
        pl.when(chosen)(functools.partial(run, width, start))
        open_ = jnp.logical_not(fits) if open_ is None else open_ & jnp.logical_not(fits)
    pl.when(open_)(functools.partial(run, size, 0))


def head_sums(left_ref, right_ref, out_ref):
    features = left_ref.shape[1]
    depth = features // HEADS
    heads = lax.broadcasted_iota(jnp.int32, (HEADS, features), 0)
    members = lax.broadcasted_iota(jnp.int32, (HEADS, features), 1) // depth
    pick = jnp.where(heads == members, 1.0, 0.0).astype(bf16)
    for rows in blocks(left_ref.shape[0]):
        product = left_ref[rows, :].astype(f32) * right_ref[rows, :].astype(f32)
        high = product.astype(bf16)
        low = (product - high.astype(f32)).astype(bf16)
        out_ref[:, rows] = nt(pick, high) + nt(pick, low)


def attend_back(q_ref, q_start, k_ref, k_start, v_ref, v_start, grad_ref, span_ref, query_row, column_ref, causal,
                mass_ref, delta_ref, dq_ref, dq_start, dk_ref, dk_start, dv_ref, dv_start, sum_ref):
    size = q_ref.shape[0]
    scale = 64 ** -0.5
    scaled, plain = half_masks(scale), half_masks(1.0)
    query_ids = jnp.broadcast_to(query_row, (8, size))
    sum_ref[...] = jnp.zeros_like(sum_ref)

    def one_block(block, carry):
        base = pl.multiple_of(block * STRIP, STRIP)
        rows = pl.ds(base, STRIP)
        lowest, highest = span_ref[0, block], span_ref[1, block]

        def run(width, start):
            ids = turn(query_ids, start, width)[:1, :]
            mass, delta = turn(mass_ref[...], start, width), turn(delta_ref[...], start, width)
            allowed = column_ref[rows, :1] == ids
            if causal is not None:
                behind = (lax.broadcasted_iota(jnp.int32, (STRIP, width), 0) + base
                          - lax.broadcasted_iota(jnp.int32, (STRIP, width), 1) - start)
                allowed = allowed & ((behind <= 0) | jnp.logical_not(causal))
            bias = jnp.where(allowed, 0.0, MASKED)
            at = pl.ds(pl.multiple_of(start, 16), width) if width < size else slice(None)
            lanes = lax.broadcasted_iota(jnp.int32, (STRIP, 128), 1)
            for pair in range(PAIRS):
                keys = k_ref[rows, k_start + pair * 128:k_start + pair * 128 + 128]
                values = v_ref[rows, v_start + pair * 128:v_start + pair * 128 + 128]
                query = q_ref[at, q_start + pair * 128:q_start + pair * 128 + 128]
                grad = grad_ref[at, pair * 128:pair * 128 + 128]
                both_keys = jnp.concatenate([keys * scaled[0], keys * scaled[1]], axis=0)
                both_values = jnp.concatenate([values * plain[0], values * plain[1]], axis=0)
                scores = nt(both_keys, query)
                inner = nt(both_values, grad)
                weights, slopes = [], []
                for a in range(2):
                    part = slice(a * STRIP, a * STRIP + STRIP)
                    head = slice(2 * pair + a, 2 * pair + a + 1)
                    weight = jnp.exp(scores[part] + (bias - mass[head, :]))
                    slopes.append((weight * (inner[part] - delta[head, :])).astype(bf16))
                    weights.append(weight.astype(bf16))
                slope = jnp.concatenate(slopes, axis=0)
                dv = nn(jnp.concatenate(weights, axis=0), grad)
                dk = nn(slope, query) * scale
                dv_ref[rows, dv_start + pair * 128:dv_start + pair * 128 + 128] = jnp.where(
                    lanes < 64, dv[:STRIP], dv[STRIP:]).astype(bf16)
                dk_ref[rows, dk_start + pair * 128:dk_start + pair * 128 + 128] = jnp.where(
                    lanes < 64, dk[:STRIP], dk[STRIP:]).astype(bf16)
                sum_ref[at, pair * 128:pair * 128 + 128] += nn(both_keys.T, slope).T

        by_width(lowest, highest, size, run)
        return carry

    lax.fori_loop(0, size // STRIP, one_block, 0)
    dq_ref[:, dq_start:dq_start + sum_ref.shape[1]] = sum_ref[...].astype(bf16)


def as_column(row):
    return jnp.broadcast_to(row, (128, row.shape[1])).T


def role():
    return lax.axis_index("section") == 0


def front_kernel(row, x_hbm, ids_ref, id_ref, qkv_hbm, out_hbm, cross_hbm, up_hbm, down_hbm, gain_in, shift_in, *rest):
    if row:
        rest = rest[1:]
    front_body(row, x_hbm, ids_ref, id_ref, qkv_hbm, out_hbm, cross_hbm, up_hbm, down_hbm, gain_in, shift_in, *rest)


def front_body(row, x_hbm, ids_ref, id_ref, qkv_hbm, out_hbm, cross_hbm, up_hbm, down_hbm, gain_in, shift_in,
                 lowin_o, packed_o, mixed_o, mass_o, unit_o, scale_o, low_o, hidden_o, z_o, slope_o,
                 unit2_o, scale2_o, tail_o, layer_o,
                 gain_ref, shift_ref, span_s, x_v, wqkv, wout, wq, wup, wdown, base_v, column_v, lowin_v, packed_v, mixed_v, mass_v,
                 massrow_v, unit_v, scale_v, low_v, z_v, slope_v, unit2_v, scale2_v, tail_v, sems):
    is_encoder = role()
    features = x_v.shape[1]
    move = Mover(sems)
    load_x = move.load(x_hbm.at[0, row], x_v)
    load_qkv = move.load(qkv_hbm.at[0], wqkv)
    load_out = move.load(out_hbm.at[0], wout)
    load_up = move.make(up_hbm.at[0], wup)
    load_down = move.make(down_hbm.at[0], wdown)
    load_q = move.make(cross_hbm.at[0, :, pl.ds(0, features)], wq)

    @pl.when(is_encoder)
    def _():
        load_up.start()
        load_down.start()

    @pl.when(jnp.logical_not(is_encoder))
    def _():
        load_q.start()

    ids_row = jnp.where(is_encoder, ids_ref[pl.ds(0, 1), row, :], ids_ref[pl.ds(1, 1), row, :])
    ids_row = ids_row.astype(f32)
    column_v[...] = as_column(ids_row)
    gain_ref[...] = gain_in[0].astype(f32)
    shift_ref[...] = shift_in[0].astype(f32)
    side = jnp.where(is_encoder, 0, 1)
    spans(lambda at: id_ref[side, row, at], ids_row, jnp.logical_not(is_encoder), False, span_s)
    load_x.wait()

    @pl.when(is_encoder)
    def _():
        for rows in blocks(x_v.shape[0]):
            unit, _ = standardize(x_v[rows, :].astype(f32))
            value = unit * gain_ref[0:1, :] + shift_ref[0:1, :]
            base_v[rows, :] = value
            lowin_v[rows, :] = value.astype(bf16)

    @pl.when(jnp.logical_not(is_encoder))
    def _():
        base_v[...] = x_v[...].astype(f32)
        lowin_v[...] = x_v[...]

    move.store(lowin_v, lowin_o)
    load_qkv.wait()
    for rows in blocks(x_v.shape[0]):
        packed_v[rows, :] = nn(lowin_v[rows, :], wqkv[...]).astype(bf16)
    move.store(packed_v, packed_o)
    attend(packed_v, 0, packed_v, features, packed_v, 2 * features, span_s, ids_row,
           column_v, jnp.logical_not(is_encoder), mixed_v, mass_v)
    massrow_v[...] = mass_v[...].T[:HEADS, :]
    move.store(massrow_v, mass_o)
    move.store(mixed_v, mixed_o)
    load_out.wait()
    which = jnp.where(is_encoder, 1, 0)
    gain, shift = gain_ref[pl.ds(which, 1), :], shift_ref[pl.ds(which, 1), :]
    for rows in blocks(x_v.shape[0]):
        unit, scale = standardize(base_v[rows, :] + nn(mixed_v[rows, :], wout[...]))
        unit_v[rows, :] = unit.astype(bf16)
        scale_v[rows, :] = jnp.broadcast_to(scale, (BLOCK, 128))
        hidden = unit * gain + shift
        base_v[rows, :] = hidden
        low_v[rows, :] = hidden.astype(bf16)
    move.store(unit_v, unit_o)
    move.store(scale_v, scale_o)
    move.store(low_v, low_o)

    store_hidden = move.make(base_v, hidden_o)
    stores = [move.make(a, b) for a, b in ((z_v, z_o), (slope_v, slope_o), (unit2_v, unit2_o), (scale2_v, scale2_o),
                                           (tail_v, layer_o.at[0, row]))]

    @pl.when(jnp.logical_not(is_encoder))
    def _():
        store_hidden.start()
        load_q.wait()
        for rows in blocks(x_v.shape[0]):
            tail_v[rows, :] = nn(low_v[rows, :], wq[...]).astype(bf16)
        store_hidden.wait()

    @pl.when(is_encoder)
    def _():
        load_up.wait()
        load_down.wait()
        for rows in blocks(x_v.shape[0]):
            feed_forward(low_v, rows, wup, z_v, slope_v)
            unit, scale = standardize(base_v[rows, :] + nn(z_v[rows, :], wdown[...]))
            unit2_v[rows, :] = unit.astype(bf16)
            scale2_v[rows, :] = jnp.broadcast_to(scale, (BLOCK, 128))
            tail_v[rows, :] = (unit * gain_ref[2:3, :] + shift_ref[2:3, :]).astype(bf16)
        for copy in stores:
            copy.start()
        for copy in stores:
            copy.wait()

    move.store(tail_v, tail_o)
    move.finish()


def feed_forward(low_ref, rows, wup, z_ref, slope_ref):
    for start in range(0, wup.shape[1], 512):
        columns = slice(start, start + 512)
        up = nn(low_ref[rows, :], wup[:, columns])
        gate = 1.0 / (1.0 + jnp.exp(-up))
        z = up * gate
        z_ref[rows, columns] = z.astype(bf16)
        slope_ref[rows, columns] = (gate + z * (1.0 - gate)).astype(bf16)


def feed_back(grad_ref, rows, wup, wdown, slope_ref, du_ref):
    for start in range(0, wup.shape[1], 512):
        columns = slice(start, start + 512)
        dz = nt(grad_ref[rows, :], wdown[columns, :])
        du_ref[rows, columns] = (dz * slope_ref[rows, columns].astype(f32)).astype(bf16)
    return nt(du_ref[rows, :], wup[...])


def cross_kernel(row, memory_hbm, query_hbm, hidden_hbm, cot_hbm, ids_ref, id_ref, kv_hbm, cross_hbm, up_hbm, down_hbm,
                 gain_in, shift_in, before,
                 layer_o, low_o, z_o, du_o, df_o, mixed_o, dbranch_o, dr_o, dq_o, dkv_o, dmem_o, sums_o,
                 gain_ref, shift_ref, span_s, turned_s, memory_v, query_v, hidden_v, cot_v, wkv, wout, wup, wdown, kv_v, column_v, mixed_v, mass_v, massrow_v,
                 delta_v, low_v, z_v, slope_v, unit_v, scale_v, du_v, df_v, dbranch_v, dmixed_v, dq_v, dkv_v, dmem_v,
                 out_v, sum_v, sums_v, sems):
    is_encoder = role()
    features = memory_v.shape[1]
    size = memory_v.shape[0]

    @pl.when(jnp.logical_not(is_encoder))
    def _():
        move = Mover(sems)
        load_kv = move.load(kv_hbm, wkv)
        load_memory = move.load(memory_hbm, memory_v)
        load_query = move.load(query_hbm, query_v)
        load_hidden = move.load(hidden_hbm, hidden_v)
        load_out = move.load(cross_hbm.at[0, :, pl.ds(features, features)], wout)
        load_up = move.load(up_hbm.at[0], wup)
        load_down = move.load(down_hbm.at[0], wdown)
        load_cot = move.load(cot_hbm.at[row], cot_v)
        source, target = ids_ref[0, row:row + 1, :], ids_ref[1, row:row + 1, :]
        source, target = source.astype(f32), target.astype(f32)
        column_v[...] = as_column(target)
        gain_ref[...] = gain_in[0].astype(f32)
        shift_ref[...] = shift_in[0].astype(f32)
        spans(lambda at: id_ref[1, row, at], source, None, False, span_s)
        spans(lambda at: id_ref[0, row, at], target, None, True, turned_s)
        sums_v[...] = jnp.zeros_like(sums_v)
        load_kv.wait()
        load_memory.wait()
        for rows in blocks(size):
            kv_v[rows, :] = nn(memory_v[rows, :], wkv[...]).astype(bf16)
        load_query.wait()
        attend(query_v, 0, kv_v, 0, kv_v, features, span_s, source, column_v, None, mixed_v, mass_v)
        massrow_v[...] = mass_v[...].T[:HEADS, :]
        move.store(mixed_v, mixed_o)
        load_hidden.wait()
        load_out.wait()
        for rows in blocks(size):
            unit, scale = standardize(hidden_v[rows, :] + nn(mixed_v[rows, :], wout[...]))
            unit_v[rows, :] = unit.astype(bf16)
            scale_v[rows, :] = jnp.broadcast_to(scale, (BLOCK, 128))
            hidden = unit * gain_ref[1:2, :] + shift_ref[1:2, :]
            hidden_v[rows, :] = hidden
            low_v[rows, :] = hidden.astype(bf16)
        move.store(low_v, low_o)
        load_up.wait()
        load_down.wait()
        load_cot.wait()
        for rows in blocks(size):
            feed_forward(low_v, rows, wup, z_v, slope_v)
            unit, scale = standardize(hidden_v[rows, :] + nn(z_v[rows, :], wdown[...]))
            out_v[rows, :] = (unit * gain_ref[2:3, :] + shift_ref[2:3, :]).astype(bf16)
            grad = cot_v[rows, :].astype(f32)
            sums_v[2] += fold(grad * unit)
            sums_v[5] += fold(grad)
            dr = norm_back(grad, unit, scale, gain_ref[2:3, :])
            hidden_v[rows, :] = dr
            df_v[rows, :] = dr.astype(bf16)
        move.store(z_v, z_o)
        move.store(df_v, df_o)
        move.store(out_v, layer_o.at[0, row])
        for rows in blocks(size):
            grad = hidden_v[rows, :] + feed_back(df_v, rows, wup, wdown, slope_v, du_v)
            unit = unit_v[rows, :].astype(f32)
            sums_v[1] += fold(grad * unit)
            sums_v[4] += fold(grad)
            dr = norm_back(grad, unit, scale_v[rows, :1], gain_ref[1:2, :])
            hidden_v[rows, :] = dr
            dbranch_v[rows, :] = dr.astype(bf16)
            dmixed_v[rows, :] = nt(dbranch_v[rows, :], wout[...]).astype(bf16)
        move.store(du_v, du_o)
        move.store(dbranch_v, dbranch_o)
        move.store(hidden_v, dr_o)
        move.store(sums_v, sums_o)
        column_v[...] = as_column(source)
        head_sums(dmixed_v, mixed_v, delta_v)
        attend_back(query_v, 0, kv_v, 0, kv_v, features, dmixed_v, turned_s, target, column_v, None,
                    massrow_v, delta_v, dq_v, 0, dkv_v, 0, dkv_v, features, sum_v)
        move.store(dq_v, dq_o)
        move.store(dkv_v, dkv_o)
        for rows in blocks(size):
            dmem_v[rows, :] = nt(dkv_v[rows, :], wkv[...]).astype(bf16)
        move.store(dmem_v, dmem_o)
        move.finish()


def back_kernel(enc_row, dec_row, dmem_hbm, unit2_hbm, scale2_hbm, slope_hbm, dr_hbm, dq_hbm,
                eunit_hbm, escale_hbm, epacked_hbm, emixed_hbm, emass_hbm,
                dunit_hbm, dscale_hbm, dpacked_hbm, dmixed_hbm, dmass_hbm,
                x_hbm, ids_ref, id_ref, qkv_hbm, out_hbm, cross_hbm, up_hbm, down_hbm, gain_in, *rest):
    if enc_row != 0:
        rest = rest[1:]
    back_body(enc_row, dec_row, dmem_hbm, unit2_hbm, scale2_hbm, slope_hbm, dr_hbm, dq_hbm,
              eunit_hbm, escale_hbm, epacked_hbm, emixed_hbm, emass_hbm,
              dunit_hbm, dscale_hbm, dpacked_hbm, dmixed_hbm, dmass_hbm,
              x_hbm, ids_ref, id_ref, qkv_hbm, out_hbm, cross_hbm, up_hbm, down_hbm, gain_in, *rest)


def back_body(enc_row, dec_row, dmem_hbm, unit2_hbm, scale2_hbm, slope_hbm, dr_hbm, dq_hbm,
                eunit_hbm, escale_hbm, epacked_hbm, emixed_hbm, emass_hbm,
                dunit_hbm, dscale_hbm, dpacked_hbm, dmixed_hbm, dmass_hbm,
                x_hbm, ids_ref, id_ref, qkv_hbm, out_hbm, cross_hbm, up_hbm, down_hbm, gain_in,
                du_o, df_o, dbranch_o, dpacked_o, dx_o, sums_o,
                gain_ref, span_s,
                dmem_v, unit2_v, scale2_v, slope_v, dr_v, dq_v, unit_v, scale_v, packed_v, mixed_v, mass_v, x_v,
                wqkv, wout, wq, wup, wdown, column_v, delta_v, du_v, df_v, dbranch_v, dout_v, dpacked_v, sum_v,
                sums_v, sems):
    is_encoder = role()
    features = mixed_v.shape[1]
    size = mixed_v.shape[0]

    def run():
        move = Mover(sems)
        is_decoder = jnp.logical_not(is_encoder)
        load_dmem = move.make(dmem_hbm, dmem_v)
        load_unit2 = move.make(unit2_hbm, unit2_v)
        load_scale2 = move.make(scale2_hbm, scale2_v)
        load_slope = move.make(slope_hbm, slope_v)
        load_down = move.make(down_hbm.at[0], wdown)
        load_up = move.make(up_hbm.at[0], wup)
        load_dr = move.make(dr_hbm, dr_v)
        load_dq = move.make(dq_hbm, dq_v)
        load_q = move.make(cross_hbm.at[0, :, pl.ds(0, features)], wq)
        firsts = [load_dmem, load_unit2, load_scale2, load_down, load_slope, load_up]

        sums_v[...] = jnp.zeros_like(sums_v)
        enc_selfs = [(eunit_hbm, unit_v), (escale_hbm, scale_v), (emixed_hbm, mixed_v), (epacked_hbm, packed_v), (emass_hbm, mass_v)]
        dec_selfs = [(dunit_hbm, unit_v), (dscale_hbm, scale_v), (dmixed_hbm, mixed_v), (dpacked_hbm, packed_v), (dmass_hbm, mass_v)]
        enc_pairs, dec_pairs = [], []
        for (es, ev), (ds, dv) in zip(enc_selfs, dec_selfs):
            enc_pairs.append(move.make(es, ev))
            dec_pairs.append(pltpu.make_async_copy(ds, dv, sems.at[move.used - 1]))
        load_x = move.make(x_hbm.at[0, enc_row or 0], x_v)
        load_out = move.make(out_hbm.at[0], wout)
        load_qkv = move.make(qkv_hbm.at[0], wqkv)
        dx_sem = sems.at[move.used]
        move.used += 1

        @pl.when(is_encoder)
        def _():
            for copy in firsts:
                copy.start()
            for copy in enc_pairs:
                copy.start()
            load_x.start()

        @pl.when(is_decoder)
        def _():
            load_dq.start()
            load_q.start()
            load_dr.start()
            for copy in dec_pairs:
                copy.start()

        load_out.start()
        load_qkv.start()
        enc_ids, dec_ids = ids_ref[0:1, enc_row or 0, :], ids_ref[1:2, dec_row or 0, :]
        ids_row = jnp.where(is_encoder, enc_ids, dec_ids)
        ids_row = ids_row.astype(f32)
        column_v[...] = as_column(ids_row)

        def key_id(at):
            return jnp.where(is_encoder, id_ref[0, enc_row or 0, at], id_ref[1, dec_row or 0, at])

        gain_ref[...] = gain_in[0].astype(f32)
        spans(key_id, ids_row, is_decoder, True, span_s)

        stores = [move.make(du_v, du_o), move.make(df_v, df_o)]

        @pl.when(is_encoder)
        def _():
            for copy in firsts[:3]:
                copy.wait()
            for rows in blocks(size):
                grad = dmem_v[rows, :].astype(f32)
                unit = unit2_v[rows, :].astype(f32)
                sums_v[2] += fold(grad * unit)
                sums_v[5] += fold(grad)
                dr = norm_back(grad, unit, scale2_v[rows, :1], gain_ref[2:3, :])
                dr_v[rows, :] = dr
                df_v[rows, :] = dr.astype(bf16)
            stores[1].start()
            for copy in firsts[3:]:
                copy.wait()
            for rows in blocks(size):
                dr_v[rows, :] += feed_back(df_v, rows, wup, wdown, slope_v, du_v)
            stores[0].start()

        @pl.when(is_decoder)
        def _():
            load_dq.wait()
            load_q.wait()
            load_dr.wait()
            for rows in blocks(size):
                dr_v[rows, :] += nt(dq_v[rows, :], wq[...])

        for copy in enc_pairs:
            copy.wait()
        load_out.wait()
        which = jnp.where(is_encoder, 1, 0)
        gain = gain_ref[pl.ds(which, 1), :]
        for rows in blocks(size):
            grad = dr_v[rows, :]
            unit = unit_v[rows, :].astype(f32)
            sums_v[pl.ds(which, 1)] += fold(grad * unit)[None]
            sums_v[pl.ds(which + 3, 1)] += fold(grad)[None]
            dr = norm_back(grad, unit, scale_v[rows, :1], gain)
            dr_v[rows, :] = dr
            dbranch_v[rows, :] = dr.astype(bf16)
            dout_v[rows, :] = nt(dbranch_v[rows, :], wout[...]).astype(bf16)
        move.store(dbranch_v, dbranch_o)
        head_sums(dout_v, mixed_v, delta_v)
        attend_back(packed_v, 0, packed_v, features, packed_v, 2 * features, dout_v, span_s, ids_row, column_v, is_decoder,
                    mass_v, delta_v, dpacked_v, 0, dpacked_v, features, dpacked_v, 2 * features, sum_v)
        move.store(dpacked_v, dpacked_o)
        load_qkv.wait()
        for rows in blocks(size):
            dr_v[rows, :] += nt(dpacked_v[rows, :], wqkv[...])

        @pl.when(is_encoder)
        def _():
            load_x.wait()
            for rows in blocks(size):
                unit, scale = standardize(x_v[rows, :].astype(f32))
                grad = dr_v[rows, :]
                sums_v[0] += fold(grad * unit)
                sums_v[3] += fold(grad)
                dr_v[rows, :] = norm_back(grad, unit, scale, gain_ref[0:1, :])
            for copy in stores:
                copy.wait()

        pl.when(is_encoder)(lambda: pltpu.make_async_copy(dr_v, dx_o.at[0, enc_row or 0], dx_sem).start())
        pl.when(is_decoder)(lambda: pltpu.make_async_copy(dr_v, dx_o.at[0, dec_row or 0], dx_sem).start())
        pltpu.make_async_copy(dr_v, dx_o.at[0, 0], dx_sem).wait()
        move.store(sums_v, sums_o)
        move.finish()

    if enc_row is not None and dec_row is not None:
        run()
    elif enc_row is not None:
        pl.when(is_encoder)(run)
    else:
        pl.when(jnp.logical_not(is_encoder))(run)


def memory_weight_kernel(*refs):
    memories, grads, out_o = refs[0:3], refs[3:6], refs[6]
    left_v, right_v, out_v, sems = refs[7:]
    size = left_v.shape[0] // 3

    @pl.when(jnp.logical_not(role()))
    def _():
        move = Mover(sems)
        loads = []
        for i in range(3):
            loads.append(move.load(memories[i], left_v.at[pl.ds(i * size, size)]))
            loads.append(move.load(grads[i], right_v.at[pl.ds(i * size, size)]))
        for copy in loads:
            copy.wait()
        for start in range(0, right_v.shape[1], 512):
            out_v[:, start:start + 512] = tn(left_v[...], right_v[:, start:start + 512]).astype(bf16)
        move.store(out_v, out_o)
        move.finish()


def weight_kernel(count, *refs):
    names = ("lowin", "dpacked_e", "dpacked_d", "mixed", "dbranch_e", "dbranch_d", "low", "dq", "cmixed", "cdbranch",
             "du_e", "du_d", "clow", "z_e", "z_d", "df_e", "df_d")
    hbm = {name: refs[i * count:(i + 1) * count] for i, name in enumerate(names)}
    at = len(names) * count
    cross_hbm, esums, csums, bsums, = refs[at], refs[at + 1:at + 1 + count], refs[at + 1 + count:at + 1 + 2 * count], refs[at + 1 + 2 * count:at + 1 + 3 * count]
    out_o = refs[at + 1 + 3 * count]
    in_v, dpacked_v, mixed_v, dbranch_v, low_v, dq_v, cmixed_v, cdbranch_v, du_v, flow_v, z_v, df_v, cross_v, norm_v, out_v, sems = refs[at + 2 + 3 * count:]
    is_encoder = role()
    is_decoder = jnp.logical_not(is_encoder)
    size = in_v.shape[0] // count
    features = in_v.shape[1]
    move = Mover(sems)

    def gather(target, enc=None, dec=None):
        pieces = []
        for i in range(count):
            spot = target.at[pl.ds(i * size, size)]
            at = move.used
            move.used += 1
            pieces.append((enc and pltpu.make_async_copy(hbm[enc][i], spot, sems.at[at]),
                           dec and pltpu.make_async_copy(hbm[dec][i], spot, sems.at[at])))

        def start(side):
            for piece in pieces:
                piece[side].start()

        if enc:
            pl.when(is_encoder)(lambda: start(0))
        if dec:
            pl.when(is_decoder)(lambda: start(1))

        def wait():
            for piece in pieces:
                (piece[0] or piece[1]).wait()
        return wait

    wait_z = gather(z_v, "z_e", "z_d")
    wait_df = gather(df_v, "df_e", "df_d")
    wait_flow = gather(flow_v, "low", "clow")
    wait_du = gather(du_v, "du_e", "du_d")
    wait_in = gather(in_v, "lowin", "lowin")
    wait_dpacked = gather(dpacked_v, "dpacked_e", "dpacked_d")
    wait_mixed = gather(mixed_v, "mixed", "mixed")
    wait_dbranch = gather(dbranch_v, "dbranch_e", "dbranch_d")
    wait_low = gather(low_v, None, "low")
    wait_dq = gather(dq_v, None, "dq")
    wait_cmixed = gather(cmixed_v, None, "cmixed")
    wait_cdbranch = gather(cdbranch_v, None, "cdbranch")
    load_cross = move.make(cross_hbm, cross_v)
    pl.when(is_encoder)(load_cross.start)

    base = 6 * features
    qkv_width = dpacked_v.shape[1]

    def place(start, value):
        out_v[:, start:start + value.shape[1]] = value.astype(bf16)
    wait_z()
    wait_df()
    for j in range(0, z_v.shape[1], features):
        place(base + du_v.shape[1] + j, tn(z_v[:, j:j + features], df_v[...]))
    wait_flow()
    wait_du()
    for j in range(0, du_v.shape[1], features):
        place(base + j, tn(flow_v[...], du_v[:, j:j + features]))
    wait_in()
    wait_dpacked()
    for j in range(0, qkv_width, features):
        place(j, tn(in_v[...], dpacked_v[:, j:j + features]))
    wait_mixed()
    wait_dbranch()
    place(qkv_width, tn(mixed_v[...], dbranch_v[...]))

    @pl.when(is_encoder)
    def _():
        load_cross.wait()
        out_v[:, 4 * features:6 * features] = cross_v[...]
        total = sum(esum[...] for esum in esums)
        norm_v[0:6, :] = jnp.sum(total, axis=1)

    @pl.when(is_decoder)
    def _():
        wait_low()
        wait_dq()
        place(4 * features, tn(low_v[...], dq_v[...]))
        wait_cmixed()
        wait_cdbranch()
        place(5 * features, tn(cmixed_v[...], cdbranch_v[...]))
        total = sum(csum[...] + bsum[...] for csum, bsum in zip(csums, bsums))
        norm_v[0:6, :] = jnp.sum(total, axis=1)

    norm_v[6:, :] = jnp.zeros((norm_v.shape[0] - 6, features), f32)
    out_v[:, base + 2 * du_v.shape[1]:] = norm_v[...].T.astype(bf16)
    move.store(out_v, out_o)
    move.finish()


ANY = pl.BlockSpec(memory_space=pl.ANY)
IN_VMEM = pl.BlockSpec(memory_space=pltpu.VMEM)
IN_SMEM = pl.BlockSpec(memory_space=pltpu.SMEM)


def shape(*dims, dtype=bf16):
    return jax.ShapeDtypeStruct(dims, dtype)


def scratch_of(member):
    return member if not isinstance(member, jax.ShapeDtypeStruct) else pltpu.VMEM(member.shape, member.dtype)


def call(name, body, in_specs, outs, scratch, sems, args, flops=0, aliases=()):
    return pl.pallas_call(
        body,
        name=name,
        input_output_aliases=dict(aliases),
        out_shape=outs,
        in_specs=in_specs,
        out_specs=[ANY] * len(outs),
        scratch_shapes=[scratch_of(s) for s in scratch] + [pltpu.SemaphoreType.DMA((sems,))],
        compiler_params=pltpu.CompilerParams(vmem_limit_bytes=VMEM_LIMIT, has_side_effects=True),
        cost_estimate=pl.CostEstimate(flops=flops, bytes_accessed=10 << 20, transcendentals=0),
    )(*args)


def front(row, embed, ids, weights, before):
    qkv, out, cross, up, down, gain, shift = weights
    size, d = embed.shape[2:]
    hidden = up.shape[2]
    outs = [shape(size, d), shape(size, 3 * d), shape(size, d), shape(HEADS, size, dtype=f32), shape(size, d),
            shape(size, 128, dtype=f32), shape(size, d), shape(size, d, dtype=f32), shape(size, hidden),
            shape(size, hidden), shape(size, d), shape(size, 128, dtype=f32), shape(size, d), shape(*embed.shape)]
    scratch = [shape(3, d, dtype=f32), shape(3, d, dtype=f32), pltpu.SMEM((2, size // STRIP), jnp.int32),
               shape(size, d), shape(d, 3 * d), shape(d, d), shape(d, d), shape(d, hidden), shape(hidden, d),
               shape(size, d, dtype=f32), shape(size, 128, dtype=f32), shape(size, d), shape(size, 3 * d),
               shape(size, d), shape(size, 128, dtype=f32), shape(HEADS, size, dtype=f32), shape(size, d),
               shape(size, 128, dtype=f32), shape(size, d), shape(size, hidden), shape(size, hidden),
               shape(size, d), shape(size, 128, dtype=f32), shape(size, d)]
    more = [before] if row else []
    return call(f"front{row}", functools.partial(front_kernel, row),
                [ANY, IN_VMEM, IN_SMEM] + [ANY] * 5 + [IN_VMEM] * 2 + [ANY] * len(more), outs, scratch, 24,
                (embed, ids, ids, qkv, out, cross, up, down, gain, shift, *more), flops=8 * 10**9,
                aliases=[(10, len(outs) - 1)] if row else [])


def cross(row, memory, query, hidden_f, cot, ids, kv_weight, weights, before):
    qkv, out, cross_w, up, down, gain, shift = weights
    size, d = memory.shape
    hidden = up.shape[2]
    outs = [shape(*before.shape), shape(size, d), shape(size, hidden), shape(size, hidden), shape(size, d), shape(size, d),
            shape(size, d), shape(size, d, dtype=f32), shape(size, d), shape(size, 2 * d), shape(size, d),
            shape(6, 8, d, dtype=f32)]
    scratch = [shape(3, d, dtype=f32), shape(3, d, dtype=f32), pltpu.SMEM((2, size // STRIP), jnp.int32),
               pltpu.SMEM((2, size // STRIP), jnp.int32),
               shape(size, d), shape(size, d), shape(size, d, dtype=f32), shape(size, d), shape(d, 2 * d),
               shape(d, d), shape(d, hidden), shape(hidden, d), shape(size, 2 * d), shape(size, 128, dtype=f32),
               shape(size, d), shape(size, 128, dtype=f32), shape(HEADS, size, dtype=f32), shape(HEADS, size, dtype=f32),
               shape(size, d), shape(size, hidden), shape(size, hidden), shape(size, d), shape(size, 128, dtype=f32),
               shape(size, hidden), shape(size, d), shape(size, d), shape(size, d), shape(size, d), shape(size, 2 * d),
               shape(size, d), shape(size, d), shape(size, d, dtype=f32), shape(6, 8, d, dtype=f32)]
    return call(f"cross{row}", functools.partial(cross_kernel, row),
                [ANY] * 4 + [IN_VMEM, IN_SMEM] + [ANY] * 4 + [IN_VMEM] * 2 + [ANY], outs, scratch,
                24, (memory, query, hidden_f, cot, ids, ids, kv_weight, cross_w, up, down, gain, shift, before),
                flops=20 * 10**9, aliases=[(12, 0)])


def back(enc_row, dec_row, dmem, e_front, d_front, d_cross, embed, ids, weights, before):
    qkv, out, cross_w, up, down, gain, shift = weights
    size, d = embed.shape[2:]
    hidden = up.shape[2]
    outs = [shape(size, hidden), shape(size, d), shape(size, d), shape(size, 3 * d), shape(*embed.shape, dtype=f32),
            shape(6, 8, d, dtype=f32)]
    scratch = [shape(3, d, dtype=f32), pltpu.SMEM((2, size // STRIP), jnp.int32),
               shape(size, d), shape(size, d), shape(size, 128, dtype=f32), shape(size, hidden),
               shape(size, d, dtype=f32), shape(size, d), shape(size, d), shape(size, 128, dtype=f32),
               shape(size, 3 * d), shape(size, d), shape(HEADS, size, dtype=f32), shape(size, d),
               shape(d, 3 * d), shape(d, d), shape(d, d), shape(d, hidden), shape(hidden, d),
               shape(size, 128, dtype=f32), shape(HEADS, size, dtype=f32), shape(size, hidden), shape(size, d),
               shape(size, d), shape(size, d), shape(size, 3 * d), shape(size, d, dtype=f32),
               shape(6, 8, d, dtype=f32)]
    args = (dmem, e_front["unit2"], e_front["scale2"], e_front["slope"], d_cross["dr"], d_cross["dq"],
            e_front["unit"], e_front["scale"], e_front["packed"], e_front["mixed"], e_front["mass"],
            d_front["unit"], d_front["scale"], d_front["packed"], d_front["mixed"], d_front["mass"],
            embed, ids, ids, qkv, out, cross_w, up, down, gain)
    names = ("du", "df", "dbranch", "dpacked", "dx", "sums")
    more = [] if before is None else [before]
    results = call(f"back_e{enc_row}_d{dec_row}", functools.partial(back_kernel, enc_row, dec_row),
                   [ANY] * 17 + [IN_VMEM, IN_SMEM] + [ANY] * 5 + [IN_VMEM] + [ANY] * len(more),
                   outs, scratch, 28, (*args, *more), flops=12 * 10**9, aliases=[(len(args), 4)] if more else [])
    return dict(zip(names, results))


def spread_kernel(packed_ref, qkv_ref, out_ref, cross_ref, up_ref, down_ref, gain_ref, shift_ref):
    start = 0
    for ref in (qkv_ref, out_ref, cross_ref, up_ref):
        ref[0] = packed_ref[:, start:start + ref.shape[2]].astype(f32)
        start += ref.shape[2]
    for i in range(down_ref.shape[0]):
        down_ref[i] = packed_ref[:, start:start + down_ref.shape[2]].astype(f32)
        start += down_ref.shape[2]
    norms = packed_ref[:, start:].astype(f32).T
    gain_ref[0] = norms[0:3]
    shift_ref[0] = norms[3:6]


def spread(packed, d, hidden):
    slab = 128
    widths = [3 * d, d, 2 * d, hidden]
    wide = [jax.ShapeDtypeStruct((1, d, w), f32) for w in widths]
    return pl.pallas_call(
        spread_kernel,
        name="spread",
        grid=(d // slab,),
        in_specs=[pl.BlockSpec((slab, packed.shape[1]), lambda i: (i, 0))],
        out_shape=wide + [shape(hidden // d, d, d, dtype=f32), shape(1, 3, d, dtype=f32), shape(1, 3, d, dtype=f32)],
        out_specs=[pl.BlockSpec((1, slab, w), lambda i: (0, i, 0)) for w in widths]
        + [pl.BlockSpec((hidden // d, slab, d), lambda i: (0, i, 0))]
        + [pl.BlockSpec((1, 3, slab), lambda i: (0, 0, i))] * 2,
        compiler_params=pltpu.CompilerParams(vmem_limit_bytes=VMEM_LIMIT),
    )(packed)


def per_device(embeddings, segments, cotangent, attn_qkv, attn_out, cross_proj, ffn_up, ffn_down, norm_gain, norm_bias):
    weights = (attn_qkv, attn_out, cross_proj, ffn_up, ffn_down, norm_gain, norm_bias)
    row_total, size, d = embeddings.shape[1:]
    hidden = ffn_up.shape[2]
    devices = lax.axis_size("dp")
    kv_weight = lax.ppermute(cross_proj[0], "section", [(0, 1)])

    front_names = ("lowin", "packed", "mixed", "mass", "unit", "scale", "low", "hidden", "z", "slope", "unit2", "scale2", "tail",
                   "layer")
    cross_names = ("layer", "low", "z", "du", "df", "mixed", "dbranch", "dr", "dq", "dkv", "dmem", "sums")
    rows = range(row_total)
    fronts, memories, layer_out = [], [], None
    for row in rows:
        fronts.append(dict(zip(front_names, front(row, embeddings, segments, weights, layer_out))))
        layer_out = fronts[row]["layer"]
        memories.append(lax.ppermute(fronts[row]["tail"], "section", [(0, 1)]))
    crosses, grads = [], []
    for row in rows:
        crosses.append(dict(zip(cross_names, cross(
            row, memories[row], fronts[row]["tail"], fronts[row]["hidden"], cotangent, segments, kv_weight, weights,
            layer_out))))
        layer_out = crosses[row]["layer"]
        grads.append(lax.ppermute(crosses[row]["dmem"], "section", [(1, 0)]))
    memory_weight = pl.pallas_call(
        memory_weight_kernel,
        name="memory_weight",
        out_shape=shape(d, 2 * d),
        in_specs=[ANY] * 6,
        out_specs=ANY,
        scratch_shapes=[pltpu.VMEM((row_total * size, d), bf16), pltpu.VMEM((row_total * size, 2 * d), bf16),
                        pltpu.VMEM((d, 2 * d), bf16), pltpu.SemaphoreType.DMA((8,))],
        compiler_params=pltpu.CompilerParams(vmem_limit_bytes=VMEM_LIMIT, has_side_effects=True),
        cost_estimate=pl.CostEstimate(flops=4 * 10**9, bytes_accessed=4 << 20, transcendentals=0),
    )(*memories, *[c["dkv"] for c in crosses])
    memory_weight = lax.ppermute(memory_weight, "section", [(1, 0)])

    backs_e, backs_d, input_grad = [None] * row_total, [None] * row_total, None
    for step in range(row_total + 1):
        enc_row = step if step < row_total else None
        dec_row = step - 1 if step > 0 else None
        e, s = enc_row or 0, dec_row or 0
        if enc_row is None:
            e = row_total - 1
        result = back(enc_row, dec_row, grads[e], fronts[e], fronts[s], crosses[s], embeddings, segments, weights,
                      input_grad)
        input_grad = result["dx"]
        if enc_row is not None:
            backs_e[enc_row] = result
        if dec_row is not None:
            backs_d[dec_row] = result

    lists = [
        [f["lowin"] for f in fronts], [b["dpacked"] for b in backs_e], [b["dpacked"] for b in backs_d],
        [f["mixed"] for f in fronts], [b["dbranch"] for b in backs_e], [b["dbranch"] for b in backs_d],
        [f["low"] for f in fronts], [c["dq"] for c in crosses], [c["mixed"] for c in crosses],
        [c["dbranch"] for c in crosses], [b["du"] for b in backs_e], [c["du"] for c in crosses],
        [c["low"] for c in crosses], [f["z"] for f in fronts], [c["z"] for c in crosses],
        [b["df"] for b in backs_e], [c["df"] for c in crosses],
    ]
    flat = [member for group in lists for member in group]
    sums = [b["sums"] for b in backs_e] + [c["sums"] for c in crosses] + [b["sums"] for b in backs_d]
    tokens = row_total * size
    width = 6 * d + 2 * hidden + 128
    scratch = [(tokens, d), (tokens, 3 * d), (tokens, d), (tokens, d), (tokens, d), (tokens, d), (tokens, d), (tokens, d),
               (tokens, hidden), (tokens, d), (tokens, hidden), (tokens, d), (d, 2 * d)]
    packed = pl.pallas_call(
        functools.partial(weight_kernel, row_total),
        name="weight",
        out_shape=shape(d, width),
        in_specs=[ANY] * (len(flat) + 1) + [IN_VMEM] * len(sums),
        out_specs=ANY,
        scratch_shapes=[pltpu.VMEM(s, bf16) for s in scratch]
        + [pltpu.VMEM((128, d), f32), pltpu.VMEM((d, width), bf16), pltpu.SemaphoreType.DMA((12 * row_total + 2,))],
        compiler_params=pltpu.CompilerParams(vmem_limit_bytes=VMEM_LIMIT, has_side_effects=True),
        cost_estimate=pl.CostEstimate(flops=23 * 10**9, bytes_accessed=30 << 20, transcendentals=0),
    )(*flat, memory_weight, *sums)

    if d == 32 * devices:
        packed = sum_over(packed, devices)
    else:
        packed = lax.psum(packed, "dp")
    qkv, out, crosses, up, down, gain, shift = spread(packed, d, hidden)
    return (layer_out, input_grad, qkv, out, crosses, up, down.reshape(1, hidden, d), gain, shift)


PARTS = 3

def ring_place(index, chips):
    chip = lax.div(index, 2)
    level, side = lax.div(chip, 2), lax.rem(chip, 2)
    return jnp.where(side == 0, level, chips - 1 - level)

def ring_device(place, chips, core):
    half = chips // 2
    chip = jnp.where(place < half, 2 * place, 2 * (chips - 1 - place) + 1)
    return 2 * chip + core

def sum_kernel(chips, local, total, paired, landed, pair_sems, ring_sems, gather_sems, share_sems):
    width = local.shape[1]
    part = width // PARTS
    me = lax.axis_index("dp")
    core = lax.rem(me, 2)
    place = ring_place(me, chips)
    sibling = me + 1 - 2 * core
    ahead = ring_device(lax.rem(place + 1, chips), chips, core)
    behind = ring_device(lax.rem(place + chips - 1, chips), chips, core)
    targets = (ahead, behind)

    barrier = pltpu.get_barrier_semaphore()
    for other in (sibling, ahead, behind):
        pl.semaphore_signal(barrier, inc=1, device_id={"dp": other}, device_id_type=pl.DeviceIdType.MESH)
    pl.semaphore_wait(barrier, 3)

    def slot(way, step):
        return lax.rem(place + (chips - step if way == 0 else step), chips)

    def rows(way, step, owner):
        return pl.ds(pl.multiple_of(64 * slot(way, step) + 32 * owner + 16 * way, 16), 16)

    def pair_copy(way, step):
        return pltpu.make_async_remote_copy(
            src_ref=local.at[rows(way, step, 1 - core)],
            dst_ref=paired.at[way, step],
            send_sem=pair_sems.at[0, way, step],
            recv_sem=pair_sems.at[1, way, step],
            device_id={"dp": sibling}, device_id_type=pl.DeviceIdType.MESH)

    def columns(p):
        return pl.ds(p * part, part)

    def ring_copy(way, step, p):
        return pltpu.make_async_remote_copy(
            src_ref=paired.at[way, step, :, columns(p)],
            dst_ref=landed.at[way, step, :, columns(p)],
            send_sem=ring_sems.at[0, way, step, p],
            recv_sem=ring_sems.at[1, way, step, p],
            device_id={"dp": targets[way]}, device_id_type=pl.DeviceIdType.MESH)

    def gather_copy(way, step, p):
        span = rows_gather(way, step)
        return pltpu.make_async_remote_copy(
            src_ref=total.at[span, columns(p)],
            dst_ref=total.at[span, columns(p)],
            send_sem=gather_sems.at[0, way, step, p],
            recv_sem=gather_sems.at[1, way, step, p],
            device_id={"dp": targets[way]}, device_id_type=pl.DeviceIdType.MESH)

    def rows_gather(way, step):
        shift = lax.rem(chips - 1 + step, chips)
        place_of = lax.rem(place + (chips - shift if way == 0 else shift), chips)
        return pl.ds(pl.multiple_of(64 * place_of + 32 * core + 16 * way, 16), 16)

    def share_copy(way, step):
        span = rows_gather(way, step)
        return pltpu.make_async_remote_copy(
            src_ref=total.at[span],
            dst_ref=total.at[span],
            send_sem=share_sems.at[0, way, step],
            recv_sem=share_sems.at[1, way, step],
            device_id={"dp": sibling}, device_id_type=pl.DeviceIdType.MESH)

    def pair_start(step, carry):
        for way in range(2):
            pair_copy(way, step).start()
        return carry
    lax.fori_loop(0, chips, pair_start, 0)

    for way in range(2):
        pair_copy(way, 0).wait_recv()
        for p in range(PARTS):
            mine = local[rows(way, 0, core), p * part:(p + 1) * part].astype(f32)
            paired[way, 0, :, p * part:(p + 1) * part] = (mine + paired[way, 0, :, p * part:(p + 1) * part].astype(f32)).astype(bf16)
            ring_copy(way, 0, p).start()

    def reduce_step(step, carry):
        for way in range(2):
            pair_copy(way, step).wait_recv()
        for p in range(PARTS):
            for way in range(2):
                ring_copy(way, step - 1, p).wait_recv()
                cols = slice(p * part, (p + 1) * part)
                mine = local[rows(way, step, core), cols].astype(f32)
                paired[way, step, :, cols] = (
                    mine + paired[way, step, :, cols].astype(f32) + landed[way, step - 1, :, cols].astype(f32)
                ).astype(bf16)
                ring_copy(way, step, p).start()
        return carry
    lax.fori_loop(1, chips - 1, reduce_step, 0)

    last = chips - 1
    for way in range(2):
        pair_copy(way, last).wait_recv()
    for p in range(PARTS):
        for way in range(2):
            ring_copy(way, last - 1, p).wait_recv()
            cols = slice(p * part, (p + 1) * part)
            mine = local[rows(way, last, core), cols].astype(f32)
            total[rows(way, last, core), cols] = (
                mine + paired[way, last, :, cols].astype(f32) + landed[way, last - 1, :, cols].astype(f32)
            ).astype(bf16)
            gather_copy(way, 0, p).start()
    for way in range(2):
        share_copy(way, 0).start()

    def gather_step(step, carry):
        for p in range(PARTS):
            for way in range(2):
                gather_copy(way, step - 1, p).wait_recv()
                gather_copy(way, step, p).start()
        for way in range(2):
            share_copy(way, step).start()
        return carry
    lax.fori_loop(1, chips - 1, gather_step, 0)
    for p in range(PARTS):
        for way in range(2):
            gather_copy(way, last - 1, p).wait_recv()
    for way in range(2):
        share_copy(way, last).start()

    def finish(step, carry):
        for way in range(2):
            pair_copy(way, step).wait_send()
            share_copy(way, step).wait()
        return carry
    lax.fori_loop(0, chips, finish, 0)

    def finish_ring(step, carry):
        for way in range(2):
            for p in range(PARTS):
                ring_copy(way, step, p).wait_send()
                gather_copy(way, step, p).wait_send()
        return carry
    lax.fori_loop(0, chips - 1, finish_ring, 0)


def sum_over(local, devices):
    chips = devices // 2
    width = local.shape[1]
    return pl.pallas_call(
        functools.partial(sum_kernel, chips),
        name="ring_sum",
        out_shape=jax.ShapeDtypeStruct(local.shape, bf16),
        in_specs=[pl.BlockSpec(memory_space=pltpu.VMEM)],
        out_specs=pl.BlockSpec(memory_space=pltpu.VMEM),
        scratch_shapes=[
            pltpu.VMEM((2, chips, 16, width), bf16),
            pltpu.VMEM((2, chips - 1, 16, width), bf16),
            pltpu.SemaphoreType.DMA((2, 2, chips)),
            pltpu.SemaphoreType.DMA((2, 2, chips - 1, PARTS)),
            pltpu.SemaphoreType.DMA((2, 2, chips - 1, PARTS)),
            pltpu.SemaphoreType.DMA((2, 2, chips)),
        ],
        compiler_params=pltpu.CompilerParams(collective_id=0, has_side_effects=True, vmem_limit_bytes=60 << 20),
    )(local)


def solution(mesh):
    in_specs = (
        P("section", "dp", None, None),
        P(None, "dp", None),
        P("dp", None, None),
        P("section", None, None),
        P("section", None, None),
        P("section", None, None),
        P("section", None, None),
        P("section", None, None),
        P("section", None, None),
        P("section", None, None),
    )
    out_specs = (
        P("section", "dp", None, None),
        P("section", "dp", None, None),
        P("section", None, None),
        P("section", None, None),
        P("section", None, None),
        P("section", None, None),
        P("section", None, None),
        P("section", None, None),
        P("section", None, None),
    )
    return jax.shard_map(
        per_device, mesh=mesh, in_specs=in_specs, out_specs=out_specs, check_vma=False
    )
```

```python
import functools
import types

import jax
import jax.numpy as jnp
from jax import lax
from jax.experimental import pallas as pl
from jax.experimental.pallas import tpu as pltpu
from jax.sharding import PartitionSpec as P

HEADS = 8
PAIRS = HEADS // 2
EPSILON = 1e-05
MASKED = -1e30
BLOCK = 256
STRIP = 128
WIDTHS = (256,)
PARTS = (4, 5)
UNITS = 1
VMEM_LIMIT = 64 << 20
bf16, f32 = jnp.bfloat16, jnp.float32


def nn(left, right):
    return lax.dot_general(left, right, (((1,), (0,)), ((), ())), preferred_element_type=f32)


def nt(left, right):
    return lax.dot_general(left, right, (((1,), (1,)), ((), ())), preferred_element_type=f32)


def tn(left, right):
    return lax.dot_general(left, right, (((0,), (0,)), ((), ())), preferred_element_type=f32)


def blocks(total):
    return [slice(i, i + BLOCK) for i in range(0, total, BLOCK)]


def standardize(values):
    center = values - jnp.mean(values, axis=-1, keepdims=True)
    scale = lax.rsqrt(jnp.mean(center * center, axis=-1, keepdims=True) + EPSILON)
    return center * scale, scale


def norm_back(grad, unit, scale, gain):
    scaled = grad * gain
    first = jnp.mean(scaled, axis=-1, keepdims=True)
    second = jnp.mean(scaled * unit, axis=-1, keepdims=True)
    return (scaled - first - unit * second) * scale


def fold(values):
    return jnp.sum(values.reshape(-1, 8, values.shape[-1]), axis=0)


def half_masks(value):
    lanes = lax.broadcasted_iota(jnp.int32, (1, 128), 1)
    return [jnp.where((lanes < 64) == (a == 0), value, 0.0).astype(bf16) for a in range(2)]


def pair_lanes(pair, start=0):
    return pl.ds(pl.multiple_of(start + pair * 128, 128), 128)


class Mover:
    def __init__(self, sems):
        self.sems, self.used, self.open = sems, 0, []

    def make(self, source, target):
        copy = pltpu.make_async_copy(source, target, self.sems.at[self.used])
        self.used += 1
        return copy

    def load(self, source, target):
        copy = self.make(source, target)
        copy.start()
        return copy

    def store(self, source, target):
        copy = self.make(source, target)
        copy.start()
        self.open.append(copy)

    def finish(self):
        for copy in self.open:
            copy.wait()
        self.open = []


def window_of(lowest, highest, width, size):
    start = jnp.minimum(lax.div(lowest, 16) * 16, size - width)
    return start, highest - start <= width


def count(flags):
    return jnp.sum(jnp.where(flags, 1.0, 0.0)).astype(jnp.int32)


def turn(rows, start, width):
    size = rows.shape[1]
    if width == size:
        return rows
    return pltpu.roll(rows, size - start, 1)[:, :width]


def spans(own_id, other_row, causal, turned, span_ref):
    for block in range(other_row.shape[1] // STRIP):
        base = block * STRIP
        lowest = count(other_row < own_id(base).astype(f32))
        highest = count(other_row <= own_id(base + STRIP - 1).astype(f32))
        if causal is not None and turned:
            lowest = jnp.where(causal, jnp.maximum(lowest, base), lowest)
        elif causal is not None:
            highest = jnp.where(causal, jnp.minimum(highest, base + STRIP), highest)
        span_ref[0, block] = lowest
        span_ref[1, block] = highest


def attend(q_ref, q_start, k_ref, k_start, v_ref, v_start, span_ref, key_row, column_ref, causal, out_ref, mass_ref):
    size = q_ref.shape[0]
    masks = half_masks(64 ** -0.5)
    key_ids = jnp.broadcast_to(key_row, (8, size))

    def one_block(block, carry):
        base = pl.multiple_of(block * STRIP, STRIP)
        rows = pl.ds(base, STRIP)
        lowest, highest = span_ref[0, block], span_ref[1, block]

        def run(width, start):
            ids = turn(key_ids, start, width)[:1, :]
            allowed = column_ref[rows, :1] == ids
            if causal is not None:
                ahead = (lax.broadcasted_iota(jnp.int32, (STRIP, width), 1) + start
                         - lax.broadcasted_iota(jnp.int32, (STRIP, width), 0) - base)
                allowed = allowed & ((ahead <= 0) | jnp.logical_not(causal))
            bias = jnp.where(allowed, 0.0, MASKED)
            bias = jnp.concatenate([bias, bias], axis=0)
            keys_at = pl.ds(pl.multiple_of(start, 16), width) if width < size else slice(None)
            lanes = lax.broadcasted_iota(jnp.int32, (STRIP, 128), 1)
            mass = jnp.zeros((STRIP, 128), f32)
            for pair in range(PAIRS):
                query = q_ref[rows, q_start + pair * 128:q_start + pair * 128 + 128]
                keys = k_ref[keys_at, k_start + pair * 128:k_start + pair * 128 + 128]
                values = v_ref[keys_at, v_start + pair * 128:v_start + pair * 128 + 128]
                both = jnp.concatenate([query * masks[0], query * masks[1]], axis=0)
                scores = nt(both, keys) + bias
                top = jnp.max(scores, axis=-1, keepdims=True)
                weight = jnp.exp(scores - top)
                mixed = nn(weight.astype(bf16), jnp.concatenate([values, jnp.ones_like(values)], axis=1))
                total = mixed[:, 128:]
                mixed = mixed[:, :128] * (1.0 / total)
                level = top + jnp.log(total)
                mass = jnp.where(lanes == 2 * pair, level[:STRIP], jnp.where(lanes == 2 * pair + 1, level[STRIP:], mass))
                out_ref[rows, pair * 128:pair * 128 + 128] = jnp.where(
                    lanes < 64, mixed[:STRIP], mixed[STRIP:]).astype(bf16)
            mass_ref[rows, :] = mass

        by_width(lowest, highest, size, run)
        return carry

    lax.fori_loop(0, size // STRIP, one_block, 0)


def by_width(lowest, highest, size, run):
    open_ = None
    for width in WIDTHS:
        start, fits = window_of(lowest, highest, width, size)
        chosen = fits if open_ is None else fits & open_
        pl.when(chosen)(functools.partial(run, width, start))
        open_ = jnp.logical_not(fits) if open_ is None else open_ & jnp.logical_not(fits)
    pl.when(open_)(functools.partial(run, size, 0))


def head_sums(left_ref, right_ref, out_ref, base=0):
    features = left_ref.shape[1]
    depth = features // HEADS
    heads = lax.broadcasted_iota(jnp.int32, (HEADS, features), 0)
    members = lax.broadcasted_iota(jnp.int32, (HEADS, features), 1) // depth
    pick = jnp.where(heads == members, 1.0, 0.0).astype(bf16)
    for rows in blocks(left_ref.shape[0]):
        product = left_ref[rows, :].astype(f32) * right_ref[pl.ds(pl.multiple_of(base + rows.start, BLOCK), BLOCK), :].astype(f32)
        high = product.astype(bf16)
        low = (product - high.astype(f32)).astype(bf16)
        out_ref[:, rows] = nt(pick, high) + nt(pick, low)


def attend_back(q_ref, q_start, k_ref, k_start, v_ref, v_start, grad_ref, span_ref, query_row, column_ref, causal,
                mass_ref, delta_ref, dq_ref, dq_start, dk_ref, dk_start, dv_ref, dv_start, sum_ref, tick=None, q_rows=slice(None),
                base_row=0):
    size = q_ref.shape[0]
    scale = 64 ** -0.5
    scaled, plain = half_masks(scale), half_masks(1.0)
    query_ids = jnp.broadcast_to(query_row, (8, size))
    sum_ref[...] = jnp.zeros_like(sum_ref)

    def one_block(block, carry):
        base = pl.multiple_of(block * STRIP, STRIP)
        rows = pl.ds(base, STRIP)
        if tick is None:
            lowest, highest = span_ref[0, block], span_ref[1, block]
        out_rows = pl.ds(pl.multiple_of(base_row + base, STRIP), STRIP)

        def run(width, start):
            ids = turn(query_ids, start, width)[:1, :]
            mass, delta = turn(mass_ref[...], start, width), turn(delta_ref[...], start, width)
            allowed = column_ref[rows, :1] == ids
            if causal is not None:
                behind = (lax.broadcasted_iota(jnp.int32, (STRIP, width), 0) + base
                          - lax.broadcasted_iota(jnp.int32, (STRIP, width), 1) - start)
                allowed = allowed & ((behind <= 0) | jnp.logical_not(causal))
            bias = jnp.where(allowed, 0.0, MASKED)
            at = pl.ds(pl.multiple_of(start, 16), width) if width < size else slice(None)
            lanes = lax.broadcasted_iota(jnp.int32, (STRIP, 128), 1)
            for pair in range(PAIRS):
                keys = k_ref[rows, k_start + pair * 128:k_start + pair * 128 + 128]
                values = v_ref[rows, v_start + pair * 128:v_start + pair * 128 + 128]
                query = q_ref[at, q_start + pair * 128:q_start + pair * 128 + 128]
                grad = grad_ref[at, pair * 128:pair * 128 + 128]
                both_keys = jnp.concatenate([keys * scaled[0], keys * scaled[1]], axis=0)
                both_values = jnp.concatenate([values * plain[0], values * plain[1]], axis=0)
                scores = nt(both_keys, query)
                inner = nt(both_values, grad)
                weights, slopes = [], []
                for a in range(2):
                    part = slice(a * STRIP, a * STRIP + STRIP)
                    head = slice(2 * pair + a, 2 * pair + a + 1)
                    weight = jnp.exp(scores[part] + (bias - mass[head, :]))
                    slopes.append((weight * (inner[part] - delta[head, :])).astype(bf16))
                    weights.append(weight.astype(bf16))
                slope = jnp.concatenate(slopes, axis=0)
                dv = nn(jnp.concatenate(weights, axis=0), grad)
                dk = nn(slope, query) * scale
                dv_ref[out_rows, dv_start + pair * 128:dv_start + pair * 128 + 128] = jnp.where(
                    lanes < 64, dv[:STRIP], dv[STRIP:]).astype(bf16)
                dk_ref[out_rows, dk_start + pair * 128:dk_start + pair * 128 + 128] = jnp.where(
                    lanes < 64, dk[:STRIP], dk[STRIP:]).astype(bf16)
                sum_ref[at, pair * 128:pair * 128 + 128] += nn(both_keys.T, slope).T
                if tick is not None and pair % 2 == 1:
                    tick(2 * block + pair // 2)

        if tick is None:
            by_width(lowest, highest, size, run)
        else:
            run(size, 0)
        return carry

    lax.fori_loop(0, size // STRIP, one_block, 0)
    dq_ref[q_rows, dq_start:dq_start + sum_ref.shape[1]] = sum_ref[...].astype(bf16)


def as_column(row):
    return jnp.broadcast_to(row, (128, row.shape[1])).T


def role():
    return lax.axis_index("section") == 0


def front_kernel(row, x_hbm, ids_ref, id_ref, qkv_hbm, out_hbm, cross_hbm, up_hbm, down_hbm, gain_in, shift_in, *rest):
    if row:
        rest = rest[1:]
    front_body(row, x_hbm, ids_ref, id_ref, qkv_hbm, out_hbm, cross_hbm, up_hbm, down_hbm, gain_in, shift_in, *rest)


def front_body(row, x_hbm, ids_ref, id_ref, qkv_hbm, out_hbm, cross_hbm, up_hbm, down_hbm, gain_in, shift_in,
                 lowin_o, packed_o, mixed_o, mass_o, unit_o, scale_o, low_o, hidden_o, z_o, slope_o,
                 unit2_o, scale2_o, tail_o, layer_o,
                 gain_ref, shift_ref, span_s, x_v, wqkv, wout, wq, wup, wdown, base_v, column_v, lowin_v, packed_v, mixed_v, mass_v,
                 massrow_v, unit_v, scale_v, low_v, z_v, slope_v, unit2_v, scale2_v, tail_v, sems):
    is_encoder = role()
    features = x_v.shape[1]
    move = Mover(sems)
    load_x = move.load(x_hbm.at[0, row], x_v)
    load_qkv = move.load(qkv_hbm.at[0], wqkv)
    load_out = move.load(out_hbm.at[0], wout)
    load_up = move.make(up_hbm.at[0], wup)
    load_down = move.make(down_hbm.at[0], wdown)
    load_q = move.make(cross_hbm.at[0, :, pl.ds(0, features)], wq)

    @pl.when(is_encoder)
    def _():
        load_up.start()
        load_down.start()

    @pl.when(jnp.logical_not(is_encoder))
    def _():
        load_q.start()

    ids_row = jnp.where(is_encoder, ids_ref[pl.ds(0, 1), row, :], ids_ref[pl.ds(1, 1), row, :])
    ids_row = ids_row.astype(f32)
    column_v[...] = as_column(ids_row)
    gain_ref[...] = gain_in[0].astype(f32)
    shift_ref[...] = shift_in[0].astype(f32)
    side = jnp.where(is_encoder, 0, 1)
    spans(lambda at: id_ref[side, row, at], ids_row, jnp.logical_not(is_encoder), False, span_s)
    load_x.wait()

    @pl.when(is_encoder)
    def _():
        for rows in blocks(x_v.shape[0]):
            unit, _ = standardize(x_v[rows, :].astype(f32))
            value = unit * gain_ref[0:1, :] + shift_ref[0:1, :]
            base_v[rows, :] = value
            lowin_v[rows, :] = value.astype(bf16)

    @pl.when(jnp.logical_not(is_encoder))
    def _():
        base_v[...] = x_v[...].astype(f32)
        lowin_v[...] = x_v[...]

    move.store(lowin_v, lowin_o)
    load_qkv.wait()
    for rows in blocks(x_v.shape[0]):
        packed_v[rows, :] = nn(lowin_v[rows, :], wqkv[...]).astype(bf16)
    move.store(packed_v, packed_o)
    attend(packed_v, 0, packed_v, features, packed_v, 2 * features, span_s, ids_row,
           column_v, jnp.logical_not(is_encoder), mixed_v, mass_v)
    massrow_v[...] = mass_v[...].T[:HEADS, :]
    move.store(massrow_v, mass_o)
    move.store(mixed_v, mixed_o)
    load_out.wait()
    which = jnp.where(is_encoder, 1, 0)
    gain, shift = gain_ref[pl.ds(which, 1), :], shift_ref[pl.ds(which, 1), :]
    for rows in blocks(x_v.shape[0]):
        unit, scale = standardize(base_v[rows, :] + nn(mixed_v[rows, :], wout[...]))
        unit_v[rows, :] = unit.astype(bf16)
        scale_v[rows, :] = jnp.broadcast_to(scale, (BLOCK, 128))
        hidden = unit * gain + shift
        base_v[rows, :] = hidden
        low_v[rows, :] = hidden.astype(bf16)
    move.store(unit_v, unit_o)
    move.store(scale_v, scale_o)
    move.store(low_v, low_o)

    store_hidden = move.make(base_v, hidden_o)
    stores = [move.make(a, b) for a, b in ((z_v, z_o), (slope_v, slope_o), (unit2_v, unit2_o), (scale2_v, scale2_o),
                                           (tail_v, layer_o.at[0, row]))]

    @pl.when(jnp.logical_not(is_encoder))
    def _():
        store_hidden.start()
        load_q.wait()
        for rows in blocks(x_v.shape[0]):
            tail_v[rows, :] = nn(low_v[rows, :], wq[...]).astype(bf16)
        store_hidden.wait()

    @pl.when(is_encoder)
    def _():
        load_up.wait()
        load_down.wait()
        for rows in blocks(x_v.shape[0]):
            feed_forward(low_v, rows, wup, z_v, slope_v)
            unit, scale = standardize(base_v[rows, :] + nn(z_v[rows, :], wdown[...]))
            unit2_v[rows, :] = unit.astype(bf16)
            scale2_v[rows, :] = jnp.broadcast_to(scale, (BLOCK, 128))
            tail_v[rows, :] = (unit * gain_ref[2:3, :] + shift_ref[2:3, :]).astype(bf16)
        for copy in stores:
            copy.start()
        for copy in stores:
            copy.wait()

    move.store(tail_v, tail_o)
    move.finish()


def feed_forward(low_ref, rows, wup, z_ref, slope_ref):
    for start in range(0, wup.shape[1], 512):
        columns = slice(start, start + 512)
        up = nn(low_ref[rows, :], wup[:, columns])
        gate = 1.0 / (1.0 + jnp.exp(-up))
        z = up * gate
        z_ref[rows, columns] = z.astype(bf16)
        slope_ref[rows, columns] = (gate + z * (1.0 - gate)).astype(bf16)


def feed_back(grad_ref, rows, wup, wdown, slope_ref, du_ref):
    for start in range(0, wup.shape[1], 512):
        columns = slice(start, start + 512)
        dz = nt(grad_ref[rows, :], wdown[columns, :])
        du_ref[rows, columns] = (dz * slope_ref[rows, columns].astype(f32)).astype(bf16)
    return nt(du_ref[rows, :], wup[...])


def cross_kernel(row, memory_hbm, query_hbm, hidden_hbm, cot_hbm, ids_ref, id_ref, kv_hbm, cross_hbm, up_hbm, down_hbm,
                 gain_in, shift_in, before,
                 layer_o, low_o, z_o, du_o, df_o, mixed_o, dbranch_o, dr_o, dq_o, dkv_o, dmem_o, sums_o,
                 gain_ref, shift_ref, span_s, turned_s, memory_v, query_v, hidden_v, cot_v, wkv, wout, wup, wdown, kv_v, column_v, mixed_v, mass_v, massrow_v,
                 delta_v, low_v, z_v, slope_v, unit_v, scale_v, du_v, df_v, dbranch_v, dmixed_v, dq_v, dkv_v, dmem_v,
                 out_v, sum_v, sums_v, sems):
    is_encoder = role()
    features = memory_v.shape[1]
    size = memory_v.shape[0]

    @pl.when(jnp.logical_not(is_encoder))
    def _():
        move = Mover(sems)
        load_kv = move.load(kv_hbm, wkv)
        load_memory = move.load(memory_hbm, memory_v)
        load_query = move.load(query_hbm, query_v)
        load_hidden = move.load(hidden_hbm, hidden_v)
        load_out = move.load(cross_hbm.at[0, :, pl.ds(features, features)], wout)
        load_up = move.load(up_hbm.at[0], wup)
        load_down = move.load(down_hbm.at[0], wdown)
        load_cot = move.load(cot_hbm.at[row], cot_v)
        source, target = ids_ref[0, row:row + 1, :], ids_ref[1, row:row + 1, :]
        source, target = source.astype(f32), target.astype(f32)
        column_v[...] = as_column(target)
        gain_ref[...] = gain_in[0].astype(f32)
        shift_ref[...] = shift_in[0].astype(f32)
        spans(lambda at: id_ref[1, row, at], source, None, False, span_s)
        spans(lambda at: id_ref[0, row, at], target, None, True, turned_s)
        sums_v[...] = jnp.zeros_like(sums_v)
        load_kv.wait()
        load_memory.wait()
        @pl.loop(0, size // BLOCK)
        def _(index):
            rows = pl.ds(pl.multiple_of(index * BLOCK, BLOCK), BLOCK)
            kv_v[rows, :] = nn(memory_v[rows, :], wkv[...]).astype(bf16)
        load_query.wait()
        attend(query_v, 0, kv_v, 0, kv_v, features, span_s, source, column_v, None, mixed_v, mass_v)
        massrow_v[...] = mass_v[...].T[:HEADS, :]
        move.store(mixed_v, mixed_o)
        load_hidden.wait()
        load_out.wait()
        for rows in blocks(size):
            unit, scale = standardize(hidden_v[rows, :] + nn(mixed_v[rows, :], wout[...]))
            unit_v[rows, :] = unit.astype(bf16)
            scale_v[rows, :] = jnp.broadcast_to(scale, (BLOCK, 128))
            hidden = unit * gain_ref[1:2, :] + shift_ref[1:2, :]
            hidden_v[rows, :] = hidden
            low_v[rows, :] = hidden.astype(bf16)
        move.store(low_v, low_o)
        load_up.wait()
        load_down.wait()
        load_cot.wait()
        for rows in blocks(size):
            feed_forward(low_v, rows, wup, z_v, slope_v)
            unit, scale = standardize(hidden_v[rows, :] + nn(z_v[rows, :], wdown[...]))
            out_v[rows, :] = (unit * gain_ref[2:3, :] + shift_ref[2:3, :]).astype(bf16)
            grad = cot_v[rows, :].astype(f32)
            sums_v[2] += fold(grad * unit)
            sums_v[5] += fold(grad)
            dr = norm_back(grad, unit, scale, gain_ref[2:3, :])
            hidden_v[rows, :] = dr
            df_v[rows, :] = dr.astype(bf16)
        move.store(z_v, z_o)
        move.store(df_v, df_o)
        move.store(out_v, layer_o.at[0, row])
        for rows in blocks(size):
            grad = hidden_v[rows, :] + feed_back(df_v, rows, wup, wdown, slope_v, du_v)
            unit = unit_v[rows, :].astype(f32)
            sums_v[1] += fold(grad * unit)
            sums_v[4] += fold(grad)
            dr = norm_back(grad, unit, scale_v[rows, :1], gain_ref[1:2, :])
            hidden_v[rows, :] = dr
            dbranch_v[rows, :] = dr.astype(bf16)
            dmixed_v[rows, :] = nt(dbranch_v[rows, :], wout[...]).astype(bf16)
        move.store(du_v, du_o)
        move.store(dbranch_v, dbranch_o)
        move.store(hidden_v, dr_o)
        move.store(sums_v, sums_o)
        column_v[...] = as_column(source)
        head_sums(dmixed_v, mixed_v, delta_v)
        attend_back(query_v, 0, kv_v, 0, kv_v, features, dmixed_v, turned_s, target, column_v, None,
                    massrow_v, delta_v, dq_v, 0, dkv_v, 0, dkv_v, features, sum_v)
        move.store(dq_v, dq_o)
        move.store(dkv_v, dkv_o)
        @pl.loop(0, size // BLOCK)
        def _(index):
            rows = pl.ds(pl.multiple_of(index * BLOCK, BLOCK), BLOCK)
            dmem_v[rows, :] = nt(dkv_v[rows, :], wkv[...]).astype(bf16)
        move.store(dmem_v, dmem_o)
        move.finish()


def back_kernel(enc_row, dec_row, dmem_hbm, unit2_hbm, scale2_hbm, slope_hbm, dr_hbm, dq_hbm,
                eunit_hbm, escale_hbm, epacked_hbm, emixed_hbm, emass_hbm,
                dunit_hbm, dscale_hbm, dpacked_hbm, dmixed_hbm, dmass_hbm,
                x_hbm, ids_ref, id_ref, qkv_hbm, out_hbm, cross_hbm, up_hbm, down_hbm, gain_in, z_hbm, low_hbm, *rest):
    more = [None, None]
    if enc_row:
        more, rest = rest[:2], rest[2:]
    else:
        more, rest = rest[:12], rest[12:]
    back_body(enc_row, dec_row, dmem_hbm, unit2_hbm, scale2_hbm, slope_hbm, dr_hbm, dq_hbm,
              eunit_hbm, escale_hbm, epacked_hbm, emixed_hbm, emass_hbm,
              dunit_hbm, dscale_hbm, dpacked_hbm, dmixed_hbm, dmass_hbm,
              x_hbm, ids_ref, id_ref, qkv_hbm, out_hbm, cross_hbm, up_hbm, down_hbm, gain_in, z_hbm, low_hbm, more, *rest)


def back_body(enc_row, dec_row, dmem_hbm, unit2_hbm, scale2_hbm, slope_hbm, dr_hbm, dq_hbm,
                eunit_hbm, escale_hbm, epacked_hbm, emixed_hbm, emass_hbm,
                dunit_hbm, dscale_hbm, dpacked_hbm, dmixed_hbm, dmass_hbm,
                x_hbm, ids_ref, id_ref, qkv_hbm, out_hbm, cross_hbm, up_hbm, down_hbm, gain_in, z_hbm, low_hbm, more,
                ffn_o, dbranch_o, dpacked_o, dx_o, sums_o,
                gain_ref, span_s, z_v, low_v, ffn_v, *rest):
    (                dmem_v, unit2_v, scale2_v, slope_v, dr_v, dq_v, unit_v, scale_v, packed_v, mixed_v, mass_v, x_v,
                wqkv, wout, wq, wup, wdown, column_v, delta_v, du_v, df_v, dbranch_v, dout_v, dpacked_v, sum_v,
                sums_v) = rest[:26]
    many, sems = rest[26:-1], rest[-1]
    is_encoder = role()
    features = mixed_v.shape[1]
    size = mixed_v.shape[0]

    def run():
        move = Mover(sems)
        is_decoder = jnp.logical_not(is_encoder)
        load_dmem = move.make(dmem_hbm, dmem_v)
        load_unit2 = move.make(unit2_hbm, unit2_v)
        load_scale2 = move.make(scale2_hbm, scale2_v)
        load_slope = move.make(slope_hbm, slope_v)
        load_down = move.make(down_hbm.at[0], wdown)
        load_up = move.make(up_hbm.at[0], wup)
        load_dr = move.make(dr_hbm, dr_v)
        load_dq = move.make(dq_hbm, dq_v)
        load_q = move.make(cross_hbm.at[0, :, pl.ds(0, features)], wq)
        firsts = [load_dmem, load_unit2, load_scale2, load_down, load_slope, load_up]

        sums_v[...] = jnp.zeros_like(sums_v)
        enc_selfs = [(eunit_hbm, unit_v), (escale_hbm, scale_v), (emixed_hbm, mixed_v), (epacked_hbm, packed_v), (emass_hbm, mass_v)]
        dec_selfs = [(dunit_hbm, unit_v), (dscale_hbm, scale_v), (dmixed_hbm, mixed_v), (dpacked_hbm, packed_v), (dmass_hbm, mass_v)]
        enc_pairs, dec_pairs = [], []
        for (es, ev), (ds, dv) in zip(enc_selfs, dec_selfs):
            enc_pairs.append(move.make(es, ev))
            dec_pairs.append(pltpu.make_async_copy(ds, dv, sems.at[move.used - 1]))
        load_x = move.make(x_hbm.at[0, enc_row or 0], x_v)
        load_out = move.make(out_hbm.at[0], wout)
        load_qkv = move.make(qkv_hbm.at[0], wqkv)
        store_ffn = move.make(ffn_v, ffn_o)
        load_low = move.make(low_hbm, low_v)
        load_z = move.make(z_hbm, z_v)
        load_before = move.make(more[1], ffn_v) if enc_row else None
        ffn_loads = [load_low, load_z] + ([load_before] if enc_row else [])
        dx_sem = sems.at[move.used]
        move.used += 1

        @pl.when(is_encoder)
        def _():
            for copy in firsts:
                copy.start()
            for copy in enc_pairs:
                copy.start()
            load_x.start()
            for copy in ffn_loads:
                copy.start()

        @pl.when(is_decoder)
        def _():
            load_dq.start()
            load_q.start()
            load_dr.start()
            for copy in dec_pairs:
                copy.start()

        load_out.start()
        load_qkv.start()
        enc_ids, dec_ids = ids_ref[0:1, enc_row or 0, :], ids_ref[1:2, dec_row or 0, :]
        ids_row = jnp.where(is_encoder, enc_ids, dec_ids)
        ids_row = ids_row.astype(f32)
        column_v[...] = as_column(ids_row)

        def key_id(at):
            return jnp.where(is_encoder, id_ref[0, enc_row or 0, at], id_ref[1, dec_row or 0, at])

        gain_ref[...] = gain_in[0].astype(f32)
        spans(key_id, ids_row, is_decoder, True, span_s)


        @pl.when(is_encoder)
        def _():
            for copy in firsts[:3]:
                copy.wait()
            for rows in blocks(size):
                grad = dmem_v[rows, :].astype(f32)
                unit = unit2_v[rows, :].astype(f32)
                sums_v[2] += fold(grad * unit)
                sums_v[5] += fold(grad)
                dr = norm_back(grad, unit, scale2_v[rows, :1], gain_ref[2:3, :])
                dr_v[rows, :] = dr
                df_v[rows, :] = dr.astype(bf16)
            for copy in firsts[3:]:
                copy.wait()
            for rows in blocks(size):
                dr_v[rows, :] += feed_back(df_v, rows, wup, wdown, slope_v, du_v)

        @pl.when(is_decoder)
        def _():
            load_dq.wait()
            load_q.wait()
            load_dr.wait()
            for rows in blocks(size):
                dr_v[rows, :] += nt(dq_v[rows, :], wq[...])

        for copy in enc_pairs:
            copy.wait()
        load_out.wait()
        which = jnp.where(is_encoder, 1, 0)
        gain = gain_ref[pl.ds(which, 1), :]
        for rows in blocks(size):
            grad = dr_v[rows, :]
            unit = unit_v[rows, :].astype(f32)
            sums_v[pl.ds(which, 1)] += fold(grad * unit)[None]
            sums_v[pl.ds(which + 3, 1)] += fold(grad)[None]
            dr = norm_back(grad, unit, scale_v[rows, :1], gain)
            dr_v[rows, :] = dr
            dbranch_v[rows, :] = dr.astype(bf16)
            dout_v[rows, :] = nt(dbranch_v[rows, :], wout[...]).astype(bf16)
        move.store(dbranch_v, dbranch_o)
        head_sums(dout_v, mixed_v, delta_v)
        attend_back(packed_v, 0, packed_v, features, packed_v, 2 * features, dout_v, span_s, ids_row, column_v, is_decoder,
                    mass_v, delta_v, dpacked_v, 0, dpacked_v, features, dpacked_v, 2 * features, sum_v)
        move.store(dpacked_v, dpacked_o)
        load_qkv.wait()
        for rows in blocks(size):
            dr_v[rows, :] += nt(dpacked_v[rows, :], wqkv[...])

        @pl.when(is_encoder)
        def _():
            load_x.wait()
            for rows in blocks(size):
                unit, scale = standardize(x_v[rows, :].astype(f32))
                grad = dr_v[rows, :]
                sums_v[0] += fold(grad * unit)
                sums_v[3] += fold(grad)
                dr_v[rows, :] = norm_back(grad, unit, scale, gain_ref[0:1, :])
            for copy in ffn_loads:
                copy.wait()
            ffn_weights(low_v, du_v, z_v, df_v, ffn_v, bool(enc_row))
            store_ffn.start()
            store_ffn.wait()

        pl.when(is_encoder)(lambda: pltpu.make_async_copy(dr_v, dx_o.at[0, enc_row or 0], dx_sem).start())
        pl.when(is_decoder)(lambda: pltpu.make_async_copy(dr_v, dx_o.at[0, dec_row or 0], dx_sem).start())
        pltpu.make_async_copy(dr_v, dx_o.at[0, 0], dx_sem).wait()
        move.store(sums_v, sums_o)
        move.finish()

    if dec_row is not None:
        run()
    else:
        @pl.when(jnp.logical_not(is_encoder))
        def _():
            move = Mover(sems)
            loads = []
            for index, target in enumerate(many):
                for i in range(3):
                    loads.append(move.load(more[3 * index + i], target.at[pl.ds(i * size, size)]))
            for copy in loads[:6]:
                copy.wait()
            z_all, df_all, low_all, du_all = many

            def ready():
                for copy in loads[6:]:
                    copy.wait()

            ffn_weights(low_all, du_all, z_all, df_all, ffn_v, False, ready)
            move.store(ffn_v, ffn_o)
            move.finish()

        pl.when(is_encoder)(run)


def named(layout, refs):
    found, at = types.SimpleNamespace(), 0
    for name, many in vars(layout).items():
        if name[0] != "_":
            setattr(found, name, refs[at] if many == 1 else refs[at:at + many])
            at += many
    assert at == len(refs)
    return found


def place(target, start, value, onto=False):
    columns = slice(start, start + value.shape[1])
    if onto:
        value = value + target[:, columns].astype(f32)
    target[:, columns] = value.astype(target.dtype)


def ffn_weights(flow_v, du_v, z_v, df_v, out_v, onto, ready=None):
    width, hidden = flow_v.shape[1], du_v.shape[1]
    for j in range(0, hidden, width):
        place(out_v, hidden + j, tn(z_v[:, j:j + width], df_v[...]), onto)
    if ready is not None:
        ready()
    for j in range(0, hidden, width):
        place(out_v, j, tn(flow_v[...], du_v[:, j:j + width]), onto)


class MiddleRefs:
    dmem = 1
    unit2 = 1
    scale2 = 1
    slope = 1
    z = 1
    low = 1
    up = 1
    down = 1
    gain_in = 1
    e_ffn = 1
    d_ffn = 1
    dr_o = 1
    sums_o = 1
    ffn_o = 1
    gain = 1
    dmem_v = 1
    unit2_v = 1
    scale2_v = 1
    slope_v = 1
    dr_v = 1
    sums_v = 1
    wup = 1
    wdown = 1
    flow_v = 1
    du_v = 1
    z_v = 1
    df_v = 1
    ffn_v = 1
    sems = 1


def encoder_middle_kernel(*refs):
    r = named(MiddleRefs, refs)
    size = r.dmem_v.shape[0]

    @pl.when(role())
    def _():
        move = Mover(r.sems)
        first = [move.load(a, b) for a, b in ((r.dmem, r.dmem_v), (r.unit2, r.unit2_v), (r.scale2, r.scale2_v))]
        loads = [move.load(r.down.at[0], r.wdown), move.load(r.slope, r.slope_v),
                 move.load(r.up.at[0], r.wup)]
        later = [move.load(r.z, r.z_v), move.load(r.low, r.flow_v), move.load(r.e_ffn, r.ffn_v)]
        gain = r.gain
        gain[...] = r.gain_in[0].astype(f32)
        sums = r.sums_v
        sums[...] = jnp.zeros_like(sums)
        for copy in first:
            copy.wait()
        for rows in blocks(size):
            grad = r.dmem_v[rows, :].astype(f32)
            unit = r.unit2_v[rows, :].astype(f32)
            sums[2] += fold(grad * unit)
            sums[5] += fold(grad)
            dr = norm_back(grad, unit, r.scale2_v[rows, :1], gain[2:3, :])
            r.dr_v[rows, :] = dr
            r.df_v[rows, :] = dr.astype(bf16)
        move.store(sums, r.sums_o)
        for copy in loads:
            copy.wait()
        for rows in blocks(size):
            for start in range(0, r.wup.shape[1], 512):
                columns = slice(start, start + 512)
                dz = nt(r.df_v[rows, :], r.wdown[columns, :])
                r.du_v[rows, columns] = (dz * r.slope_v[rows, columns].astype(f32)).astype(bf16)
            r.dr_v[rows, :] += nt(r.du_v[rows, :], r.wup[...])
        move.store(r.dr_v, r.dr_o)
        for copy in later:
            copy.wait()
        ffn_weights(r.flow_v, r.du_v, r.z_v, r.df_v, r.ffn_v, True)
        move.store(r.ffn_v, r.ffn_o)
        move.finish()


class LastRefs:
    ffn = 1
    a_dr = 1
    d_dr = 3
    d_dq = 3
    unit = 3
    scale = 3
    packed = 3
    mixed = 3
    mass = 3
    x = 1
    ids = 1
    wqkv_hbm = 1
    wout_hbm = 1
    cross_hbm = 1
    gain_in = 1
    lowin = 3
    dpacked = 2
    dbranch = 2
    low = 3
    cmixed = 3
    cdbranch = 3
    memory = 3
    dkv = 3
    e_sums = 3
    d_sums = 4
    before = 1
    ffn_o = 1
    rest_o = 1
    dx_o = 1
    gain = 1
    dr_v = 1
    dq_v = 1
    unit_v = 1
    scale_v = 1
    packed_v = 1
    mass_v = 1
    x_v = 1
    wqkv = 1
    wout = 1
    wq = 1
    column_v = 1
    delta_v = 1
    dout_v = 1
    sum_v = 1
    sums_v = 1
    in_v = 1
    mixed_v = 1
    dpacked_v = 1
    dbranch_v = 1
    low_v = 1
    dqs_v = 1
    cmixed_v = 1
    cdbranch_v = 1
    memory_v = 1
    dkv_v = 1
    kv_v = 1
    norm_v = 1
    sems = 1
    kv_sems = 1
    local1 = 1
    local2 = 1


class RingRefs:
    total1 = 1
    paired1 = 1
    landed1 = 1
    total2 = 1
    paired2 = 1
    landed2 = 1
    pair1 = 1
    ring1 = 1
    gather1 = 1
    share1 = 1
    pair2 = 1
    ring2 = 1
    gather2 = 1
    share2 = 1


def last_kernel(chips, *refs):
    ring_refs = len([name for name in vars(RingRefs) if name[0] != "_"]) if chips else 0
    r = named(LastRefs, refs[:len(refs) - ring_refs])
    ring = named(RingRefs, refs[len(refs) - ring_refs:]) if chips else None
    is_encoder = role()
    is_decoder = jnp.logical_not(is_encoder)
    features = r.dr_v.shape[1]
    size = r.dr_v.shape[0]
    move = Mover(r.sems)
    load_ffn = move.load(r.ffn, r.local1)
    load_out = move.load(r.wout_hbm.at[0], r.wout)
    load_q = move.load(r.cross_hbm.at[0, :, pl.ds(0, features)], r.wq)
    load_qkv = move.load(r.wqkv_hbm.at[0], r.wqkv)
    row_sems = [r.sems.at[move.used + i] for i in range(8)]
    move.used += 8

    def on(side, action):
        if side is None:
            action()
        else:
            pl.when(side)(action)

    def gather(target, pieces, side=None):
        made = [move.make(piece, target.at[pl.ds(i * size, size)]) for i, piece in enumerate(pieces)]

        def start():
            for copy in made:
                copy.start()

        on(side, start)
        return made, side

    def settle(*loads):
        for made, side in loads:
            def wait():
                for copy in made:
                    copy.wait()

            on(side, wait)

    gain = r.gain
    gain[...] = r.gain_in[0].astype(f32)
    sums = r.sums_v
    sums[...] = jnp.zeros_like(sums)
    if chips:
        first = Ring(chips, r.local1, ring.total1, ring.paired1, ring.landed1, ring.pair1, ring.ring1, ring.gather1, ring.share1)
        second = Ring(chips, r.local2, ring.total2, ring.paired2, ring.landed2, ring.pair2, ring.ring2, ring.gather2, ring.share2)
    else:
        first, second = NoRing(r.local1), NoRing(r.local2)
    partner = {"section": 1 - lax.axis_index("section")}
    barrier = pltpu.get_barrier_semaphore()
    for peer in (partner, *first.peers()):
        pl.semaphore_signal(barrier, inc=1, device_id=peer, device_id_type=pl.DeviceIdType.MESH)
    pl.semaphore_wait(barrier, 1 + len(first.peers()))
    send_kv = pltpu.make_async_remote_copy(
        src_ref=r.kv_v, dst_ref=r.local2.at[:, pl.ds(4 * features, 2 * features)], send_sem=r.kv_sems.at[0],
        recv_sem=r.kv_sems.at[1], device_id=partner, device_id_type=pl.DeviceIdType.MESH)
    load_ffn.wait()
    first.begin()
    early = first.units // (2 * chips - 1) if chips else 0
    load_memory = gather(r.memory_v, r.memory, is_decoder)
    load_dkv = gather(r.dkv_v, r.dkv, is_decoder)
    load_in = gather(r.in_v, r.lowin)
    load_mixed = gather(r.mixed_v, r.mixed)
    kept = []
    for target, pieces in ((r.dpacked_v, r.dpacked), (r.dbranch_v, r.dbranch)):
        for i in range(2):
            copy = move.make(pieces[i], target.at[pl.ds(i * size, size)])
            pl.when(is_encoder)(copy.start)
            kept.append((is_encoder, copy))
        copy = move.make(pieces[1], target.at[pl.ds(0, size)])
        pl.when(is_decoder)(copy.start)
        kept.append((is_decoder, copy))
    load_cross = [gather(target, pieces, is_decoder) for target, pieces in (
        (r.low_v, r.low), (r.dqs_v, r.d_dq), (r.cmixed_v, r.cmixed), (r.cdbranch_v, r.cdbranch))]
    lax.fori_loop(0, early, lambda i, carry: (first.unit(i), carry)[1], 0)
    settle(load_memory, load_dkv)

    @pl.when(is_decoder)
    def _():
        for start in range(0, 2 * features, features):
            place(r.kv_v, start, tn(r.memory_v[...], r.dkv_v[:, start:start + features]))
        send_kv.start()

    load_out.wait()
    load_q.wait()
    load_qkv.wait()
    settle(load_mixed)
    for side, copy in kept:
        pl.when(side)(copy.wait)
    start_row = jnp.where(is_encoder, 2, 1)

    def tick(at):
        def one(i, carry):
            first.unit(early + UNITS * at + i)
            return carry

        lax.fori_loop(0, UNITS, one, 0)

    per_row = 2 * (size // STRIP) + 6
    which = jnp.where(is_encoder, 1, 0)
    row_count = 3 - start_row

    def one_row(row, carry):
        done = (row - start_row) * per_row
        base = pl.multiple_of(row * size, size)
        for i in range(1, 3):
            @pl.when(row == i)
            def _():
                for j, (pieces, target) in enumerate(((r.unit, r.unit_v), (r.scale, r.scale_v), (r.packed, r.packed_v),
                                                      (r.mass, r.mass_v))):
                    pltpu.make_async_copy(pieces[i], target, row_sems[j]).start()

                @pl.when(is_decoder)
                def _():
                    pltpu.make_async_copy(r.d_dr[i], r.dr_v, row_sems[4]).start()
                    pltpu.make_async_copy(r.d_dq[i], r.dq_v, row_sems[5]).start()

        @pl.when(is_encoder)
        def _():
            pltpu.make_async_copy(r.a_dr, r.dr_v, row_sems[4]).start()
            pltpu.make_async_copy(r.x.at[0, 2], r.x_v, row_sems[5]).start()

        ids_row = jnp.where(is_encoder, r.ids[0:1, 2, :], r.ids[1:2, 1, :])
        ids_row = jnp.where(is_decoder & (row == 2), r.ids[1:2, 2, :], ids_row)
        ids_row = ids_row.astype(f32)
        r.column_v[...] = as_column(ids_row)
        for j, target in enumerate((r.unit_v, r.scale_v, r.packed_v, r.mass_v, r.dr_v)):
            pltpu.make_async_copy(target, target, row_sems[j]).wait()

        @pl.when(is_decoder)
        def _():
            pltpu.make_async_copy(r.dq_v, r.dq_v, row_sems[5]).wait()
            for rows in blocks(size):
                r.dr_v[rows, :] += nt(r.dq_v[rows, :], r.wq[...])

        for rows in blocks(size):
            moved = pl.ds(pl.multiple_of(base + rows.start, BLOCK), BLOCK)
            grad = r.dr_v[rows, :]
            unit = r.unit_v[rows, :].astype(f32)
            sums[pl.ds(which, 1)] += fold(grad * unit)[None]
            sums[pl.ds(which + 3, 1)] += fold(grad)[None]
            dr = norm_back(grad, unit, r.scale_v[rows, :1], gain[pl.ds(which, 1), :])
            r.dr_v[rows, :] = dr
            r.dbranch_v[moved, :] = dr.astype(bf16)
            r.dout_v[rows, :] = nt(dr.astype(bf16), r.wout[...]).astype(bf16)
            tick(done + rows.start // BLOCK)
        head_sums(r.dout_v, r.mixed_v, r.delta_v, base)
        tick(done + 2)
        attend_back(r.packed_v, 0, r.packed_v, features, r.packed_v, 2 * features, r.dout_v, None, ids_row,
                    r.column_v, is_decoder, r.mass_v, r.delta_v, r.dpacked_v, 0, r.dpacked_v, features,
                    r.dpacked_v, 2 * features, r.sum_v, lambda at: tick(done + 3 + at),
                    pl.ds(base, size), base)
        for rows in blocks(size):
            moved = pl.ds(pl.multiple_of(base + rows.start, BLOCK), BLOCK)
            r.dr_v[rows, :] += nt(r.dpacked_v[moved, :], r.wqkv[...])
            tick(done + per_row - 3 + rows.start // BLOCK)

        @pl.when(is_encoder)
        def _():
            pltpu.make_async_copy(r.x_v, r.x_v, row_sems[5]).wait()
            for rows in blocks(size):
                unit, scale = standardize(r.x_v[rows, :].astype(f32))
                grad = r.dr_v[rows, :]
                sums[0] += fold(grad * unit)
                sums[3] += fold(grad)
                r.dr_v[rows, :] = norm_back(grad, unit, scale, gain[0:1, :])

        store = pltpu.make_async_copy(r.dr_v, r.dx_o.at[0, row], row_sems[6])
        store.start()
        tick(done + per_row - 1)
        store.wait()
        return carry

    lax.fori_loop(start_row, 3, one_row, 0)
    done = row_count * per_row
    settle(load_in)
    for j in range(3):
        place(r.local2, j * features, tn(r.in_v[...], r.dpacked_v[:, j * features:(j + 1) * features]))
        tick(done + j)
    place(r.local2, 3 * features, tn(r.mixed_v[...], r.dbranch_v[...]))
    tick(done + 3)
    settle(*load_cross)
    norm = r.norm_v

    @pl.when(is_encoder)
    def _():
        send_kv.wait_recv()
        total = sums[...] + sum(member[...] for member in r.e_sums)
        norm[0:6, :] = jnp.sum(total, axis=1)

    @pl.when(is_decoder)
    def _():
        place(r.local2, 4 * features, tn(r.low_v[...], r.dqs_v[...]))
        place(r.local2, 5 * features, tn(r.cmixed_v[...], r.cdbranch_v[...]))
        total = sums[...] + sum(member[...] for member in r.d_sums)
        norm[0:6, :] = jnp.sum(total, axis=1)

    norm[6:, :] = jnp.zeros((norm.shape[0] - 6, features), f32)
    place(r.local2, 6 * features, norm[...].T)
    second.begin()

    def both(step, carry):
        first.unit(early + UNITS * (done + 4) + step)
        second.unit(step)
        return carry

    lax.fori_loop(0, max(first.units, second.units), both, 0)
    first.settle_shares()
    move.store(first.total, r.ffn_o)
    second.settle_shares()
    move.store(second.total, r.rest_o)
    first.finish()
    second.finish()
    pl.when(is_decoder)(send_kv.wait_send)
    move.finish()


class NoRing:
    units = 0

    def __init__(self, local):
        self.total = local

    def peers(self):
        return []

    def begin(self):
        pass

    def unit(self, count_):
        pass

    def settle_shares(self):
        pass

    def finish(self):
        pass


class Ring:
    def __init__(self, chips, local, total, paired, landed, pair_sems, ring_sems, gather_sems, share_sems):
        self.chips, self.local, self.total, self.paired, self.landed = chips, local, total, paired, landed
        self.pair_sems, self.ring_sems, self.gather_sems, self.share_sems = pair_sems, ring_sems, gather_sems, share_sems
        self.parts = ring_sems.shape[3]
        self.part = local.shape[1] // self.parts
        self.units = (2 * chips - 1) * self.parts
        me = lax.axis_index("dp")
        self.core = lax.rem(me, 2)
        self.place = ring_place(me, chips)
        self.sibling = me + 1 - 2 * self.core
        self.targets = (ring_device(lax.rem(self.place + 1, chips), chips, self.core),
                        ring_device(lax.rem(self.place + chips - 1, chips), chips, self.core))

    def peers(self):
        return [{"dp": other} for other in (self.sibling, *self.targets)]

    def rows(self, way, step, owner):
        slot = lax.rem(self.place + (self.chips - step if way == 0 else step), self.chips)
        return pl.ds(pl.multiple_of(64 * slot + 32 * owner + 16 * way, 16), 16)

    def late_rows(self, way, step):
        shift = lax.rem(self.chips - 1 + step, self.chips)
        return self.rows(way, shift, self.core)

    def columns(self, p):
        return pl.ds(pl.multiple_of(p * self.part, 128), self.part)

    def remote(self, source, target, sems, at, device):
        return pltpu.make_async_remote_copy(
            src_ref=source, dst_ref=target, send_sem=sems.at[(0, *at)], recv_sem=sems.at[(1, *at)],
            device_id={"dp": device}, device_id_type=pl.DeviceIdType.MESH)

    def pair_copy(self, way, step):
        return self.remote(self.local.at[self.rows(way, step, 1 - self.core)], self.paired.at[way, step],
                           self.pair_sems, (way, step), self.sibling)

    def ring_copy(self, way, step, p):
        return self.remote(self.paired.at[way, step, :, self.columns(p)], self.landed.at[way, step, :, self.columns(p)],
                           self.ring_sems, (way, step, p), self.targets[way])

    def gather_copy(self, way, step, p):
        spot = self.total.at[self.late_rows(way, step), self.columns(p)]
        return self.remote(spot, spot, self.gather_sems, (way, step, p), self.targets[way])

    def share_copy(self, way, step):
        spot = self.total.at[self.late_rows(way, step)]
        return self.remote(spot, spot, self.share_sems, (way, step), self.sibling)

    def begin(self):
        def start(step, carry):
            for way in range(2):
                self.pair_copy(way, step).start()
            return carry
        lax.fori_loop(0, self.chips, start, 0)

    def reduced(self, way, step, p, landed):
        columns = self.columns(p)
        value = self.local[self.rows(way, step, self.core), columns].astype(f32)
        value = value + self.paired[way, step, :, columns].astype(f32)
        if landed:
            value = value + self.landed[way, step - 1, :, columns].astype(f32)
        return value.astype(bf16)

    def unit(self, count_):
        last = self.chips - 1
        index = lax.div(count_, self.parts)
        p = count_ - index * self.parts
        reduce_at = jnp.minimum(index, last)

        @pl.when((index <= last) & (p == 0))
        def _():
            for way in range(2):
                self.pair_copy(way, reduce_at).wait_recv()

        @pl.when(index == 0)
        def _():
            for way in range(2):
                self.paired[way, 0, :, self.columns(p)] = self.reduced(way, 0, p, False)
                self.ring_copy(way, 0, p).start()

        @pl.when((index > 0) & (index < last))
        def _():
            for way in range(2):
                self.ring_copy(way, reduce_at - 1, p).wait_recv()
                self.paired[way, reduce_at, :, self.columns(p)] = self.reduced(way, reduce_at, p, True)
                self.ring_copy(way, reduce_at, p).start()

        @pl.when(index == last)
        def _():
            for way in range(2):
                self.ring_copy(way, last - 1, p).wait_recv()
                self.total[self.rows(way, last, self.core), self.columns(p)] = self.reduced(way, last, p, True)
                self.gather_copy(way, 0, p).start()

        gather_at = jnp.clip(index - last, 1, last)

        @pl.when((index > last) & (index < 2 * last))
        def _():
            for way in range(2):
                self.gather_copy(way, gather_at - 1, p).wait_recv()
                self.gather_copy(way, gather_at, p).start()

        @pl.when(index == 2 * last)
        def _():
            for way in range(2):
                self.gather_copy(way, last - 1, p).wait_recv()

        @pl.when((index >= last) & (index <= 2 * last) & (p == self.parts - 1))
        def _():
            share_at = jnp.clip(index - last, 0, last)
            for way in range(2):
                self.share_copy(way, share_at).start()

    def settle_shares(self):
        def wait(step, carry):
            for way in range(2):
                self.share_copy(way, step).wait_recv()
            return carry
        lax.fori_loop(0, self.chips, wait, 0)

    def finish(self):
        def wait(step, carry):
            for way in range(2):
                self.pair_copy(way, step).wait_send()
                self.share_copy(way, step).wait_send()
            return carry
        lax.fori_loop(0, self.chips, wait, 0)

        def wait_ring(step, carry):
            for way in range(2):
                for p in range(self.parts):
                    self.ring_copy(way, step, p).wait_send()
                    self.gather_copy(way, step, p).wait_send()
            return carry
        lax.fori_loop(0, self.chips - 1, wait_ring, 0)


def ring_place(index, chips):
    chip = lax.div(index, 2)
    level, side = lax.div(chip, 2), lax.rem(chip, 2)
    return jnp.where(side == 0, level, chips - 1 - level)


def ring_device(place_, chips, core):
    chip = jnp.where(place_ < chips // 2, 2 * place_, 2 * (chips - 1 - place_) + 1)
    return 2 * chip + core


ANY = pl.BlockSpec(memory_space=pl.ANY)
IN_VMEM = pl.BlockSpec(memory_space=pltpu.VMEM)
IN_SMEM = pl.BlockSpec(memory_space=pltpu.SMEM)


def shape(*dims, dtype=bf16):
    return jax.ShapeDtypeStruct(dims, dtype)


def scratch_of(member):
    return member if not isinstance(member, jax.ShapeDtypeStruct) else pltpu.VMEM(member.shape, member.dtype)


def call(name, body, in_specs, outs, scratch, sems, args, flops=0, aliases=()):
    return pl.pallas_call(
        body,
        name=name,
        input_output_aliases=dict(aliases),
        out_shape=outs,
        in_specs=in_specs,
        out_specs=[ANY] * len(outs),
        scratch_shapes=[scratch_of(s) for s in scratch] + [pltpu.SemaphoreType.DMA((sems,))],
        compiler_params=pltpu.CompilerParams(vmem_limit_bytes=VMEM_LIMIT, has_side_effects=True),
        cost_estimate=pl.CostEstimate(flops=flops, bytes_accessed=10 << 20, transcendentals=0),
    )(*args)


def front(row, embed, ids, weights, before):
    qkv, out, cross, up, down, gain, shift = weights
    size, d = embed.shape[2:]
    hidden = up.shape[2]
    outs = [shape(size, d), shape(size, 3 * d), shape(size, d), shape(HEADS, size, dtype=f32), shape(size, d),
            shape(size, 128, dtype=f32), shape(size, d), shape(size, d, dtype=f32), shape(size, hidden),
            shape(size, hidden), shape(size, d), shape(size, 128, dtype=f32), shape(size, d), shape(*embed.shape)]
    scratch = [shape(3, d, dtype=f32), shape(3, d, dtype=f32), pltpu.SMEM((2, size // STRIP), jnp.int32),
               shape(size, d), shape(d, 3 * d), shape(d, d), shape(d, d), shape(d, hidden), shape(hidden, d),
               shape(size, d, dtype=f32), shape(size, 128, dtype=f32), shape(size, d), shape(size, 3 * d),
               shape(size, d), shape(size, 128, dtype=f32), shape(HEADS, size, dtype=f32), shape(size, d),
               shape(size, 128, dtype=f32), shape(size, d), shape(size, hidden), shape(size, hidden),
               shape(size, d), shape(size, 128, dtype=f32), shape(size, d)]
    more = [before] if row else []
    return call(f"front{row}", functools.partial(front_kernel, row),
                [ANY, IN_VMEM, IN_SMEM] + [ANY] * 5 + [IN_VMEM] * 2 + [ANY] * len(more), outs, scratch, 24,
                (embed, ids, ids, qkv, out, cross, up, down, gain, shift, *more), flops=2 * 10**9,
                aliases=[(10, len(outs) - 1)] if row else [])


def cross(row, memory, query, hidden_f, cot, ids, kv_weight, weights, before):
    qkv, out, cross_w, up, down, gain, shift = weights
    size, d = memory.shape
    hidden = up.shape[2]
    outs = [shape(*before.shape), shape(size, d), shape(size, hidden), shape(size, hidden), shape(size, d), shape(size, d),
            shape(size, d), shape(size, d, dtype=f32), shape(size, d), shape(size, 2 * d), shape(size, d),
            shape(6, 8, d, dtype=f32)]
    scratch = [shape(3, d, dtype=f32), shape(3, d, dtype=f32), pltpu.SMEM((2, size // STRIP), jnp.int32),
               pltpu.SMEM((2, size // STRIP), jnp.int32),
               shape(size, d), shape(size, d), shape(size, d, dtype=f32), shape(size, d), shape(d, 2 * d),
               shape(d, d), shape(d, hidden), shape(hidden, d), shape(size, 2 * d), shape(size, 128, dtype=f32),
               shape(size, d), shape(size, 128, dtype=f32), shape(HEADS, size, dtype=f32), shape(HEADS, size, dtype=f32),
               shape(size, d), shape(size, hidden), shape(size, hidden), shape(size, d), shape(size, 128, dtype=f32),
               shape(size, hidden), shape(size, d), shape(size, d), shape(size, d), shape(size, d), shape(size, 2 * d),
               shape(size, d), shape(size, d), shape(size, d, dtype=f32), shape(6, 8, d, dtype=f32)]
    return call(f"cross{row}", functools.partial(cross_kernel, row),
                [ANY] * 4 + [IN_VMEM, IN_SMEM] + [ANY] * 4 + [IN_VMEM] * 2 + [ANY], outs, scratch,
                24, (memory, query, hidden_f, cot, ids, ids, kv_weight, cross_w, up, down, gain, shift, before),
                flops=20 * 10**9, aliases=[(12, 0)])


class BackOuts:
    ffn = 1
    dbranch = 1
    dpacked = 1
    dx = 1
    sums = 1


def back(enc_row, dec_row, dmem, e_front, d_front, d_cross, embed, ids, weights, before, crosses):
    qkv, out, cross_w, up, down, gain, shift = weights
    size, d = embed.shape[2:]
    hidden = up.shape[2]
    outs = [shape(d, 2 * hidden), shape(size, d), shape(size, 3 * d), shape(*embed.shape, dtype=f32),
            shape(6, 8, d, dtype=f32)]
    scratch = [shape(3, d, dtype=f32), pltpu.SMEM((2, size // STRIP), jnp.int32), shape(size, hidden), shape(size, d),
               shape(d, 2 * hidden),
               shape(size, d), shape(size, d), shape(size, 128, dtype=f32), shape(size, hidden),
               shape(size, d, dtype=f32), shape(size, d), shape(size, d), shape(size, 128, dtype=f32),
               shape(size, 3 * d), shape(size, d), shape(HEADS, size, dtype=f32), shape(size, d),
               shape(d, 3 * d), shape(d, d), shape(d, d), shape(d, hidden), shape(hidden, d),
               shape(size, 128, dtype=f32), shape(HEADS, size, dtype=f32), shape(size, hidden), shape(size, d),
               shape(size, d), shape(size, d), shape(size, 3 * d), shape(size, d, dtype=f32),
               shape(6, 8, d, dtype=f32)]
    args = (dmem, e_front.unit2, e_front.scale2, e_front.slope, d_cross.dr, d_cross.dq,
            e_front.unit, e_front.scale, e_front.packed, e_front.mixed, e_front.mass,
            d_front.unit, d_front.scale, d_front.packed, d_front.mixed, d_front.mass,
            embed, ids, ids, qkv, out, cross_w, up, down, gain, e_front.z, e_front.low)
    if before is None:
        more = [member for group in zip(*[(c.z, c.df, c.low, c.du) for c in crosses]) for member in group]
        tokens = 3 * size
        scratch = scratch + [shape(tokens, hidden), shape(tokens, d), shape(tokens, d), shape(tokens, hidden)]
    else:
        more = [before.dx, before.ffn]
    results = call(f"back_e{enc_row}_d{dec_row}", functools.partial(back_kernel, enc_row, dec_row),
                   [ANY] * 17 + [IN_VMEM, IN_SMEM] + [ANY] * 5 + [IN_VMEM] + [ANY] * (2 + len(more)),
                   outs, scratch, 36, (*args, *more), flops=12 * 10**9,
                   aliases=[(len(args), 3)] if before is not None else [])
    return named(BackOuts, results)


def spread_kernel(ffn_ref, rest_ref, dx_ref, qkv_ref, out_ref, cross_ref, up_ref, down_ref, gain_ref, shift_ref, dx_o):
    dx_o[...] = dx_ref[...]
    start = up_ref.shape[2]
    up_ref[0] = ffn_ref[:, :start].astype(f32)
    for i in range(down_ref.shape[0]):
        down_ref[i] = ffn_ref[:, start:start + down_ref.shape[2]].astype(f32)
        start += down_ref.shape[2]
    start = 0
    for ref in (qkv_ref, out_ref, cross_ref):
        ref[0] = rest_ref[:, start:start + ref.shape[2]].astype(f32)
        start += ref.shape[2]
    norms = rest_ref[:, start:].astype(f32).T
    for i in range(3):
        gain_ref[i] = norms[i:i + 1]
        shift_ref[i] = norms[3 + i:4 + i]


def spread(ffn, rest, input_grad, d, hidden):
    slab = 128
    dx_block = pl.BlockSpec((*input_grad.shape[:2], slab, d), lambda i: (0, 0, i, 0))
    widths = [3 * d, d, 2 * d, hidden]
    wide = [jax.ShapeDtypeStruct((1, d, w), f32) for w in widths]
    return pl.pallas_call(
        spread_kernel,
        name="spread",
        grid=(d // slab,),
        in_specs=[pl.BlockSpec((slab, member.shape[1]), lambda i: (i, 0)) for member in (ffn, rest)] + [dx_block],
        out_shape=wide + [shape(hidden // d, d, d, dtype=f32), shape(3, 1, d, dtype=f32), shape(3, 1, d, dtype=f32),
                          shape(*input_grad.shape, dtype=f32)],
        out_specs=[pl.BlockSpec((1, slab, w), lambda i: (0, i, 0)) for w in widths]
        + [pl.BlockSpec((hidden // d, slab, d), lambda i: (0, i, 0))]
        + [pl.BlockSpec((3, 1, slab), lambda i: (0, 0, i))] * 2 + [dx_block],
        compiler_params=pltpu.CompilerParams(vmem_limit_bytes=VMEM_LIMIT),
    )(ffn, rest, input_grad)


class FrontOuts:
    lowin = 1
    packed = 1
    mixed = 1
    mass = 1
    unit = 1
    scale = 1
    low = 1
    hidden = 1
    z = 1
    slope = 1
    unit2 = 1
    scale2 = 1
    tail = 1
    layer = 1


class CrossOuts:
    layer = 1
    low = 1
    z = 1
    du = 1
    df = 1
    mixed = 1
    dbranch = 1
    dr = 1
    dq = 1
    dkv = 1
    dmem = 1
    sums = 1


def per_device(embeddings, segments, cotangent, attn_qkv, attn_out, cross_proj, ffn_up, ffn_down, norm_gain, norm_bias):
    weights = (attn_qkv, attn_out, cross_proj, ffn_up, ffn_down, norm_gain, norm_bias)
    row_total, size, d = embeddings.shape[1:]
    hidden = ffn_up.shape[2]
    devices = lax.axis_size("dp")
    kv_weight = lax.ppermute(cross_proj[0], "section", [(0, 1)])

    rows = range(row_total)
    fronts, memories, layer_out = [], [], None
    for row in rows:
        fronts.append(named(FrontOuts, front(row, embeddings, segments, weights, layer_out)))
        layer_out = fronts[row].layer
        memories.append(lax.ppermute(fronts[row].tail, "section", [(0, 1)]))
    crosses, grads = [], []
    for row in rows:
        crosses.append(named(CrossOuts, cross(
            row, memories[row], fronts[row].tail, fronts[row].hidden, cotangent, segments, kv_weight, weights,
            layer_out)))
        layer_out = crosses[row].layer
        grads.append(lax.ppermute(crosses[row].dmem, "section", [(1, 0)]))
    tokens = row_total * size
    backs = []
    for row in range(row_total - 1):
        backs.append(back(row, row - 1 if row else None, grads[row], fronts[row], fronts[max(row - 1, 0)],
                          crosses[max(row - 1, 0)], embeddings, segments, weights, backs[-1] if backs else None, crosses))
    input_grad = backs[-1].dx
    dr, middle_sums, ffn_grad = call(
        "encoder_middle", encoder_middle_kernel, [ANY] * 8 + [IN_VMEM, ANY, ANY],
        [shape(size, d, dtype=f32), shape(6, 8, d, dtype=f32), shape(d, 2 * hidden)],
        [shape(3, d, dtype=f32), shape(size, d), shape(size, d), shape(size, 128, dtype=f32), shape(size, hidden),
         shape(size, d, dtype=f32), shape(6, 8, d, dtype=f32), shape(d, hidden), shape(hidden, d),
         shape(size, d), shape(size, hidden), shape(size, hidden), shape(size, d), shape(d, 2 * hidden)], 24,
        (grads[-1], fronts[-1].unit2, fronts[-1].scale2, fronts[-1].slope, fronts[-1].z, fronts[-1].low,
         ffn_up, ffn_down, norm_gain, backs[-1].ffn, backs[0].ffn),
        flops=16 * 10**9, aliases=[(10, 2)])

    chips = devices // 2 if d == 32 * devices else None
    ffn_width, rest_width = 2 * hidden, 6 * d + 128
    args = (ffn_grad, dr, *[m.dr for m in crosses], *[m.dq for m in crosses], *[m.unit for m in fronts],
            *[m.scale for m in fronts], *[m.packed for m in fronts], *[m.mixed for m in fronts], *[m.mass for m in fronts],
            embeddings, segments, attn_qkv, attn_out, cross_proj, norm_gain, *[m.lowin for m in fronts],
            *[m.dpacked for m in backs], *[m.dbranch for m in backs], *[m.low for m in fronts],
            *[m.mixed for m in crosses], *[m.dbranch for m in crosses], *memories, *[m.dkv for m in crosses],
            *[m.sums for m in backs], middle_sums, *[m.sums for m in crosses], backs[1].sums, input_grad)
    specs = [ANY] * 24 + [IN_VMEM] + [ANY] * 3 + [IN_VMEM] + [ANY] * 22 + [IN_VMEM] * 7 + [ANY]
    scratch = [shape(3, d, dtype=f32), shape(size, d, dtype=f32), shape(size, d), shape(size, d), shape(size, 128, dtype=f32),
               shape(size, 3 * d), shape(HEADS, size, dtype=f32), shape(size, d), shape(d, 3 * d), shape(d, d), shape(d, d),
               shape(size, 128, dtype=f32), shape(HEADS, size, dtype=f32), shape(size, d), shape(size, d, dtype=f32),
               shape(6, 8, d, dtype=f32), shape(tokens, d), shape(tokens, d), shape(tokens, 3 * d), shape(tokens, d),
               shape(tokens, d), shape(tokens, d), shape(tokens, d), shape(tokens, d), shape(tokens, d),
               shape(tokens, 2 * d), shape(d, 2 * d), shape(128, d, dtype=f32)]
    sems = pltpu.SemaphoreType.DMA
    rings = []
    if chips:
        for width in (ffn_width, rest_width):
            rings += [pltpu.VMEM((d, width), bf16), pltpu.VMEM((2, chips, 16, width), bf16),
                      pltpu.VMEM((2, chips - 1, 16, width), bf16)]
        for parts in PARTS:
            rings += [sems((2, 2, chips)), sems((2, 2, chips - 1, parts)), sems((2, 2, chips - 1, parts)), sems((2, 2, chips))]
    ffn_total, rest_total, input_grad = pl.pallas_call(
        functools.partial(last_kernel, chips),
        name="last",
        out_shape=[shape(d, ffn_width), shape(d, rest_width), shape(*embeddings.shape, dtype=f32)],
        in_specs=specs,
        out_specs=[ANY] * 3,
        scratch_shapes=[pltpu.VMEM(m.shape, m.dtype) for m in scratch] + [sems((52,)), sems((2,)),
                        pltpu.VMEM((d, ffn_width), bf16), pltpu.VMEM((d, rest_width), bf16)] + rings,
        input_output_aliases={len(args) - 1: 2},
        compiler_params=pltpu.CompilerParams(vmem_limit_bytes=VMEM_LIMIT, has_side_effects=True, collective_id=0),
        cost_estimate=pl.CostEstimate(flops=60 * 10**9, bytes_accessed=30 << 20, transcendentals=0),
    )(*args)
    if not chips:
        ffn_total, rest_total = lax.psum((ffn_total, rest_total), "dp")
    qkv, out, crossed, up, down, gain, shift, input_grad = spread(ffn_total, rest_total, input_grad, d, hidden)
    return (layer_out, input_grad, qkv, out, crossed, up, down.reshape(1, hidden, d), gain.transpose(1, 0, 2),
            shift.transpose(1, 0, 2))


def solution(mesh):
    in_specs = (
        P("section", "dp", None, None),
        P(None, "dp", None),
        P("dp", None, None),
        P("section", None, None),
        P("section", None, None),
        P("section", None, None),
        P("section", None, None),
        P("section", None, None),
        P("section", None, None),
        P("section", None, None),
    )
    out_specs = (
        P("section", "dp", None, None),
        P("section", "dp", None, None),
        P("section", None, None),
        P("section", None, None),
        P("section", None, None),
        P("section", None, None),
        P("section", None, None),
        P("section", None, None),
        P("section", None, None),
    )
    return jax.shard_map(
        per_device, mesh=mesh, in_specs=in_specs, out_specs=out_specs, check_vma=False
    )
```

```python
import functools
import types

import jax
import jax.numpy as jnp
from jax import lax
from jax.experimental import pallas as pl
from jax.experimental.pallas import tpu as pltpu
from jax.sharding import PartitionSpec as P

HEADS = 8
PAIRS = HEADS // 2
EPSILON = 1e-05
MASKED = -1e30
BLOCK = 256
STRIP = 128
WIDTHS = (256,)
PARTS = (4, 5)
UNITS = 1
VMEM_LIMIT = 64 << 20
bf16, f32 = jnp.bfloat16, jnp.float32


def nn(left, right):
    return lax.dot_general(left, right, (((1,), (0,)), ((), ())), preferred_element_type=f32)


def nt(left, right):
    return lax.dot_general(left, right, (((1,), (1,)), ((), ())), preferred_element_type=f32)


def tn(left, right):
    return lax.dot_general(left, right, (((0,), (0,)), ((), ())), preferred_element_type=f32)


def blocks(total):
    return [slice(i, i + BLOCK) for i in range(0, total, BLOCK)]


def standardize(values):
    center = values - jnp.mean(values, axis=-1, keepdims=True)
    scale = lax.rsqrt(jnp.mean(center * center, axis=-1, keepdims=True) + EPSILON)
    return center * scale, scale


def norm_back(grad, unit, scale, gain):
    scaled = grad * gain
    first = jnp.mean(scaled, axis=-1, keepdims=True)
    second = jnp.mean(scaled * unit, axis=-1, keepdims=True)
    return (scaled - first - unit * second) * scale


def fold(values):
    return jnp.sum(values.reshape(-1, 8, values.shape[-1]), axis=0)


def half_masks(value):
    lanes = lax.broadcasted_iota(jnp.int32, (1, 128), 1)
    return [jnp.where((lanes < 64) == (a == 0), value, 0.0).astype(bf16) for a in range(2)]


def pair_lanes(pair, start=0):
    return pl.ds(pl.multiple_of(start + pair * 128, 128), 128)


class Mover:
    def __init__(self, sems):
        self.sems, self.used, self.open = sems, 0, []

    def make(self, source, target):
        copy = pltpu.make_async_copy(source, target, self.sems.at[self.used])
        self.used += 1
        return copy

    def load(self, source, target):
        copy = self.make(source, target)
        copy.start()
        return copy

    def store(self, source, target):
        copy = self.make(source, target)
        copy.start()
        self.open.append(copy)

    def finish(self):
        for copy in self.open:
            copy.wait()
        self.open = []


def window_of(lowest, highest, width, size):
    start = jnp.minimum(lax.div(lowest, 16) * 16, size - width)
    return start, highest - start <= width


def count(flags):
    return jnp.sum(jnp.where(flags, 1.0, 0.0)).astype(jnp.int32)


def turn(rows, start, width):
    size = rows.shape[1]
    if width == size:
        return rows
    return pltpu.roll(rows, size - start, 1)[:, :width]


def spans(own_id, other_row, causal, turned, span_ref):
    for block in range(other_row.shape[1] // STRIP):
        base = block * STRIP
        lowest = count(other_row < own_id(base).astype(f32))
        highest = count(other_row <= own_id(base + STRIP - 1).astype(f32))
        if causal is not None and turned:
            lowest = jnp.where(causal, jnp.maximum(lowest, base), lowest)
        elif causal is not None:
            highest = jnp.where(causal, jnp.minimum(highest, base + STRIP), highest)
        span_ref[0, block] = lowest
        span_ref[1, block] = highest


def attend(q_ref, q_start, k_ref, k_start, v_ref, v_start, span_ref, key_row, column_ref, causal, out_ref, mass_ref):
    size = q_ref.shape[0]
    masks = half_masks(64 ** -0.5)
    key_ids = jnp.broadcast_to(key_row, (8, size))

    def one_block(block, carry):
        base = pl.multiple_of(block * STRIP, STRIP)
        rows = pl.ds(base, STRIP)
        lowest, highest = span_ref[0, block], span_ref[1, block]

        def run(width, start):
            ids = turn(key_ids, start, width)[:1, :]
            allowed = column_ref[rows, :1] == ids
            if causal is not None:
                ahead = (lax.broadcasted_iota(jnp.int32, (STRIP, width), 1) + start
                         - lax.broadcasted_iota(jnp.int32, (STRIP, width), 0) - base)
                allowed = allowed & ((ahead <= 0) | jnp.logical_not(causal))
            bias = jnp.where(allowed, 0.0, MASKED)
            bias = jnp.concatenate([bias, bias], axis=0)
            keys_at = pl.ds(pl.multiple_of(start, 16), width) if width < size else slice(None)
            lanes = lax.broadcasted_iota(jnp.int32, (STRIP, 128), 1)
            mass = jnp.zeros((STRIP, 128), f32)
            for pair in range(PAIRS):
                query = q_ref[rows, q_start + pair * 128:q_start + pair * 128 + 128]
                keys = k_ref[keys_at, k_start + pair * 128:k_start + pair * 128 + 128]
                values = v_ref[keys_at, v_start + pair * 128:v_start + pair * 128 + 128]
                both = jnp.concatenate([query * masks[0], query * masks[1]], axis=0)
                scores = nt(both, keys) + bias
                top = jnp.max(scores, axis=-1, keepdims=True)
                weight = jnp.exp(scores - top)
                mixed = nn(weight.astype(bf16), jnp.concatenate([values, jnp.ones_like(values)], axis=1))
                total = mixed[:, 128:]
                mixed = mixed[:, :128] * (1.0 / total)
                level = top + jnp.log(total)
                mass = jnp.where(lanes == 2 * pair, level[:STRIP], jnp.where(lanes == 2 * pair + 1, level[STRIP:], mass))
                out_ref[rows, pair * 128:pair * 128 + 128] = jnp.where(
                    lanes < 64, mixed[:STRIP], mixed[STRIP:]).astype(bf16)
            mass_ref[rows, :] = mass

        by_width(lowest, highest, size, run)
        return carry

    lax.fori_loop(0, size // STRIP, one_block, 0)


def by_width(lowest, highest, size, run):
    open_ = None
    for width in WIDTHS:
        start, fits = window_of(lowest, highest, width, size)
        chosen = fits if open_ is None else fits & open_
        pl.when(chosen)(functools.partial(run, width, start))
        open_ = jnp.logical_not(fits) if open_ is None else open_ & jnp.logical_not(fits)
    pl.when(open_)(functools.partial(run, size, 0))


def head_sums(left_ref, right_ref, out_ref, base=0):
    features = left_ref.shape[1]
    depth = features // HEADS
    heads = lax.broadcasted_iota(jnp.int32, (HEADS, features), 0)
    members = lax.broadcasted_iota(jnp.int32, (HEADS, features), 1) // depth
    pick = jnp.where(heads == members, 1.0, 0.0).astype(bf16)
    for rows in blocks(left_ref.shape[0]):
        product = left_ref[rows, :].astype(f32) * right_ref[pl.ds(pl.multiple_of(base + rows.start, BLOCK), BLOCK), :].astype(f32)
        high = product.astype(bf16)
        low = (product - high.astype(f32)).astype(bf16)
        out_ref[:, rows] = nt(pick, high) + nt(pick, low)


def attend_back(q_ref, q_start, k_ref, k_start, v_ref, v_start, grad_ref, span_ref, query_row, column_ref, causal,
                mass_ref, delta_ref, dq_ref, dq_start, dk_ref, dk_start, dv_ref, dv_start, sum_ref, tick=None, q_rows=slice(None),
                base_row=0):
    size = q_ref.shape[0]
    scale = 64 ** -0.5
    scaled, plain = half_masks(scale), half_masks(1.0)
    query_ids = jnp.broadcast_to(query_row, (8, size))
    sum_ref[...] = jnp.zeros_like(sum_ref)

    def one_block(block, carry):
        base = pl.multiple_of(block * STRIP, STRIP)
        rows = pl.ds(base, STRIP)
        if tick is None:
            lowest, highest = span_ref[0, block], span_ref[1, block]
        out_rows = pl.ds(pl.multiple_of(base_row + base, STRIP), STRIP)

        def run(width, start):
            ids = turn(query_ids, start, width)[:1, :]
            mass, delta = turn(mass_ref[...], start, width), turn(delta_ref[...], start, width)
            allowed = column_ref[rows, :1] == ids
            if causal is not None:
                behind = (lax.broadcasted_iota(jnp.int32, (STRIP, width), 0) + base
                          - lax.broadcasted_iota(jnp.int32, (STRIP, width), 1) - start)
                allowed = allowed & ((behind <= 0) | jnp.logical_not(causal))
            bias = jnp.where(allowed, 0.0, MASKED)
            at = pl.ds(pl.multiple_of(start, 16), width) if width < size else slice(None)
            lanes = lax.broadcasted_iota(jnp.int32, (STRIP, 128), 1)
            for pair in range(PAIRS):
                keys = k_ref[rows, k_start + pair * 128:k_start + pair * 128 + 128]
                values = v_ref[rows, v_start + pair * 128:v_start + pair * 128 + 128]
                query = q_ref[at, q_start + pair * 128:q_start + pair * 128 + 128]
                grad = grad_ref[at, pair * 128:pair * 128 + 128]
                both_keys = jnp.concatenate([keys * scaled[0], keys * scaled[1]], axis=0)
                both_values = jnp.concatenate([values * plain[0], values * plain[1]], axis=0)
                scores = nt(both_keys, query)
                inner = nt(both_values, grad)
                weights, slopes = [], []
                for a in range(2):
                    part = slice(a * STRIP, a * STRIP + STRIP)
                    head = slice(2 * pair + a, 2 * pair + a + 1)
                    weight = jnp.exp(scores[part] + (bias - mass[head, :]))
                    slopes.append((weight * (inner[part] - delta[head, :])).astype(bf16))
                    weights.append(weight.astype(bf16))
                slope = jnp.concatenate(slopes, axis=0)
                dv = nn(jnp.concatenate(weights, axis=0), grad)
                dk = nn(slope, query) * scale
                dv_ref[out_rows, dv_start + pair * 128:dv_start + pair * 128 + 128] = jnp.where(
                    lanes < 64, dv[:STRIP], dv[STRIP:]).astype(bf16)
                dk_ref[out_rows, dk_start + pair * 128:dk_start + pair * 128 + 128] = jnp.where(
                    lanes < 64, dk[:STRIP], dk[STRIP:]).astype(bf16)
                sum_ref[at, pair * 128:pair * 128 + 128] += nn(both_keys.T, slope).T
                if tick is not None and pair % 2 == 1:
                    tick(2 * block + pair // 2)

        if tick is None:
            by_width(lowest, highest, size, run)
        else:
            late = causal & (base >= size // 2)
            pl.when(late)(functools.partial(run, size // 2, size // 2))
            pl.when(jnp.logical_not(late))(functools.partial(run, size, 0))
        return carry

    lax.fori_loop(0, size // STRIP, one_block, 0)
    dq_ref[q_rows, dq_start:dq_start + sum_ref.shape[1]] = sum_ref[...].astype(bf16)


def as_column(row):
    return jnp.broadcast_to(row, (128, row.shape[1])).T


def role():
    return lax.axis_index("section") == 0


def front_kernel(row, x_hbm, ids_ref, id_ref, qkv_hbm, out_hbm, cross_hbm, up_hbm, down_hbm, gain_in, shift_in, *rest):
    if row:
        rest = rest[1:]
    front_body(row, x_hbm, ids_ref, id_ref, qkv_hbm, out_hbm, cross_hbm, up_hbm, down_hbm, gain_in, shift_in, *rest)


def front_body(row, x_hbm, ids_ref, id_ref, qkv_hbm, out_hbm, cross_hbm, up_hbm, down_hbm, gain_in, shift_in,
                 lowin_o, packed_o, mixed_o, mass_o, unit_o, scale_o, low_o, hidden_o, z_o, slope_o,
                 unit2_o, scale2_o, tail_o, layer_o,
                 gain_ref, shift_ref, span_s, x_v, wqkv, wout, wq, wup, wdown, base_v, column_v, lowin_v, packed_v, mixed_v, mass_v,
                 massrow_v, unit_v, scale_v, low_v, z_v, slope_v, unit2_v, scale2_v, tail_v, sems):
    is_encoder = role()
    features = x_v.shape[1]
    move = Mover(sems)
    load_x = move.load(x_hbm.at[0, row], x_v)
    load_qkv = move.load(qkv_hbm.at[0], wqkv)
    load_out = move.load(out_hbm.at[0], wout)
    load_up = move.make(up_hbm.at[0], wup)
    load_down = move.make(down_hbm.at[0], wdown)
    load_q = move.make(cross_hbm.at[0, :, pl.ds(0, features)], wq)

    @pl.when(is_encoder)
    def _():
        load_up.start()
        load_down.start()

    @pl.when(jnp.logical_not(is_encoder))
    def _():
        load_q.start()

    ids_row = jnp.where(is_encoder, ids_ref[pl.ds(0, 1), row, :], ids_ref[pl.ds(1, 1), row, :])
    ids_row = ids_row.astype(f32)
    column_v[...] = as_column(ids_row)
    gain_ref[...] = gain_in[0].astype(f32)
    shift_ref[...] = shift_in[0].astype(f32)
    side = jnp.where(is_encoder, 0, 1)
    spans(lambda at: id_ref[side, row, at], ids_row, jnp.logical_not(is_encoder), False, span_s)
    load_x.wait()

    @pl.when(is_encoder)
    def _():
        for rows in blocks(x_v.shape[0]):
            unit, _ = standardize(x_v[rows, :].astype(f32))
            value = unit * gain_ref[0:1, :] + shift_ref[0:1, :]
            base_v[rows, :] = value
            lowin_v[rows, :] = value.astype(bf16)

    @pl.when(jnp.logical_not(is_encoder))
    def _():
        base_v[...] = x_v[...].astype(f32)
        lowin_v[...] = x_v[...]

    move.store(lowin_v, lowin_o)
    load_qkv.wait()
    for rows in blocks(x_v.shape[0]):
        packed_v[rows, :] = nn(lowin_v[rows, :], wqkv[...]).astype(bf16)
    move.store(packed_v, packed_o)
    attend(packed_v, 0, packed_v, features, packed_v, 2 * features, span_s, ids_row,
           column_v, jnp.logical_not(is_encoder), mixed_v, mass_v)
    massrow_v[...] = mass_v[...].T[:HEADS, :]
    move.store(massrow_v, mass_o)
    move.store(mixed_v, mixed_o)
    load_out.wait()
    which = jnp.where(is_encoder, 1, 0)
    gain, shift = gain_ref[pl.ds(which, 1), :], shift_ref[pl.ds(which, 1), :]
    for rows in blocks(x_v.shape[0]):
        unit, scale = standardize(base_v[rows, :] + nn(mixed_v[rows, :], wout[...]))
        unit_v[rows, :] = unit.astype(bf16)
        scale_v[rows, :] = jnp.broadcast_to(scale, (BLOCK, 128))
        hidden = unit * gain + shift
        base_v[rows, :] = hidden
        low_v[rows, :] = hidden.astype(bf16)
    move.store(unit_v, unit_o)
    move.store(scale_v, scale_o)
    move.store(low_v, low_o)

    store_hidden = move.make(base_v, hidden_o)
    stores = [move.make(a, b) for a, b in ((z_v, z_o), (slope_v, slope_o), (unit2_v, unit2_o), (scale2_v, scale2_o),
                                           (tail_v, layer_o.at[0, row]))]

    @pl.when(jnp.logical_not(is_encoder))
    def _():
        store_hidden.start()
        load_q.wait()
        for rows in blocks(x_v.shape[0]):
            tail_v[rows, :] = nn(low_v[rows, :], wq[...]).astype(bf16)
        store_hidden.wait()

    @pl.when(is_encoder)
    def _():
        load_up.wait()
        load_down.wait()
        for rows in blocks(x_v.shape[0]):
            feed_forward(low_v, rows, wup, z_v, slope_v)
            unit, scale = standardize(base_v[rows, :] + nn(z_v[rows, :], wdown[...]))
            unit2_v[rows, :] = unit.astype(bf16)
            scale2_v[rows, :] = jnp.broadcast_to(scale, (BLOCK, 128))
            tail_v[rows, :] = (unit * gain_ref[2:3, :] + shift_ref[2:3, :]).astype(bf16)
        for copy in stores:
            copy.start()
        for copy in stores:
            copy.wait()

    move.store(tail_v, tail_o)
    move.finish()


def feed_forward(low_ref, rows, wup, z_ref, slope_ref):
    for start in range(0, wup.shape[1], 512):
        columns = slice(start, start + 512)
        up = nn(low_ref[rows, :], wup[:, columns])
        gate = 1.0 / (1.0 + jnp.exp(-up))
        z = up * gate
        z_ref[rows, columns] = z.astype(bf16)
        slope_ref[rows, columns] = (gate + z * (1.0 - gate)).astype(bf16)


def feed_back(grad_ref, rows, wup, wdown, slope_ref, du_ref):
    for start in range(0, wup.shape[1], 512):
        columns = slice(start, start + 512)
        dz = nt(grad_ref[rows, :], wdown[columns, :])
        du_ref[rows, columns] = (dz * slope_ref[rows, columns].astype(f32)).astype(bf16)
    return nt(du_ref[rows, :], wup[...])


def cross_kernel(row, memory_hbm, query_hbm, hidden_hbm, cot_hbm, ids_ref, id_ref, kv_hbm, cross_hbm, up_hbm, down_hbm,
                 gain_in, shift_in, before,
                 layer_o, low_o, z_o, du_o, df_o, mixed_o, dbranch_o, dr_o, dq_o, dkv_o, dmem_o, sums_o,
                 gain_ref, shift_ref, span_s, turned_s, memory_v, query_v, hidden_v, cot_v, wkv, wout, wup, wdown, kv_v, column_v, mixed_v, mass_v, massrow_v,
                 delta_v, low_v, z_v, slope_v, unit_v, scale_v, du_v, df_v, dbranch_v, dmixed_v, dq_v, dkv_v, dmem_v,
                 out_v, sum_v, sums_v, sems):
    is_encoder = role()
    features = memory_v.shape[1]
    size = memory_v.shape[0]

    @pl.when(jnp.logical_not(is_encoder))
    def _():
        move = Mover(sems)
        load_kv = move.load(kv_hbm, wkv)
        load_memory = move.load(memory_hbm, memory_v)
        load_query = move.load(query_hbm, query_v)
        load_hidden = move.load(hidden_hbm, hidden_v)
        load_out = move.load(cross_hbm.at[0, :, pl.ds(features, features)], wout)
        load_up = move.load(up_hbm.at[0], wup)
        load_down = move.load(down_hbm.at[0], wdown)
        load_cot = move.load(cot_hbm.at[row], cot_v)
        source, target = ids_ref[0, row:row + 1, :], ids_ref[1, row:row + 1, :]
        source, target = source.astype(f32), target.astype(f32)
        column_v[...] = as_column(target)
        gain_ref[...] = gain_in[0].astype(f32)
        shift_ref[...] = shift_in[0].astype(f32)
        spans(lambda at: id_ref[1, row, at], source, None, False, span_s)
        spans(lambda at: id_ref[0, row, at], target, None, True, turned_s)
        sums_v[...] = jnp.zeros_like(sums_v)
        load_kv.wait()
        load_memory.wait()
        @pl.loop(0, size // BLOCK)
        def _(index):
            rows = pl.ds(pl.multiple_of(index * BLOCK, BLOCK), BLOCK)
            kv_v[rows, :] = nn(memory_v[rows, :], wkv[...]).astype(bf16)
        load_query.wait()
        attend(query_v, 0, kv_v, 0, kv_v, features, span_s, source, column_v, None, mixed_v, mass_v)
        massrow_v[...] = mass_v[...].T[:HEADS, :]
        move.store(mixed_v, mixed_o)
        load_hidden.wait()
        load_out.wait()
        for rows in blocks(size):
            unit, scale = standardize(hidden_v[rows, :] + nn(mixed_v[rows, :], wout[...]))
            unit_v[rows, :] = unit.astype(bf16)
            scale_v[rows, :] = jnp.broadcast_to(scale, (BLOCK, 128))
            hidden = unit * gain_ref[1:2, :] + shift_ref[1:2, :]
            hidden_v[rows, :] = hidden
            low_v[rows, :] = hidden.astype(bf16)
        move.store(low_v, low_o)
        load_up.wait()
        load_down.wait()
        load_cot.wait()
        for rows in blocks(size):
            feed_forward(low_v, rows, wup, z_v, slope_v)
            unit, scale = standardize(hidden_v[rows, :] + nn(z_v[rows, :], wdown[...]))
            out_v[rows, :] = (unit * gain_ref[2:3, :] + shift_ref[2:3, :]).astype(bf16)
            grad = cot_v[rows, :].astype(f32)
            sums_v[2] += fold(grad * unit)
            sums_v[5] += fold(grad)
            dr = norm_back(grad, unit, scale, gain_ref[2:3, :])
            hidden_v[rows, :] = dr
            df_v[rows, :] = dr.astype(bf16)
        move.store(z_v, z_o)
        move.store(df_v, df_o)
        move.store(out_v, layer_o.at[0, row])
        for rows in blocks(size):
            grad = hidden_v[rows, :] + feed_back(df_v, rows, wup, wdown, slope_v, du_v)
            unit = unit_v[rows, :].astype(f32)
            sums_v[1] += fold(grad * unit)
            sums_v[4] += fold(grad)
            dr = norm_back(grad, unit, scale_v[rows, :1], gain_ref[1:2, :])
            hidden_v[rows, :] = dr
            dbranch_v[rows, :] = dr.astype(bf16)
            dmixed_v[rows, :] = nt(dbranch_v[rows, :], wout[...]).astype(bf16)
        move.store(du_v, du_o)
        move.store(dbranch_v, dbranch_o)
        move.store(hidden_v, dr_o)
        move.store(sums_v, sums_o)
        column_v[...] = as_column(source)
        head_sums(dmixed_v, mixed_v, delta_v)
        attend_back(query_v, 0, kv_v, 0, kv_v, features, dmixed_v, turned_s, target, column_v, None,
                    massrow_v, delta_v, dq_v, 0, dkv_v, 0, dkv_v, features, sum_v)
        move.store(dq_v, dq_o)
        move.store(dkv_v, dkv_o)
        @pl.loop(0, size // BLOCK)
        def _(index):
            rows = pl.ds(pl.multiple_of(index * BLOCK, BLOCK), BLOCK)
            dmem_v[rows, :] = nt(dkv_v[rows, :], wkv[...]).astype(bf16)
        move.store(dmem_v, dmem_o)
        move.finish()


def back_kernel(enc_row, dec_row, dmem_hbm, unit2_hbm, scale2_hbm, slope_hbm, dr_hbm, dq_hbm,
                eunit_hbm, escale_hbm, epacked_hbm, emixed_hbm, emass_hbm,
                dunit_hbm, dscale_hbm, dpacked_hbm, dmixed_hbm, dmass_hbm,
                x_hbm, ids_ref, id_ref, qkv_hbm, out_hbm, cross_hbm, up_hbm, down_hbm, gain_in, z_hbm, low_hbm, *rest):
    more = [None, None]
    if enc_row:
        more, rest = rest[:2], rest[2:]
    else:
        more, rest = rest[:12], rest[12:]
    back_body(enc_row, dec_row, dmem_hbm, unit2_hbm, scale2_hbm, slope_hbm, dr_hbm, dq_hbm,
              eunit_hbm, escale_hbm, epacked_hbm, emixed_hbm, emass_hbm,
              dunit_hbm, dscale_hbm, dpacked_hbm, dmixed_hbm, dmass_hbm,
              x_hbm, ids_ref, id_ref, qkv_hbm, out_hbm, cross_hbm, up_hbm, down_hbm, gain_in, z_hbm, low_hbm, more, *rest)


def back_body(enc_row, dec_row, dmem_hbm, unit2_hbm, scale2_hbm, slope_hbm, dr_hbm, dq_hbm,
                eunit_hbm, escale_hbm, epacked_hbm, emixed_hbm, emass_hbm,
                dunit_hbm, dscale_hbm, dpacked_hbm, dmixed_hbm, dmass_hbm,
                x_hbm, ids_ref, id_ref, qkv_hbm, out_hbm, cross_hbm, up_hbm, down_hbm, gain_in, z_hbm, low_hbm, more,
                ffn_o, dbranch_o, dpacked_o, dx_o, sums_o,
                gain_ref, span_s, z_v, low_v, ffn_v, *rest):
    (                dmem_v, unit2_v, scale2_v, slope_v, dr_v, dq_v, unit_v, scale_v, packed_v, mixed_v, mass_v, x_v,
                wqkv, wout, wq, wup, wdown, column_v, delta_v, du_v, df_v, dbranch_v, dout_v, dpacked_v, sum_v,
                sums_v) = rest[:26]
    many, sems = rest[26:-1], rest[-1]
    is_encoder = role()
    features = mixed_v.shape[1]
    size = mixed_v.shape[0]

    def run():
        move = Mover(sems)
        is_decoder = jnp.logical_not(is_encoder)
        load_dmem = move.make(dmem_hbm, dmem_v)
        load_unit2 = move.make(unit2_hbm, unit2_v)
        load_scale2 = move.make(scale2_hbm, scale2_v)
        load_slope = move.make(slope_hbm, slope_v)
        load_down = move.make(down_hbm.at[0], wdown)
        load_up = move.make(up_hbm.at[0], wup)
        load_dr = move.make(dr_hbm, dr_v)
        load_dq = move.make(dq_hbm, dq_v)
        load_q = move.make(cross_hbm.at[0, :, pl.ds(0, features)], wq)
        firsts = [load_dmem, load_unit2, load_scale2, load_down, load_slope, load_up]

        sums_v[...] = jnp.zeros_like(sums_v)
        enc_selfs = [(eunit_hbm, unit_v), (escale_hbm, scale_v), (emixed_hbm, mixed_v), (epacked_hbm, packed_v), (emass_hbm, mass_v)]
        dec_selfs = [(dunit_hbm, unit_v), (dscale_hbm, scale_v), (dmixed_hbm, mixed_v), (dpacked_hbm, packed_v), (dmass_hbm, mass_v)]
        enc_pairs, dec_pairs = [], []
        for (es, ev), (ds, dv) in zip(enc_selfs, dec_selfs):
            enc_pairs.append(move.make(es, ev))
            dec_pairs.append(pltpu.make_async_copy(ds, dv, sems.at[move.used - 1]))
        load_x = move.make(x_hbm.at[0, enc_row or 0], x_v)
        load_out = move.make(out_hbm.at[0], wout)
        load_qkv = move.make(qkv_hbm.at[0], wqkv)
        store_ffn = move.make(ffn_v, ffn_o)
        load_low = move.make(low_hbm, low_v)
        load_z = move.make(z_hbm, z_v)
        load_before = move.make(more[1], ffn_v) if enc_row else None
        ffn_loads = [load_low, load_z] + ([load_before] if enc_row else [])
        dx_sem = sems.at[move.used]
        move.used += 1

        @pl.when(is_encoder)
        def _():
            for copy in firsts:
                copy.start()
            for copy in enc_pairs:
                copy.start()
            load_x.start()
            for copy in ffn_loads:
                copy.start()

        @pl.when(is_decoder)
        def _():
            load_dq.start()
            load_q.start()
            load_dr.start()
            for copy in dec_pairs:
                copy.start()

        load_out.start()
        load_qkv.start()
        enc_ids, dec_ids = ids_ref[0:1, enc_row or 0, :], ids_ref[1:2, dec_row or 0, :]
        ids_row = jnp.where(is_encoder, enc_ids, dec_ids)
        ids_row = ids_row.astype(f32)
        column_v[...] = as_column(ids_row)

        def key_id(at):
            return jnp.where(is_encoder, id_ref[0, enc_row or 0, at], id_ref[1, dec_row or 0, at])

        gain_ref[...] = gain_in[0].astype(f32)
        spans(key_id, ids_row, is_decoder, True, span_s)


        @pl.when(is_encoder)
        def _():
            for copy in firsts[:3]:
                copy.wait()
            for rows in blocks(size):
                grad = dmem_v[rows, :].astype(f32)
                unit = unit2_v[rows, :].astype(f32)
                sums_v[2] += fold(grad * unit)
                sums_v[5] += fold(grad)
                dr = norm_back(grad, unit, scale2_v[rows, :1], gain_ref[2:3, :])
                dr_v[rows, :] = dr
                df_v[rows, :] = dr.astype(bf16)
            for copy in firsts[3:]:
                copy.wait()
            for rows in blocks(size):
                dr_v[rows, :] += feed_back(df_v, rows, wup, wdown, slope_v, du_v)

        @pl.when(is_decoder)
        def _():
            load_dq.wait()
            load_q.wait()
            load_dr.wait()
            for rows in blocks(size):
                dr_v[rows, :] += nt(dq_v[rows, :], wq[...])

        for copy in enc_pairs:
            copy.wait()
        load_out.wait()
        which = jnp.where(is_encoder, 1, 0)
        gain = gain_ref[pl.ds(which, 1), :]
        for rows in blocks(size):
            grad = dr_v[rows, :]
            unit = unit_v[rows, :].astype(f32)
            sums_v[pl.ds(which, 1)] += fold(grad * unit)[None]
            sums_v[pl.ds(which + 3, 1)] += fold(grad)[None]
            dr = norm_back(grad, unit, scale_v[rows, :1], gain)
            dr_v[rows, :] = dr
            dbranch_v[rows, :] = dr.astype(bf16)
            dout_v[rows, :] = nt(dbranch_v[rows, :], wout[...]).astype(bf16)
        move.store(dbranch_v, dbranch_o)
        head_sums(dout_v, mixed_v, delta_v)
        attend_back(packed_v, 0, packed_v, features, packed_v, 2 * features, dout_v, span_s, ids_row, column_v, is_decoder,
                    mass_v, delta_v, dpacked_v, 0, dpacked_v, features, dpacked_v, 2 * features, sum_v)
        move.store(dpacked_v, dpacked_o)
        load_qkv.wait()
        for rows in blocks(size):
            dr_v[rows, :] += nt(dpacked_v[rows, :], wqkv[...])

        @pl.when(is_encoder)
        def _():
            load_x.wait()
            for rows in blocks(size):
                unit, scale = standardize(x_v[rows, :].astype(f32))
                grad = dr_v[rows, :]
                sums_v[0] += fold(grad * unit)
                sums_v[3] += fold(grad)
                dr_v[rows, :] = norm_back(grad, unit, scale, gain_ref[0:1, :])
            for copy in ffn_loads:
                copy.wait()
            ffn_weights(low_v, du_v, z_v, df_v, ffn_v, bool(enc_row))
            store_ffn.start()
            store_ffn.wait()

        pl.when(is_encoder)(lambda: pltpu.make_async_copy(dr_v, dx_o.at[0, enc_row or 0], dx_sem).start())
        pl.when(is_decoder)(lambda: pltpu.make_async_copy(dr_v, dx_o.at[0, dec_row or 0], dx_sem).start())
        pltpu.make_async_copy(dr_v, dx_o.at[0, 0], dx_sem).wait()
        move.store(sums_v, sums_o)
        move.finish()

    if dec_row is not None:
        run()
    else:
        @pl.when(jnp.logical_not(is_encoder))
        def _():
            move = Mover(sems)
            z_all, df_all, low_all, du_all = many
            width = df_all.shape[1]
            groups = []

            def start(pieces, target, columns=slice(None)):
                return [move.load(piece.at[:, columns], target.at[pl.ds(i * size, size), columns])
                        for i, piece in enumerate(pieces)]

            for j in range(0, z_all.shape[1], width):
                group = start(more[3:6], df_all) if j == 0 else []
                groups.append(group + start(more[0:3], z_all, pl.ds(j, width)))
            groups.append(start(more[6:9], low_all) + start(more[9:12], du_all))

            def ready(stage):
                for copy in groups[stage]:
                    copy.wait()

            ffn_weights(low_all, du_all, z_all, df_all, ffn_v, False, ready)
            move.store(ffn_v, ffn_o)
            move.finish()

        pl.when(is_encoder)(run)


def named(layout, refs):
    found, at = types.SimpleNamespace(), 0
    for name, many in vars(layout).items():
        if name[0] != "_":
            setattr(found, name, refs[at] if many == 1 else refs[at:at + many])
            at += many
    assert at == len(refs)
    return found


def place(target, start, value, onto=False):
    columns = slice(start, start + value.shape[1])
    if onto:
        value = value + target[:, columns].astype(f32)
    target[:, columns] = value.astype(target.dtype)


def ffn_weights(flow_v, du_v, z_v, df_v, out_v, onto, ready=None):
    width, hidden = flow_v.shape[1], du_v.shape[1]
    for j in range(0, hidden, width):
        if ready is not None:
            ready(j // width)
        place(out_v, hidden + j, tn(z_v[:, j:j + width], df_v[...]), onto)
    if ready is not None:
        ready(hidden // width)
    turned = flow_v[...].T
    for j in range(0, hidden, width):
        place(out_v, j, nn(turned, du_v[:, j:j + width]), onto)


class MiddleRefs:
    dmem = 1
    unit2 = 1
    scale2 = 1
    slope = 1
    z = 1
    low = 1
    up = 1
    down = 1
    gain_in = 1
    e_ffn = 1
    d_ffn = 1
    dr_o = 1
    sums_o = 1
    ffn_o = 1
    gain = 1
    dmem_v = 1
    unit2_v = 1
    scale2_v = 1
    slope_v = 1
    dr_v = 1
    sums_v = 1
    wup = 1
    wdown = 1
    flow_v = 1
    du_v = 1
    z_v = 1
    df_v = 1
    ffn_v = 1
    sems = 1


def encoder_middle_kernel(*refs):
    r = named(MiddleRefs, refs)
    size = r.dmem_v.shape[0]

    @pl.when(role())
    def _():
        move = Mover(r.sems)
        first = [move.load(a, b) for a, b in ((r.dmem, r.dmem_v), (r.unit2, r.unit2_v), (r.scale2, r.scale2_v))]
        loads = [move.load(r.down.at[0], r.wdown), move.load(r.slope, r.slope_v),
                 move.load(r.up.at[0], r.wup)]
        later = [move.load(r.z, r.z_v), move.load(r.low, r.flow_v), move.load(r.e_ffn, r.ffn_v)]
        gain = r.gain
        gain[...] = r.gain_in[0].astype(f32)
        sums = r.sums_v
        sums[...] = jnp.zeros_like(sums)
        for copy in first:
            copy.wait()
        for rows in blocks(size):
            grad = r.dmem_v[rows, :].astype(f32)
            unit = r.unit2_v[rows, :].astype(f32)
            sums[2] += fold(grad * unit)
            sums[5] += fold(grad)
            dr = norm_back(grad, unit, r.scale2_v[rows, :1], gain[2:3, :])
            r.dr_v[rows, :] = dr
            r.df_v[rows, :] = dr.astype(bf16)
        move.store(sums, r.sums_o)
        for copy in loads:
            copy.wait()
        for rows in blocks(size):
            for start in range(0, r.wup.shape[1], 512):
                columns = slice(start, start + 512)
                dz = nt(r.df_v[rows, :], r.wdown[columns, :])
                r.du_v[rows, columns] = (dz * r.slope_v[rows, columns].astype(f32)).astype(bf16)
            r.dr_v[rows, :] += nt(r.du_v[rows, :], r.wup[...])
        move.store(r.dr_v, r.dr_o)
        for copy in later:
            copy.wait()
        ffn_weights(r.flow_v, r.du_v, r.z_v, r.df_v, r.ffn_v, True)
        move.store(r.ffn_v, r.ffn_o)
        move.finish()


class LastRefs:
    ffn = 1
    a_dr = 1
    d_dr = 3
    d_dq = 3
    unit = 3
    scale = 3
    packed = 3
    mixed = 3
    mass = 3
    x = 1
    ids = 1
    wqkv_hbm = 1
    wout_hbm = 1
    cross_hbm = 1
    gain_in = 1
    lowin = 3
    dpacked = 2
    dbranch = 2
    low = 3
    cmixed = 3
    cdbranch = 3
    memory = 3
    dkv = 3
    e_sums = 3
    d_sums = 4
    before = 1
    ffn_o = 1
    rest_o = 1
    dx_o = 1
    gain = 1
    dr_v = 1
    dq_v = 1
    unit_v = 1
    scale_v = 1
    packed_v = 1
    mass_v = 1
    x_v = 1
    wqkv = 1
    wout = 1
    wq = 1
    column_v = 1
    delta_v = 1
    dout_v = 1
    sum_v = 1
    sums_v = 1
    in_v = 1
    mixed_v = 1
    dpacked_v = 1
    dbranch_v = 1
    low_v = 1
    dqs_v = 1
    cmixed_v = 1
    cdbranch_v = 1
    memory_v = 1
    dkv_v = 1
    kv_v = 1
    norm_v = 1
    sems = 1
    kv_sems = 1
    local1 = 1
    local2 = 1


class RingRefs:
    total1 = 1
    paired1 = 1
    landed1 = 1
    total2 = 1
    paired2 = 1
    landed2 = 1
    pair1 = 1
    ring1 = 1
    gather1 = 1
    share1 = 1
    pair2 = 1
    ring2 = 1
    gather2 = 1
    share2 = 1


def last_kernel(chips, *refs):
    ring_refs = len([name for name in vars(RingRefs) if name[0] != "_"]) if chips else 0
    r = named(LastRefs, refs[:len(refs) - ring_refs])
    ring = named(RingRefs, refs[len(refs) - ring_refs:]) if chips else None
    is_encoder = role()
    is_decoder = jnp.logical_not(is_encoder)
    features = r.dr_v.shape[1]
    size = r.dr_v.shape[0]
    move = Mover(r.sems)
    load_ffn = move.load(r.ffn, r.local1)
    load_out = move.load(r.wout_hbm.at[0], r.wout)
    load_q = move.load(r.cross_hbm.at[0, :, pl.ds(0, features)], r.wq)
    load_qkv = move.load(r.wqkv_hbm.at[0], r.wqkv)
    row_sems = [r.sems.at[move.used + i] for i in range(8)]
    move.used += 8

    def on(side, action):
        if side is None:
            action()
        else:
            pl.when(side)(action)

    def gather(target, pieces, side=None):
        made = [move.make(piece, target.at[pl.ds(i * size, size)]) for i, piece in enumerate(pieces)]

        def start():
            for copy in made:
                copy.start()

        on(side, start)
        return made, side

    def settle(*loads):
        for made, side in loads:
            def wait():
                for copy in made:
                    copy.wait()

            on(side, wait)

    def load_row(row):
        for i in range(1, 3):
            @pl.when(row == i)
            def _():
                for j, (pieces, target) in enumerate(((r.unit, r.unit_v), (r.scale, r.scale_v), (r.packed, r.packed_v),
                                                      (r.mass, r.mass_v))):
                    pltpu.make_async_copy(pieces[i], target, row_sems[j]).start()

                @pl.when(is_decoder)
                def _():
                    pltpu.make_async_copy(r.d_dr[i], r.dr_v, row_sems[4]).start()
                    pltpu.make_async_copy(r.d_dq[i], r.dq_v, row_sems[5]).start()

        @pl.when(is_encoder)
        def _():
            pltpu.make_async_copy(r.a_dr, r.dr_v, row_sems[4]).start()
            pltpu.make_async_copy(r.x.at[0, 2], r.x_v, row_sems[5]).start()

    start_row = jnp.where(is_encoder, 2, 1)
    gain = r.gain
    gain[...] = r.gain_in[0].astype(f32)
    sums = r.sums_v
    sums[...] = jnp.zeros_like(sums)
    if chips:
        first = Ring(chips, r.local1, ring.total1, ring.paired1, ring.landed1, ring.pair1, ring.ring1, ring.gather1, ring.share1)
        second = Ring(chips, r.local2, ring.total2, ring.paired2, ring.landed2, ring.pair2, ring.ring2, ring.gather2, ring.share2)
    else:
        first, second = NoRing(r.local1), NoRing(r.local2)
    partner = {"section": 1 - lax.axis_index("section")}
    barrier = pltpu.get_barrier_semaphore()
    for peer in (partner, *first.peers()):
        pl.semaphore_signal(barrier, inc=1, device_id=peer, device_id_type=pl.DeviceIdType.MESH)
    pl.semaphore_wait(barrier, 1 + len(first.peers()))
    send_kv = pltpu.make_async_remote_copy(
        src_ref=r.kv_v, dst_ref=r.local2.at[:, pl.ds(4 * features, 2 * features)], send_sem=r.kv_sems.at[0],
        recv_sem=r.kv_sems.at[1], device_id=partner, device_id_type=pl.DeviceIdType.MESH)
    load_ffn.wait()
    first.begin()
    early = first.units // (2 * chips - 1) if chips else 0
    load_memory = gather(r.memory_v, r.memory, is_decoder)
    load_dkv = gather(r.dkv_v, r.dkv, is_decoder)
    load_in = gather(r.in_v, r.lowin)
    load_mixed = gather(r.mixed_v, r.mixed)
    kept = []
    for target, pieces in ((r.dpacked_v, r.dpacked), (r.dbranch_v, r.dbranch)):
        for i in range(2):
            copy = move.make(pieces[i], target.at[pl.ds(i * size, size)])
            pl.when(is_encoder)(copy.start)
            kept.append((is_encoder, copy))
        copy = move.make(pieces[1], target.at[pl.ds(0, size)])
        pl.when(is_decoder)(copy.start)
        kept.append((is_decoder, copy))
    load_cross = [gather(target, pieces, is_decoder) for target, pieces in (
        (r.low_v, r.low), (r.dqs_v, r.d_dq), (r.cmixed_v, r.cmixed), (r.cdbranch_v, r.cdbranch))]
    load_row(start_row)
    lax.fori_loop(0, early, lambda i, carry: (first.unit(i), carry)[1], 0)
    settle(load_memory, load_dkv)

    @pl.when(is_decoder)
    def _():
        turned = r.memory_v[...].T
        for start in range(0, 2 * features, features):
            place(r.kv_v, start, nn(turned, r.dkv_v[:, start:start + features]))
        send_kv.start()

    load_out.wait()
    load_q.wait()
    load_qkv.wait()
    settle(load_mixed)
    for side, copy in kept:
        pl.when(side)(copy.wait)

    def tick(at):
        def one(i, carry):
            first.unit(early + UNITS * at + i)
            return carry

        lax.fori_loop(0, UNITS, one, 0)

    per_row = 2 * (size // STRIP) + 6
    which = jnp.where(is_encoder, 1, 0)
    row_count = 3 - start_row

    def one_row(row, carry):
        done = (row - start_row) * per_row
        base = pl.multiple_of(row * size, size)
        pl.when(row > start_row)(functools.partial(load_row, row))
        ids_row = jnp.where(is_encoder, r.ids[0:1, 2, :], r.ids[1:2, 1, :])
        ids_row = jnp.where(is_decoder & (row == 2), r.ids[1:2, 2, :], ids_row)
        ids_row = ids_row.astype(f32)
        r.column_v[...] = as_column(ids_row)
        for j, target in enumerate((r.unit_v, r.scale_v, r.packed_v, r.mass_v, r.dr_v)):
            pltpu.make_async_copy(target, target, row_sems[j]).wait()

        @pl.when(is_decoder)
        def _():
            pltpu.make_async_copy(r.dq_v, r.dq_v, row_sems[5]).wait()
            for rows in blocks(size):
                r.dr_v[rows, :] += nt(r.dq_v[rows, :], r.wq[...])

        for rows in blocks(size):
            moved = pl.ds(pl.multiple_of(base + rows.start, BLOCK), BLOCK)
            grad = r.dr_v[rows, :]
            unit = r.unit_v[rows, :].astype(f32)
            sums[pl.ds(which, 1)] += fold(grad * unit)[None]
            sums[pl.ds(which + 3, 1)] += fold(grad)[None]
            dr = norm_back(grad, unit, r.scale_v[rows, :1], gain[pl.ds(which, 1), :])
            r.dr_v[rows, :] = dr
            r.dbranch_v[moved, :] = dr.astype(bf16)
            r.dout_v[rows, :] = nt(dr.astype(bf16), r.wout[...]).astype(bf16)
            tick(done + rows.start // BLOCK)
        head_sums(r.dout_v, r.mixed_v, r.delta_v, base)
        tick(done + 2)
        attend_back(r.packed_v, 0, r.packed_v, features, r.packed_v, 2 * features, r.dout_v, None, ids_row,
                    r.column_v, is_decoder, r.mass_v, r.delta_v, r.dpacked_v, 0, r.dpacked_v, features,
                    r.dpacked_v, 2 * features, r.sum_v, lambda at: tick(done + 3 + at),
                    pl.ds(base, size), base)
        for rows in blocks(size):
            moved = pl.ds(pl.multiple_of(base + rows.start, BLOCK), BLOCK)
            r.dr_v[rows, :] += nt(r.dpacked_v[moved, :], r.wqkv[...])
            tick(done + per_row - 3 + rows.start // BLOCK)

        @pl.when(is_encoder)
        def _():
            pltpu.make_async_copy(r.x_v, r.x_v, row_sems[5]).wait()
            for rows in blocks(size):
                unit, scale = standardize(r.x_v[rows, :].astype(f32))
                grad = r.dr_v[rows, :]
                sums[0] += fold(grad * unit)
                sums[3] += fold(grad)
                r.dr_v[rows, :] = norm_back(grad, unit, scale, gain[0:1, :])

        store = pltpu.make_async_copy(r.dr_v, r.dx_o.at[0, row], row_sems[6])
        store.start()
        tick(done + per_row - 1)
        store.wait()
        return carry

    lax.fori_loop(start_row, 3, one_row, 0)
    done = row_count * per_row
    settle(load_in)
    turned = r.in_v[...].T
    for j in range(3):
        place(r.local2, j * features, nn(turned, r.dpacked_v[:, j * features:(j + 1) * features]))
        tick(done + j)
    place(r.local2, 3 * features, tn(r.mixed_v[...], r.dbranch_v[...]))
    tick(done + 3)
    settle(*load_cross)
    norm = r.norm_v

    @pl.when(is_encoder)
    def _():
        send_kv.wait_recv()
        total = sums[...] + sum(member[...] for member in r.e_sums)
        norm[0:6, :] = jnp.sum(total, axis=1)

    @pl.when(is_decoder)
    def _():
        place(r.local2, 4 * features, tn(r.low_v[...], r.dqs_v[...]))
        place(r.local2, 5 * features, tn(r.cmixed_v[...], r.cdbranch_v[...]))
        total = sums[...] + sum(member[...] for member in r.d_sums)
        norm[0:6, :] = jnp.sum(total, axis=1)

    norm[6:, :] = jnp.zeros((norm.shape[0] - 6, features), f32)
    place(r.local2, 6 * features, norm[...].T)
    second.begin()

    def both(step, carry):
        first.unit(early + UNITS * (done + 4) + step)
        second.unit(step)
        return carry

    shared = max(first.units - early - UNITS * (per_row + 4), 0)
    lax.fori_loop(0, shared, both, 0)
    first.settle_shares()
    move.store(first.total, r.ffn_o)
    lax.fori_loop(shared, max(shared, second.units), both, 0)
    second.settle_shares()
    move.store(second.total, r.rest_o)
    first.finish()
    second.finish()
    pl.when(is_decoder)(send_kv.wait_send)
    move.finish()


class NoRing:
    units = 0

    def __init__(self, local):
        self.total = local

    def peers(self):
        return []

    def begin(self):
        pass

    def unit(self, count_):
        pass

    def settle_shares(self):
        pass

    def finish(self):
        pass


class Ring:
    def __init__(self, chips, local, total, paired, landed, pair_sems, ring_sems, gather_sems, share_sems):
        self.chips, self.local, self.total, self.paired, self.landed = chips, local, total, paired, landed
        self.pair_sems, self.ring_sems, self.gather_sems, self.share_sems = pair_sems, ring_sems, gather_sems, share_sems
        self.parts = ring_sems.shape[3]
        self.part = local.shape[1] // self.parts
        self.units = (2 * chips - 1) * self.parts
        me = lax.axis_index("dp")
        self.core = lax.rem(me, 2)
        self.place = ring_place(me, chips)
        self.sibling = me + 1 - 2 * self.core
        self.targets = (ring_device(lax.rem(self.place + 1, chips), chips, self.core),
                        ring_device(lax.rem(self.place + chips - 1, chips), chips, self.core))

    def peers(self):
        return [{"dp": other} for other in (self.sibling, *self.targets)]

    def rows(self, way, step, owner):
        slot = lax.rem(self.place + (self.chips - step if way == 0 else step), self.chips)
        return pl.ds(pl.multiple_of(64 * slot + 32 * owner + 16 * way, 16), 16)

    def late_rows(self, way, step):
        shift = lax.rem(self.chips - 1 + step, self.chips)
        return self.rows(way, shift, self.core)

    def columns(self, p):
        return pl.ds(pl.multiple_of(p * self.part, 128), self.part)

    def remote(self, source, target, sems, at, device):
        return pltpu.make_async_remote_copy(
            src_ref=source, dst_ref=target, send_sem=sems.at[(0, *at)], recv_sem=sems.at[(1, *at)],
            device_id={"dp": device}, device_id_type=pl.DeviceIdType.MESH)

    def pair_copy(self, way, step):
        return self.remote(self.local.at[self.rows(way, step, 1 - self.core)], self.paired.at[way, step],
                           self.pair_sems, (way, step), self.sibling)

    def ring_copy(self, way, step, p):
        return self.remote(self.paired.at[way, step, :, self.columns(p)], self.landed.at[way, step, :, self.columns(p)],
                           self.ring_sems, (way, step, p), self.targets[way])

    def gather_copy(self, way, step, p):
        spot = self.total.at[self.late_rows(way, step), self.columns(p)]
        return self.remote(spot, spot, self.gather_sems, (way, step, p), self.targets[way])

    def share_copy(self, way, step):
        spot = self.total.at[self.late_rows(way, step)]
        return self.remote(spot, spot, self.share_sems, (way, step), self.sibling)

    def begin(self):
        def start(step, carry):
            for way in range(2):
                self.pair_copy(way, step).start()
            return carry
        lax.fori_loop(0, self.chips, start, 0)

    def reduced(self, way, step, p, landed):
        columns = self.columns(p)
        value = self.local[self.rows(way, step, self.core), columns].astype(f32)
        value = value + self.paired[way, step, :, columns].astype(f32)
        if landed:
            value = value + self.landed[way, step - 1, :, columns].astype(f32)
        return value.astype(bf16)

    def unit(self, count_):
        last = self.chips - 1
        index = lax.div(count_, self.parts)
        p = count_ - index * self.parts
        reduce_at = jnp.minimum(index, last)

        @pl.when((index <= last) & (p == 0))
        def _():
            for way in range(2):
                self.pair_copy(way, reduce_at).wait_recv()

        @pl.when(index == 0)
        def _():
            for way in range(2):
                self.paired[way, 0, :, self.columns(p)] = self.reduced(way, 0, p, False)
                self.ring_copy(way, 0, p).start()

        @pl.when((index > 0) & (index < last))
        def _():
            for way in range(2):
                self.ring_copy(way, reduce_at - 1, p).wait_recv()
                self.paired[way, reduce_at, :, self.columns(p)] = self.reduced(way, reduce_at, p, True)
                self.ring_copy(way, reduce_at, p).start()

        @pl.when(index == last)
        def _():
            for way in range(2):
                self.ring_copy(way, last - 1, p).wait_recv()
                self.total[self.rows(way, last, self.core), self.columns(p)] = self.reduced(way, last, p, True)
                self.gather_copy(way, 0, p).start()

        gather_at = jnp.clip(index - last, 1, last)

        @pl.when((index > last) & (index < 2 * last))
        def _():
            for way in range(2):
                self.gather_copy(way, gather_at - 1, p).wait_recv()
                self.gather_copy(way, gather_at, p).start()

        @pl.when(index == 2 * last)
        def _():
            for way in range(2):
                self.gather_copy(way, last - 1, p).wait_recv()

        @pl.when((index >= last) & (index <= 2 * last) & (p == self.parts - 1))
        def _():
            share_at = jnp.clip(index - last, 0, last)
            for way in range(2):
                self.share_copy(way, share_at).start()

    def settle_shares(self):
        def wait(step, carry):
            for way in range(2):
                self.share_copy(way, step).wait_recv()
            return carry
        lax.fori_loop(0, self.chips, wait, 0)

    def finish(self):
        def wait(step, carry):
            for way in range(2):
                self.pair_copy(way, step).wait_send()
                self.share_copy(way, step).wait_send()
            return carry
        lax.fori_loop(0, self.chips, wait, 0)

        def wait_ring(step, carry):
            for way in range(2):
                for p in range(self.parts):
                    self.ring_copy(way, step, p).wait_send()
                    self.gather_copy(way, step, p).wait_send()
            return carry
        lax.fori_loop(0, self.chips - 1, wait_ring, 0)


def ring_place(index, chips):
    chip = lax.div(index, 2)
    level, side = lax.div(chip, 2), lax.rem(chip, 2)
    return jnp.where(side == 0, level, chips - 1 - level)


def ring_device(place_, chips, core):
    chip = jnp.where(place_ < chips // 2, 2 * place_, 2 * (chips - 1 - place_) + 1)
    return 2 * chip + core


ANY = pl.BlockSpec(memory_space=pl.ANY)
IN_VMEM = pl.BlockSpec(memory_space=pltpu.VMEM)
IN_SMEM = pl.BlockSpec(memory_space=pltpu.SMEM)


def shape(*dims, dtype=bf16):
    return jax.ShapeDtypeStruct(dims, dtype)


def scratch_of(member):
    return member if not isinstance(member, jax.ShapeDtypeStruct) else pltpu.VMEM(member.shape, member.dtype)


def call(name, body, in_specs, outs, scratch, sems, args, flops=0, aliases=()):
    return pl.pallas_call(
        body,
        name=name,
        input_output_aliases=dict(aliases),
        out_shape=outs,
        in_specs=in_specs,
        out_specs=[ANY] * len(outs),
        scratch_shapes=[scratch_of(s) for s in scratch] + [pltpu.SemaphoreType.DMA((sems,))],
        compiler_params=pltpu.CompilerParams(vmem_limit_bytes=VMEM_LIMIT, has_side_effects=True),
        cost_estimate=pl.CostEstimate(flops=flops, bytes_accessed=10 << 20, transcendentals=0),
    )(*args)


def front(row, embed, ids, weights, before):
    qkv, out, cross, up, down, gain, shift = weights
    size, d = embed.shape[2:]
    hidden = up.shape[2]
    outs = [shape(size, d), shape(size, 3 * d), shape(size, d), shape(HEADS, size, dtype=f32), shape(size, d),
            shape(size, 128, dtype=f32), shape(size, d), shape(size, d, dtype=f32), shape(size, hidden),
            shape(size, hidden), shape(size, d), shape(size, 128, dtype=f32), shape(size, d), shape(*embed.shape)]
    scratch = [shape(3, d, dtype=f32), shape(3, d, dtype=f32), pltpu.SMEM((2, size // STRIP), jnp.int32),
               shape(size, d), shape(d, 3 * d), shape(d, d), shape(d, d), shape(d, hidden), shape(hidden, d),
               shape(size, d, dtype=f32), shape(size, 128, dtype=f32), shape(size, d), shape(size, 3 * d),
               shape(size, d), shape(size, 128, dtype=f32), shape(HEADS, size, dtype=f32), shape(size, d),
               shape(size, 128, dtype=f32), shape(size, d), shape(size, hidden), shape(size, hidden),
               shape(size, d), shape(size, 128, dtype=f32), shape(size, d)]
    more = [before] if row else []
    return call(f"front{row}", functools.partial(front_kernel, row),
                [ANY, IN_VMEM, IN_SMEM] + [ANY] * 5 + [IN_VMEM] * 2 + [ANY] * len(more), outs, scratch, 24,
                (embed, ids, ids, qkv, out, cross, up, down, gain, shift, *more), flops=2 * 10**9,
                aliases=[(10, len(outs) - 1)] if row else [])


def cross(row, memory, query, hidden_f, cot, ids, kv_weight, weights, before):
    qkv, out, cross_w, up, down, gain, shift = weights
    size, d = memory.shape
    hidden = up.shape[2]
    outs = [shape(*before.shape), shape(size, d), shape(size, hidden), shape(size, hidden), shape(size, d), shape(size, d),
            shape(size, d), shape(size, d, dtype=f32), shape(size, d), shape(size, 2 * d), shape(size, d),
            shape(6, 8, d, dtype=f32)]
    scratch = [shape(3, d, dtype=f32), shape(3, d, dtype=f32), pltpu.SMEM((2, size // STRIP), jnp.int32),
               pltpu.SMEM((2, size // STRIP), jnp.int32),
               shape(size, d), shape(size, d), shape(size, d, dtype=f32), shape(size, d), shape(d, 2 * d),
               shape(d, d), shape(d, hidden), shape(hidden, d), shape(size, 2 * d), shape(size, 128, dtype=f32),
               shape(size, d), shape(size, 128, dtype=f32), shape(HEADS, size, dtype=f32), shape(HEADS, size, dtype=f32),
               shape(size, d), shape(size, hidden), shape(size, hidden), shape(size, d), shape(size, 128, dtype=f32),
               shape(size, hidden), shape(size, d), shape(size, d), shape(size, d), shape(size, d), shape(size, 2 * d),
               shape(size, d), shape(size, d), shape(size, d, dtype=f32), shape(6, 8, d, dtype=f32)]
    return call(f"cross{row}", functools.partial(cross_kernel, row),
                [ANY] * 4 + [IN_VMEM, IN_SMEM] + [ANY] * 4 + [IN_VMEM] * 2 + [ANY], outs, scratch,
                24, (memory, query, hidden_f, cot, ids, ids, kv_weight, cross_w, up, down, gain, shift, before),
                flops=20 * 10**9, aliases=[(12, 0)])


class BackOuts:
    ffn = 1
    dbranch = 1
    dpacked = 1
    dx = 1
    sums = 1


def back(enc_row, dec_row, dmem, e_front, d_front, d_cross, embed, ids, weights, before, crosses):
    qkv, out, cross_w, up, down, gain, shift = weights
    size, d = embed.shape[2:]
    hidden = up.shape[2]
    outs = [shape(d, 2 * hidden), shape(size, d), shape(size, 3 * d), shape(*embed.shape, dtype=f32),
            shape(6, 8, d, dtype=f32)]
    scratch = [shape(3, d, dtype=f32), pltpu.SMEM((2, size // STRIP), jnp.int32), shape(size, hidden), shape(size, d),
               shape(d, 2 * hidden),
               shape(size, d), shape(size, d), shape(size, 128, dtype=f32), shape(size, hidden),
               shape(size, d, dtype=f32), shape(size, d), shape(size, d), shape(size, 128, dtype=f32),
               shape(size, 3 * d), shape(size, d), shape(HEADS, size, dtype=f32), shape(size, d),
               shape(d, 3 * d), shape(d, d), shape(d, d), shape(d, hidden), shape(hidden, d),
               shape(size, 128, dtype=f32), shape(HEADS, size, dtype=f32), shape(size, hidden), shape(size, d),
               shape(size, d), shape(size, d), shape(size, 3 * d), shape(size, d, dtype=f32),
               shape(6, 8, d, dtype=f32)]
    args = (dmem, e_front.unit2, e_front.scale2, e_front.slope, d_cross.dr, d_cross.dq,
            e_front.unit, e_front.scale, e_front.packed, e_front.mixed, e_front.mass,
            d_front.unit, d_front.scale, d_front.packed, d_front.mixed, d_front.mass,
            embed, ids, ids, qkv, out, cross_w, up, down, gain, e_front.z, e_front.low)
    if before is None:
        more = [member for group in zip(*[(c.z, c.df, c.low, c.du) for c in crosses]) for member in group]
        tokens = 3 * size
        scratch = scratch + [shape(tokens, hidden), shape(tokens, d), shape(tokens, d), shape(tokens, hidden)]
    else:
        more = [before.dx, before.ffn]
    results = call(f"back_e{enc_row}_d{dec_row}", functools.partial(back_kernel, enc_row, dec_row),
                   [ANY] * 17 + [IN_VMEM, IN_SMEM] + [ANY] * 5 + [IN_VMEM] + [ANY] * (2 + len(more)),
                   outs, scratch, 36, (*args, *more), flops=12 * 10**9,
                   aliases=[(len(args), 3)] if before is not None else [])
    return named(BackOuts, results)


def spread_kernel(ffn_ref, rest_ref, dx_ref, qkv_ref, out_ref, cross_ref, up_ref, down_ref, gain_ref, shift_ref, dx_o):
    dx_o[...] = dx_ref[...]
    start = up_ref.shape[2]
    up_ref[0] = ffn_ref[:, :start].astype(f32)
    for i in range(down_ref.shape[0]):
        down_ref[i] = ffn_ref[:, start:start + down_ref.shape[2]].astype(f32)
        start += down_ref.shape[2]
    start = 0
    for ref in (qkv_ref, out_ref, cross_ref):
        ref[0] = rest_ref[:, start:start + ref.shape[2]].astype(f32)
        start += ref.shape[2]
    norms = rest_ref[:, start:].astype(f32).T
    for i in range(3):
        gain_ref[i] = norms[i:i + 1]
        shift_ref[i] = norms[3 + i:4 + i]


def spread(ffn, rest, input_grad, d, hidden):
    slab = 128
    dx_block = pl.BlockSpec((*input_grad.shape[:2], slab, d), lambda i: (0, 0, i, 0))
    widths = [3 * d, d, 2 * d, hidden]
    wide = [jax.ShapeDtypeStruct((1, d, w), f32) for w in widths]
    return pl.pallas_call(
        spread_kernel,
        name="spread",
        grid=(d // slab,),
        in_specs=[pl.BlockSpec((slab, member.shape[1]), lambda i: (i, 0)) for member in (ffn, rest)] + [dx_block],
        out_shape=wide + [shape(hidden // d, d, d, dtype=f32), shape(3, 1, d, dtype=f32), shape(3, 1, d, dtype=f32),
                          shape(*input_grad.shape, dtype=f32)],
        out_specs=[pl.BlockSpec((1, slab, w), lambda i: (0, i, 0)) for w in widths]
        + [pl.BlockSpec((hidden // d, slab, d), lambda i: (0, i, 0))]
        + [pl.BlockSpec((3, 1, slab), lambda i: (0, 0, i))] * 2 + [dx_block],
        compiler_params=pltpu.CompilerParams(vmem_limit_bytes=VMEM_LIMIT),
    )(ffn, rest, input_grad)


class FrontOuts:
    lowin = 1
    packed = 1
    mixed = 1
    mass = 1
    unit = 1
    scale = 1
    low = 1
    hidden = 1
    z = 1
    slope = 1
    unit2 = 1
    scale2 = 1
    tail = 1
    layer = 1


class CrossOuts:
    layer = 1
    low = 1
    z = 1
    du = 1
    df = 1
    mixed = 1
    dbranch = 1
    dr = 1
    dq = 1
    dkv = 1
    dmem = 1
    sums = 1


def per_device(embeddings, segments, cotangent, attn_qkv, attn_out, cross_proj, ffn_up, ffn_down, norm_gain, norm_bias):
    weights = (attn_qkv, attn_out, cross_proj, ffn_up, ffn_down, norm_gain, norm_bias)
    row_total, size, d = embeddings.shape[1:]
    hidden = ffn_up.shape[2]
    devices = lax.axis_size("dp")
    kv_weight = lax.ppermute(cross_proj[0], "section", [(0, 1)])

    rows = range(row_total)
    fronts, memories, layer_out = [], [], None
    for row in rows:
        fronts.append(named(FrontOuts, front(row, embeddings, segments, weights, layer_out)))
        layer_out = fronts[row].layer
        memories.append(lax.ppermute(fronts[row].tail, "section", [(0, 1)]))
    crosses, grads = [], []
    for row in rows:
        crosses.append(named(CrossOuts, cross(
            row, memories[row], fronts[row].tail, fronts[row].hidden, cotangent, segments, kv_weight, weights,
            layer_out)))
        layer_out = crosses[row].layer
        grads.append(lax.ppermute(crosses[row].dmem, "section", [(1, 0)]))
    tokens = row_total * size
    backs = []
    for row in range(row_total - 1):
        backs.append(back(row, row - 1 if row else None, grads[row], fronts[row], fronts[max(row - 1, 0)],
                          crosses[max(row - 1, 0)], embeddings, segments, weights, backs[-1] if backs else None, crosses))
    input_grad = backs[-1].dx
    dr, middle_sums, ffn_grad = call(
        "encoder_middle", encoder_middle_kernel, [ANY] * 8 + [IN_VMEM, ANY, ANY],
        [shape(size, d, dtype=f32), shape(6, 8, d, dtype=f32), shape(d, 2 * hidden)],
        [shape(3, d, dtype=f32), shape(size, d), shape(size, d), shape(size, 128, dtype=f32), shape(size, hidden),
         shape(size, d, dtype=f32), shape(6, 8, d, dtype=f32), shape(d, hidden), shape(hidden, d),
         shape(size, d), shape(size, hidden), shape(size, hidden), shape(size, d), shape(d, 2 * hidden)], 24,
        (grads[-1], fronts[-1].unit2, fronts[-1].scale2, fronts[-1].slope, fronts[-1].z, fronts[-1].low,
         ffn_up, ffn_down, norm_gain, backs[-1].ffn, backs[0].ffn),
        flops=16 * 10**9, aliases=[(10, 2)])

    chips = devices // 2 if d == 32 * devices else None
    ffn_width, rest_width = 2 * hidden, 6 * d + 128
    args = (ffn_grad, dr, *[m.dr for m in crosses], *[m.dq for m in crosses], *[m.unit for m in fronts],
            *[m.scale for m in fronts], *[m.packed for m in fronts], *[m.mixed for m in fronts], *[m.mass for m in fronts],
            embeddings, segments, attn_qkv, attn_out, cross_proj, norm_gain, *[m.lowin for m in fronts],
            *[m.dpacked for m in backs], *[m.dbranch for m in backs], *[m.low for m in fronts],
            *[m.mixed for m in crosses], *[m.dbranch for m in crosses], *memories, *[m.dkv for m in crosses],
            *[m.sums for m in backs], middle_sums, *[m.sums for m in crosses], backs[1].sums, input_grad)
    specs = [ANY] * 24 + [IN_VMEM] + [ANY] * 3 + [IN_VMEM] + [ANY] * 22 + [IN_VMEM] * 7 + [ANY]
    scratch = [shape(3, d, dtype=f32), shape(size, d, dtype=f32), shape(size, d), shape(size, d), shape(size, 128, dtype=f32),
               shape(size, 3 * d), shape(HEADS, size, dtype=f32), shape(size, d), shape(d, 3 * d), shape(d, d), shape(d, d),
               shape(size, 128, dtype=f32), shape(HEADS, size, dtype=f32), shape(size, d), shape(size, d, dtype=f32),
               shape(6, 8, d, dtype=f32), shape(tokens, d), shape(tokens, d), shape(tokens, 3 * d), shape(tokens, d),
               shape(tokens, d), shape(tokens, d), shape(tokens, d), shape(tokens, d), shape(tokens, d),
               shape(tokens, 2 * d), shape(d, 2 * d), shape(128, d, dtype=f32)]
    sems = pltpu.SemaphoreType.DMA
    rings = []
    if chips:
        for width in (ffn_width, rest_width):
            rings += [pltpu.VMEM((d, width), bf16), pltpu.VMEM((2, chips, 16, width), bf16),
                      pltpu.VMEM((2, chips - 1, 16, width), bf16)]
        for parts in PARTS:
            rings += [sems((2, 2, chips)), sems((2, 2, chips - 1, parts)), sems((2, 2, chips - 1, parts)), sems((2, 2, chips))]
    ffn_total, rest_total, input_grad = pl.pallas_call(
        functools.partial(last_kernel, chips),
        name="last",
        out_shape=[shape(d, ffn_width), shape(d, rest_width), shape(*embeddings.shape, dtype=f32)],
        in_specs=specs,
        out_specs=[ANY] * 3,
        scratch_shapes=[pltpu.VMEM(m.shape, m.dtype) for m in scratch] + [sems((52,)), sems((2,)),
                        pltpu.VMEM((d, ffn_width), bf16), pltpu.VMEM((d, rest_width), bf16)] + rings,
        input_output_aliases={len(args) - 1: 2},
        compiler_params=pltpu.CompilerParams(vmem_limit_bytes=VMEM_LIMIT, has_side_effects=True, collective_id=0),
        cost_estimate=pl.CostEstimate(flops=60 * 10**9, bytes_accessed=30 << 20, transcendentals=0),
    )(*args)
    if not chips:
        ffn_total, rest_total = lax.psum((ffn_total, rest_total), "dp")
    qkv, out, crossed, up, down, gain, shift, input_grad = spread(ffn_total, rest_total, input_grad, d, hidden)
    return (layer_out, input_grad, qkv, out, crossed, up, down.reshape(1, hidden, d), gain.transpose(1, 0, 2),
            shift.transpose(1, 0, 2))


def solution(mesh):
    in_specs = (
        P("section", "dp", None, None),
        P(None, "dp", None),
        P("dp", None, None),
        P("section", None, None),
        P("section", None, None),
        P("section", None, None),
        P("section", None, None),
        P("section", None, None),
        P("section", None, None),
        P("section", None, None),
    )
    out_specs = (
        P("section", "dp", None, None),
        P("section", "dp", None, None),
        P("section", None, None),
        P("section", None, None),
        P("section", None, None),
        P("section", None, None),
        P("section", None, None),
        P("section", None, None),
        P("section", None, None),
    )
    return jax.shard_map(
        per_device, mesh=mesh, in_specs=in_specs, out_specs=out_specs, check_vma=False
    )
```
